32 devices in a mesh: subset: 8 (over z, core), tile: 4 (over y, x).
Axes of the slice: x: 2, y: 2, z: 4, core: 2. Of those that a mesh axis runs over, the one named last changes fastest.
Arguments:
- blocks: bfloat16 [8, 4, 80, 128, 128], P('subset', 'tile'), may hold values from -11.8585412 to 11.8585412
- block_rows: int32 [8, 4, 80], P('subset', 'tile'), may hold values from 0 to 15, as said below
- block_cols: int32 [8, 4, 80], P('subset', 'tile'), may hold values from 0 to 31
- sinogram: float32 [4, 8, 16384], P(None, None, ('subset', 'tile')), may hold values from -6 to 6
Outputs:
- images: bfloat16 [8, 4, 8, 16384], P('subset', None, None, 'tile')
The draws below stay inside these ranges and needn't reach their ends.
Inputs may be any that keep to these rules, and one draw needn't show every extreme that they name: `block_rows`: on each device every row block appears exactly 5 times, and no pair of row block and column block repeats on a device.
All inputs are finite; a program needn't handle non-finite values.
Results may differ from the reference program's by a relative error of at most 0.012.
Values may be sent and summed in bfloat16 or wider, within the bound.
No kernel may reach another device: no remote copies, remote signals or barrier semaphores. Data moves between devices by JAX's collectives and lax.ppermute only.
A program may use at most 64 MiB of HBM per device.

```python
import jax
import jax.numpy as jnp
from jax import lax

BS = 128
CROSSING_RAYS = 2048
PIX = 4096
NB = 80
SL = 8
SLICE_BATCHES = 4
RB = 16
CB = 32
SUBSETS = 8
TILES = 4


def pattern_draw(key):
    base_key = jax.random.fold_in(key, 11)
    count = SUBSETS * TILES
    order_keys = jax.random.split(base_key, count)
    orders = jax.vmap(lambda sub_key: jax.random.permutation(sub_key, NB))(order_keys)
    col_keys = jax.random.split(jax.random.fold_in(base_key, 1), count * RB)
    picks = jax.vmap(lambda sub_key: jax.random.permutation(sub_key, CB)[:NB // RB])(col_keys)
    picks = picks.reshape(count, RB, NB // RB)
    row_ids = orders % RB
    ranks = orders // RB
    col_ids = picks[jnp.arange(count)[:, None], row_ids, ranks]
    return (row_ids.reshape(SUBSETS, TILES, NB).astype(jnp.int32), col_ids.reshape(SUBSETS, TILES, NB).astype(jnp.int32))


def draw_block_rows(key, part):
    return pattern_draw(key)[0]


def draw_block_cols(key, part):
    return pattern_draw(key)[1]


def draw_blocks(key, part):
    row_ids, col_ids = pattern_draw(key)
    base_scale = 1.0 / (3.0 * (TILES * (NB // RB) * BS) ** 0.5)
    shape = (SUBSETS, TILES, NB, BS, BS)
    values = jnp.clip(jax.random.normal(jax.random.fold_in(key, 21), shape, jnp.float32), -4.0, 4.0)
    top_scale = 3.0
    row_scale = jnp.exp(jax.random.uniform(jax.random.fold_in(key, 22), (SUBSETS, RB, BS), jnp.float32) * jnp.log(10.0))
    col_scale = jnp.exp(jax.random.uniform(jax.random.fold_in(key, 23), (TILES, CB, BS), jnp.float32) * jnp.log(10.0))
    tile_scale = top_scale ** (jnp.arange(TILES, dtype=jnp.float32) / max(TILES - 1, 1))
    row_pick = row_scale[jnp.arange(SUBSETS)[:, None, None], row_ids]
    col_pick = col_scale[jnp.arange(TILES)[None, :, None], col_ids]
    full = values * row_pick[:, :, :, :, None] * col_pick[:, :, :, None, :]
    full = full * tile_scale[None, :, None, None, None] * base_scale
    return full.astype(jnp.bfloat16)


def block_levels(own_key, dims, cuts, least, high):
    gain, own = 1.0, jax.random.fold_in(own_key, 6)
    for dim, blocks in cuts:
        heights = jnp.exp(jax.random.uniform(jax.random.fold_in(own, dim), (blocks,), jnp.float32, least / len(cuts), high / len(cuts)))
        gain = gain * jnp.repeat(heights, dims[dim] // blocks).reshape([-1 if axis == dim else 1 for axis in range(len(dims))])
    return gain


def scatter_about(own_key, dims, spread, bound, pieces=(), held_as=jnp.bfloat16):
    result = jax.random.normal(own_key, dims, jnp.float32) * spread
    if len(pieces) > 0:
        result = block_levels(own_key, dims, pieces, -0.22, 0.18) * result
    return jnp.clip(result, min=-bound, max=bound).astype(held_as)


def setup_inputs(seed: int = 0) -> dict:
    arg_keys = jax.random.split(jax.random.key(seed), 5)
    return {
        "blocks": draw_blocks(jax.random.fold_in(arg_keys[4], 71), 0),
        "block_rows": draw_block_rows(jax.random.fold_in(arg_keys[4], 71), 0),
        "block_cols": draw_block_cols(jax.random.fold_in(arg_keys[4], 71), 0),
        "sinogram": scatter_about(arg_keys[3], (SLICE_BATCHES, SL, SUBSETS * CROSSING_RAYS), 1.0, 6.0, ((2, 32),), jnp.float32),
    }


relaxation = 0.5


def reference(blocks, block_rows, block_cols, sinogram):
    slice_total_count = SLICE_BATCHES * SL
    measured_all = sinogram.reshape(slice_total_count, SUBSETS, CROSSING_RAYS).transpose(1, 0, 2)
    tile_range = jnp.arange(TILES, dtype=jnp.int32)[:, None]

    def advance(current, inputs):
        block_vals, row_ids, col_ids, measured = inputs
        block_wide = block_vals.astype(jnp.float32)
        row_onehot = (row_ids[:, :, None] == jnp.arange(RB, dtype=jnp.int32)[None, None, :]).astype(jnp.float32)
        col_hot = (col_ids[:, :, None] == jnp.arange(CB, dtype=jnp.int32)[None, None, :]).astype(jnp.float32)
        squares = jnp.sum(block_wide * block_wide, axis=3)
        norm_values = jnp.einsum("tnb,tnr->rb", squares, row_onehot, precision=lax.Precision.HIGHEST).reshape(CROSSING_RAYS)
        rounded_values = current.astype(jnp.bfloat16)
        gathered = rounded_values[:, tile_range, col_ids].astype(jnp.float32)
        ray_products = jnp.einsum("mtnq,tnbq->mtnb", gathered, block_wide)
        projected_rays = jnp.einsum("kejs,eja->kas", ray_products, row_onehot, precision=lax.Precision.HIGHEST).reshape(slice_total_count, CROSSING_RAYS)
        weights = (relaxation * (measured - projected_rays) / norm_values[None, :]).astype(jnp.bfloat16)
        weight_rows = weights.reshape(slice_total_count, RB, BS)[:, row_ids].astype(jnp.float32)
        back_terms = jnp.einsum("mtnb,tnbq->mtnq", weight_rows, block_wide)
        update = jnp.einsum("mtnq,tnc->mtcq", back_terms, col_hot, precision=lax.Precision.HIGHEST)
        image_new = current + update
        return image_new, image_new.astype(jnp.bfloat16)

    initial = jnp.zeros((slice_total_count, TILES, CB, BS), jnp.float32)
    final_image, history = lax.scan(advance, initial, (blocks, block_rows, block_cols, measured_all))
    return history.reshape(SUBSETS, SLICE_BATCHES, SL, TILES * PIX)
```

```python
import functools

import jax
import jax.numpy as jnp
from jax import lax
from jax.experimental import pallas as pl
from jax.experimental.pallas import tpu as pltpu
from jax.sharding import PartitionSpec as P

BS = 128
PIX = 4096
CB = PIX // BS
relaxation = 0.5

DIRECT = 4

NN = (((1,), (0,)), ((), ()))
NT = (((1,), (1,)), ((), ()))
VMEM = pl.BlockSpec(memory_space=pltpu.VMEM)
SMEM = pl.BlockSpec(memory_space=pltpu.SMEM)
PARAMS = pltpu.CompilerParams(vmem_limit_bytes=20 * 2**20)


def dot(lhs, rhs, dims):
    return lax.dot_general(lhs, rhs, dims, preferred_element_type=jnp.float32)


def head_kernel(pos, index, blocks, rays, term, norm_scr):
    count = blocks.shape[0]
    row_blocks = norm_scr.shape[0]
    quarter = rays.shape[0]
    slices = rays.shape[1]
    norm_scr[...] = jnp.zeros_like(norm_scr)
    on_diagonal = lax.broadcasted_iota(jnp.int32, (BS, BS), 0) == lax.broadcasted_iota(
        jnp.int32, (BS, BS), 1
    )
    for n in range(count):
        block = blocks[n]
        gram = jnp.where(on_diagonal, dot(block, block, NT), 0.0)
        part = gram[0:8]
        for k in range(8, BS, 8):
            part = part + gram[k : k + 8]
        row = index[0, n]
        norm_scr[row] = norm_scr[row] + part
    sums = jnp.sum(norm_scr[...], axis=1)
    coarse = sums.astype(jnp.bfloat16)
    fine = (sums - coarse.astype(jnp.float32)).astype(jnp.bfloat16)
    term[0:row_blocks] = jnp.zeros((row_blocks, slices, BS), jnp.bfloat16)
    for i in range(quarter):
        term[pos[1] * quarter + i] = (-rays[i]).astype(jnp.bfloat16)
    pad = slices - 2 * row_blocks
    parts = [coarse, fine]
    if pad:
        parts.append(jnp.zeros((pad, BS), jnp.bfloat16))
    term[row_blocks] = jnp.concatenate(parts, axis=0)


def weights_of(terms, row_blocks, w_scr):
    norms = 0.0
    for ref in terms:
        slab = ref[row_blocks].astype(jnp.float32)
        norms = norms + slab[0:row_blocks] + slab[row_blocks : 2 * row_blocks]
    scale = -relaxation / norms
    for r in range(row_blocks):
        total = terms[0][r].astype(jnp.float32)
        for ref in terms[1:]:
            total = total + ref[r].astype(jnp.float32)
        w_scr[r] = (total * scale[r : r + 1]).astype(jnp.bfloat16)


def back_project(index, blocks, w_scr, x_scr):
    for n in range(blocks.shape[0]):
        col = index[1, n]
        x_scr[col] = x_scr[col] + dot(w_scr[index[0, n]], blocks[n], NN)


def step_kernel(step, n_terms, has_image, *refs):
    refs = list(refs)
    pos, index_prev, index = refs[:3]
    terms = refs[3 : 3 + n_terms]
    rest = refs[3 + n_terms :]
    if has_image:
        image, offset = rest.pop(0)
    blocks_prev, blocks, rays, head, held, full, term, w_scr, x_scr, p_scr = rest
    row_blocks = p_scr.shape[0]
    quarter = rays.shape[0]
    active = pos[0] == step

    @pl.when(active)
    def _():
        weights_of(terms, row_blocks, w_scr)
        if has_image:
            x_scr[...] = image[offset : offset + CB].astype(jnp.float32)
        else:
            x_scr[...] = jnp.zeros_like(x_scr)
        back_project(index_prev, blocks_prev, w_scr, x_scr)
        base = row_blocks + 1
        full[base : base + CB] = x_scr[...].astype(jnp.bfloat16)
        p_scr[...] = jnp.zeros_like(p_scr)
        for i in range(quarter):
            p_scr[pos[1] * quarter + i] = -rays[i]
        for n in range(blocks.shape[0]):
            row = index[0, n]
            p_scr[row] = p_scr[row] + dot(full[base + index[1, n]], blocks[n], NT)
        out = p_scr[...].astype(jnp.bfloat16)
        full[0:row_blocks] = out
        full[row_blocks] = head[row_blocks]
        term[0:row_blocks] = out
        term[row_blocks] = head[row_blocks]

    @pl.when(jnp.logical_not(active))
    def _():
        full[...] = held[...]


def last_kernel(last, n_terms, *refs):
    pos, index = refs[:2]
    terms = refs[2 : 2 + n_terms]
    blocks, full, back, images, w_scr, x_scr = refs[2 + n_terms :]
    row_blocks = w_scr.shape[0]
    base = row_blocks + 1
    batches, slices, _ = images.shape
    active = pos[0] == last

    @pl.when(active)
    def _():
        weights_of(terms, row_blocks, w_scr)
        x_scr[...] = full[base : base + CB].astype(jnp.float32)
        back_project(index, blocks, w_scr, x_scr)
        for c in range(CB):
            value = x_scr[c].reshape(batches, slices, BS)
            images[:, :, c * BS : (c + 1) * BS] = value.astype(jnp.bfloat16)

    @pl.when(jnp.logical_not(active))
    def _():
        for c in range(CB):
            value = back[base + c].astype(jnp.float32).reshape(batches, slices, BS)
            images[:, :, c * BS : (c + 1) * BS] = value.astype(jnp.bfloat16)


def per_device(blocks, block_rows, block_cols, sinogram):
    blocks = blocks[0, 0]
    index = jnp.concatenate([block_rows[0], block_cols[0]], axis=0)
    batches, per_batch, rays_here = sinogram.shape
    slices = batches * per_batch
    quarter = rays_here // BS
    subsets = lax.axis_size("subset")
    tiles = lax.axis_size("tile")
    row_blocks = quarter * tiles
    pos = jnp.stack([lax.axis_index("subset"), lax.axis_index("tile")]).astype(jnp.int32)
    rays = sinogram.reshape(slices, quarter, BS).transpose(1, 0, 2)
    axes = ("subset", "tile")

    def moved(value, sources, by, turn=0):
        pairs = [
            (s * tiles + t, (s + by) * tiles + (t + turn) % tiles)
            for s in sources
            for t in range(tiles)
            if 0 <= s + by < subsets
        ]
        return lax.ppermute(value, axes, pairs)

    full_shape = jax.ShapeDtypeStruct((row_blocks + 1 + CB, slices, BS), jnp.bfloat16)
    term_shape = jax.ShapeDtypeStruct((row_blocks + 1, slices, BS), jnp.bfloat16)
    w_scr = pltpu.VMEM((row_blocks, slices, BS), jnp.bfloat16)
    x_scr = pltpu.VMEM((CB, slices, BS), jnp.float32)
    p_scr = pltpu.VMEM((row_blocks, slices, BS), jnp.float32)

    from_even = moved(blocks, range(0, subsets, 2), 1)
    from_odd = moved(blocks, range(1, subsets, 2), 1)
    head = pl.pallas_call(
        head_kernel,
        out_shape=term_shape,
        in_specs=[SMEM, SMEM, VMEM, VMEM],
        out_specs=VMEM,
        scratch_shapes=[pltpu.VMEM((row_blocks, 8, BS), jnp.float32)],
        compiler_params=PARAMS,
        name="head",
    )(pos, index, blocks, rays)
    index_prev = moved(index, range(subsets), 1)

    term = head
    full = jnp.zeros(full_shape.shape, full_shape.dtype)
    for step in range(1, subsets):
        image = None
        if tiles <= DIRECT:
            first = term if step == 1 else full
            terms = [moved(first, [step - 1], 1)]
            if step > 1:
                image = terms[0]
            terms += [moved(term, [step - 1], 1, turn) for turn in range(1, tiles)]
            n_terms = tiles
        else:
            summed = lax.psum(term.astype(jnp.float32), "tile")
            terms = [moved(summed, [step - 1], 1)]
            n_terms = 1
            if step > 1:
                image = moved(full, [step - 1], 1)
        operands = list(terms)
        if image is not None and tiles > DIRECT:
            operands.append(image)
        blocks_prev = from_even if step % 2 else from_odd

        def body(*refs, step=step, n_terms=n_terms, image=image):
            refs = list(refs)
            at = 3 + n_terms
            if image is not None:
                if tiles <= DIRECT:
                    refs.insert(at, (refs[3], row_blocks + 1))
                else:
                    refs[at] = (refs[at], row_blocks + 1)
            step_kernel(step, n_terms, image is not None, *refs)

        full, term = pl.pallas_call(
            body,
            out_shape=(full_shape, term_shape),
            in_specs=[SMEM] * 3 + [VMEM] * (len(operands) + 5),
            out_specs=(VMEM, VMEM),
            scratch_shapes=[w_scr, x_scr, p_scr],
            compiler_params=PARAMS,
            name="step",
        )(pos, index_prev, index, *operands, blocks_prev, blocks, rays, head, full)

    last = subsets - 1
    if tiles <= DIRECT:
        terms = [term] + [moved(term, [last], 0, turn) for turn in range(1, tiles)]
    else:
        terms = [lax.psum(term.astype(jnp.float32), "tile")]
    back = moved(full, range(1, subsets), -1)
    images = pl.pallas_call(
        functools.partial(last_kernel, last, len(terms)),
        out_shape=jax.ShapeDtypeStruct((batches, per_batch, PIX), jnp.bfloat16),
        in_specs=[SMEM] * 2 + [VMEM] * (len(terms) + 3),
        out_specs=VMEM,
        scratch_shapes=[w_scr, x_scr],
        compiler_params=PARAMS,
        name="last",
    )(pos, index, *terms, blocks, full, back)
    return images[None]


def solution(mesh):
    in_specs = (
        P("subset", "tile", None, None, None),
        P("subset", "tile", None),
        P("subset", "tile", None),
        P(None, None, ("subset", "tile")),
    )
    out_specs = P("subset", None, None, "tile")
    return jax.shard_map(
        per_device, mesh=mesh, in_specs=in_specs, out_specs=out_specs, check_vma=False
    )
```

```python
import functools

import jax
import jax.numpy as jnp
from jax import lax
from jax.experimental import pallas as pl
from jax.experimental.pallas import tpu as pltpu
from jax.sharding import PartitionSpec as P

BS = 128
PIX = 4096
CB = PIX // BS
relaxation = 0.5

NN = (((1,), (0,)), ((), ()))
NT = (((1,), (1,)), ((), ()))
VMEM = pl.BlockSpec(memory_space=pltpu.VMEM)
SMEM = pl.BlockSpec(memory_space=pltpu.SMEM)
PARAMS = pltpu.CompilerParams(vmem_limit_bytes=20 * 2**20)


def dot(lhs, rhs, dims):
    return lax.dot_general(lhs, rhs, dims, preferred_element_type=jnp.float32)


def head_kernel(row_blocks, rows, cols, blocks, rays, note, table, seen):
    count = blocks.shape[2]
    each = count // row_blocks
    batches, per_batch, here = rays.shape
    quarter = here // BS
    half = note.shape[1]
    for r in range(row_blocks):
        seen[r] = r * each
    for n in range(count):
        row = rows[0, 0, n]
        at = seen[row]
        seen[row] = at + 1
        table[0, at] = n
        table[1, at] = cols[0, 0, n]
    group = half // per_batch
    for h in range(2):
        for i in range(quarter):
            parts = [rays[h * group + g, :, i * BS : (i + 1) * BS] for g in range(group)]
            note[h * quarter + i] = jnp.concatenate(parts, axis=0)
    ones = jnp.ones((16, BS), jnp.bfloat16)
    for r in range(row_blocks):
        squares = 0.0
        for k in range(each):
            block = blocks[0, 0, table[0, r * each + k]].astype(jnp.float32)
            squares = squares + block * block
        total = 0.0
        for _ in range(3):
            part = squares.astype(jnp.bfloat16)
            total = total + dot(ones, part, NT)
            squares = squares - part.astype(jnp.float32)
        note[2 * quarter, r : r + 1] = total[0:1]


def weights(core, note, terms, w_scr):
    tiles, slabs, _, _ = note.shape
    quarter = (slabs - 1) // 2
    row_blocks = w_scr.shape[0]
    norms = note[0, slabs - 1, 0:row_blocks]
    for t in range(1, tiles):
        norms = norms + note[t, slabs - 1, 0:row_blocks]
    scale = relaxation / norms
    for r in range(row_blocks):
        left = note[r // quarter, core * quarter + r % quarter]
        if terms is not None:
            total = terms[0, r].astype(jnp.float32)
            for t in range(1, tiles):
                total = total + terms[t, r].astype(jnp.float32)
            left = left - total
        w_scr[r] = (left * scale[r : r + 1]).astype(jnp.bfloat16)


def back_project(table, blocks, w_scr, image):
    row_blocks = w_scr.shape[0]
    count = blocks.shape[2]
    each = count // row_blocks
    for k in range(count):
        col = table[1, k]
        image[col] = image[col] + dot(w_scr[k // each], blocks[0, 0, table[0, k]], NN)


def project(table, blocks, image, terms):
    row_blocks = terms.shape[0]
    each = blocks.shape[2] // row_blocks
    for r in range(row_blocks):
        total = 0.0
        for k in range(r * each, (r + 1) * each):
            total = total + dot(image[table[1, k]], blocks[0, 0, table[0, k]], NT)
        terms[r] = total.astype(jnp.bfloat16)


def on_core(pos, place, run, own, other):
    active = pos[0] == place

    @pl.when(jnp.logical_and(active, pos[1] == 0))
    def _():
        run(own, other)

    @pl.when(jnp.logical_and(active, pos[1] == 1))
    def _():
        run(other, own)

    return active


def first_kernel(place, has_image, *refs):
    refs = list(refs)
    pos, table, table2, note, note2, blocks, blocks2 = refs[:7]
    refs = refs[7:]
    terms_in, image_in = None, None
    if has_image:
        terms_in, image_in = refs[:2]
        refs = refs[2:]
    image, shot, terms, w_scr = refs

    def run(first, second):
        weights(pos[1], first[1], terms_in, w_scr)
        if has_image:
            image[...] = image_in[...].astype(jnp.float32)
        else:
            image[...] = jnp.zeros_like(image)
        back_project(first[0], first[2], w_scr, image)
        shot[...] = image[...].astype(jnp.bfloat16)
        project(second[0], second[2], shot, terms)

    on_core(pos, place, run, (table, note, blocks), (table2, note2, blocks2))


def second_kernel(place, *refs):
    pos, table, table2, note, note2, blocks, blocks2 = refs[:7]
    terms_in, image_in, shot, kept_in, given_in = refs[7:12]
    image, kept, given, w_scr, x_scr = refs[12:]

    def run(first, second):
        weights(pos[1], second[1], terms_in, w_scr)
        x_scr[...] = image_in[...]
        back_project(second[0], second[2], w_scr, x_scr)
        out = x_scr[...].astype(jnp.bfloat16)
        image[...] = out

        @pl.when(pos[1] == 0)
        def _():
            kept[...] = shot[...]
            given[...] = out

        @pl.when(pos[1] == 1)
        def _():
            kept[...] = out
            given[...] = shot[...]

    active = on_core(pos, place, run, (table, note, blocks), (table2, note2, blocks2))

    @pl.when(jnp.logical_not(active))
    def _():
        kept[...] = kept_in[...]
        given[...] = given_in[...]


def project_kernel(place, pos, table, table2, image, blocks, blocks2, terms):
    def run(first, second):
        project(first[0], first[1], image, terms)

    on_core(pos, place, run, (table, blocks), (table2, blocks2))


def last_kernel(pos, kept, given, images):
    batches, per_batch, _ = images.shape
    half = kept.shape[1]
    group = half // per_batch

    def write(refs):
        for c in range(CB):
            for h in range(2):
                value = refs[h][c].astype(jnp.float32).reshape(group, per_batch, BS)
                where = slice(h * group, (h + 1) * group)
                images[where, :, c * BS : (c + 1) * BS] = value.astype(jnp.bfloat16)

    @pl.when(pos[1] == 0)
    def _():
        write((kept, given))

    @pl.when(pos[1] == 1)
    def _():
        write((given, kept))


def per_device(blocks, block_rows, block_cols, sinogram):
    batches, per_batch, here = sinogram.shape
    half = batches * per_batch // 2
    quarter = here // BS
    count = blocks.shape[2]
    subsets = lax.axis_size("subset")
    tiles = lax.axis_size("tile")
    row_blocks = quarter * tiles
    places = subsets // 2
    subset = lax.axis_index("subset")
    pos = jnp.stack([subset // 2, subset % 2]).astype(jnp.int32)

    image_shape = (CB, half, BS)
    image_out = jax.ShapeDtypeStruct(image_shape, jnp.bfloat16)
    terms_out = jax.ShapeDtypeStruct((row_blocks, half, BS), jnp.bfloat16)
    w_scr = pltpu.VMEM((row_blocks, half, BS), jnp.bfloat16)
    x_scr = pltpu.VMEM(image_shape, jnp.float32)

    def swapped(value):
        return lax.ppermute(value, "subset", [(s, s ^ 1) for s in range(subsets)])

    def call(kernel, smem, operands, out_shape, scratch, name):
        many = isinstance(out_shape, tuple)
        return pl.pallas_call(
            kernel,
            out_shape=out_shape,
            in_specs=[SMEM] * smem + [VMEM] * (len(operands) - smem),
            out_specs=(VMEM,) * len(out_shape) if many else VMEM,
            scratch_shapes=scratch,
            compiler_params=PARAMS,
            name=name,
        )(*operands)

    blocks2 = swapped(blocks)
    note, table = pl.pallas_call(
        functools.partial(head_kernel, row_blocks),
        out_shape=(
            jax.ShapeDtypeStruct((2 * quarter + 1, half, BS), jnp.float32),
            jax.ShapeDtypeStruct((2, count), jnp.int32),
        ),
        in_specs=[SMEM, SMEM, VMEM, VMEM],
        out_specs=(VMEM, SMEM),
        scratch_shapes=[pltpu.SMEM((row_blocks,), jnp.int32)],
        compiler_params=PARAMS,
        name="head",
    )(block_rows, block_cols, blocks, sinogram)
    table2 = swapped(table)
    note = lax.all_gather(note, "tile")
    note2 = swapped(note)

    kept = jnp.zeros(image_shape, jnp.bfloat16)
    given = kept
    image = None
    for place in range(places):
        fixed = [pos, table, table2, note, note2, blocks, blocks2]
        extra = []
        if place > 0:
            pairs = [(2 * place - 2 + c, 2 * place + c) for c in range(2)]
            image = lax.ppermute(image, "subset", pairs)
            terms = call(
                functools.partial(project_kernel, place),
                3,
                [pos, table, table2, image, blocks, blocks2],
                terms_out,
                [],
                "project",
            )
            extra = [lax.all_gather(terms, "tile"), image]
        image32, shot, terms = call(
            functools.partial(first_kernel, place, place > 0),
            3,
            fixed + extra,
            (jax.ShapeDtypeStruct(image_shape, jnp.float32), image_out, terms_out),
            [w_scr],
            "first",
        )
        terms = lax.all_gather(terms, "tile")
        image, kept, given = call(
            functools.partial(second_kernel, place),
            3,
            fixed + [terms, image32, shot, kept, given],
            (image_out, image_out, image_out),
            [w_scr, x_scr],
            "second",
        )
    images = call(
        last_kernel,
        1,
        [pos, kept, swapped(given)],
        jax.ShapeDtypeStruct((batches, per_batch, PIX), jnp.bfloat16),
        [],
        "last",
    )
    return images[None]


def solution(mesh):
    in_specs = (
        P("subset", "tile", None, None, None),
        P("subset", "tile", None),
        P("subset", "tile", None),
        P(None, None, ("subset", "tile")),
    )
    out_specs = P("subset", None, None, "tile")
    return jax.shard_map(
        per_device, mesh=mesh, in_specs=in_specs, out_specs=out_specs, check_vma=False
    )
```

```python
import functools

import jax
import jax.numpy as jnp
from jax import lax
from jax.experimental import pallas as pl
from jax.experimental.pallas import tpu as pltpu
from jax.sharding import PartitionSpec as P

BS = 128
PIX = 4096
CB = PIX // BS
relaxation = 0.5

DIRECT = 4

NN = (((1,), (0,)), ((), ()))
NT = (((1,), (1,)), ((), ()))
VMEM = pl.BlockSpec(memory_space=pltpu.VMEM)
SMEM = pl.BlockSpec(memory_space=pltpu.SMEM)
PARAMS = pltpu.CompilerParams(vmem_limit_bytes=20 * 2**20)


def dot(lhs, rhs, dims):
    return lax.dot_general(lhs, rhs, dims, preferred_element_type=jnp.float32)


def head_kernel(row_blocks, chunks, pos, rows_in, cols_in, blocks_in, rays_in, *refs):
    note, note2, table, blocks, rows, cols, rays, seen, squares, sems = refs
    count = blocks.shape[2]
    each = count // row_blocks
    per_chunk = count // chunks
    batches, per_batch, here = rays.shape
    quarter = here // BS
    half = note.shape[1]
    group = half // per_batch
    small = [
        pltpu.make_async_copy(src, dst, sems.at[i])
        for i, (src, dst) in enumerate(((rows_in, rows), (cols_in, cols), (rays_in, rays)))
    ]
    large = []
    for k in range(chunks):
        where = pl.ds(k * per_chunk, per_chunk)
        large.append(
            pltpu.make_async_copy(
                blocks_in.at[0, 0, where], blocks.at[0, 0, where], sems.at[3 + k]
            )
        )
    for copy in small + large:
        copy.start()
    squares[...] = jnp.zeros_like(squares)
    for copy in small:
        copy.wait()
    for r in range(row_blocks):
        seen[r] = r * each
    for n in range(count):
        row = rows[0, 0, n]
        at = seen[row]
        seen[row] = at + 1
        table[0, at] = n
        table[1, at] = cols[0, 0, n]
    for out, core in ((note, pos[1]), (note2, 1 - pos[1])):
        for i in range(quarter):
            parts = [
                rays[core * group + g, :, i * BS : (i + 1) * BS] for g in range(group)
            ]
            out[i] = jnp.concatenate(parts, axis=0)
    for k in range(chunks):
        large[k].wait()
        for n in range(k * per_chunk, (k + 1) * per_chunk):
            block = blocks[0, 0, n].astype(jnp.float32)
            row = rows[0, 0, n]
            squares[row] = squares[row] + block * block
    ones = jnp.ones((16, BS), jnp.bfloat16)
    for r in range(row_blocks):
        left = squares[r]
        total = 0.0
        for _ in range(2):
            part = left.astype(jnp.bfloat16)
            total = total + dot(ones, part, NT)
            left = left - part.astype(jnp.float32)
        note[quarter, r : r + 1] = total[0:1]
        note2[quarter, r : r + 1] = total[0:1]


def slabs(refs, *where):
    if len(refs) > 1:
        return [ref[where] for ref in refs]
    return [refs[0][(t,) + where] for t in range(refs[0].shape[0])]


def weights(pos, notes, terms, w_scr, rays_scr):
    row_blocks = w_scr.shape[0]
    quarter = rays_scr.shape[1]
    norms = sum(slabs(notes, quarter))[0:row_blocks]
    scale = relaxation / norms
    if len(notes) > 1:
        for d, ref in enumerate(notes):
            rays_scr[pos[2] ^ d] = ref[0:quarter]
    else:
        rays_scr[...] = notes[0][:, 0:quarter]
    for r in range(row_blocks):
        left = rays_scr[r // quarter, r % quarter]
        if terms is not None:
            left = left - sum(part.astype(jnp.float32) for part in slabs(terms, r))
        w_scr[r] = (left * scale[r : r + 1]).astype(jnp.bfloat16)


def back_project(table, blocks, w_scr, image):
    row_blocks = w_scr.shape[0]
    count = blocks.shape[2]
    each = count // row_blocks
    for k in range(count):
        col = table[1, k]
        image[col] = image[col] + dot(w_scr[k // each], blocks[0, 0, table[0, k]], NN)


def project(table, blocks, image, terms):
    row_blocks = terms.shape[0]
    each = blocks.shape[2] // row_blocks
    for r in range(row_blocks):
        total = 0.0
        for k in range(r * each, (r + 1) * each):
            total = total + dot(image[table[1, k]], blocks[0, 0, table[0, k]], NT)
        terms[r] = total.astype(jnp.bfloat16)


def take(refs, n):
    taken = refs[:n]
    del refs[:n]
    return taken


def on_core(pos, place, run, own, other):
    active = pos[0] == place

    @pl.when(jnp.logical_and(active, pos[1] == 0))
    def _():
        run(own, other)

    @pl.when(jnp.logical_and(active, pos[1] == 1))
    def _():
        run(other, own)

    return active


def first_kernel(place, n_notes, n_terms, *refs):
    refs = list(refs)
    pos, table, table2, blocks, blocks2 = take(refs, 5)
    notes, notes2 = take(refs, n_notes), take(refs, n_notes)
    terms_in, image_in = None, None
    if n_terms:
        terms_in = take(refs, n_terms)
        (image_in,) = take(refs, 1)
    image, shot, terms, w_scr, rays_scr = refs

    def run(first, second):
        weights(pos, first[1], terms_in, w_scr, rays_scr)
        if n_terms:
            image[...] = image_in[...].astype(jnp.float32)
        else:
            image[...] = jnp.zeros_like(image)
        back_project(first[0], first[2], w_scr, image)
        shot[...] = image[...].astype(jnp.bfloat16)
        project(second[0], second[2], shot, terms)

    on_core(pos, place, run, (table, notes, blocks), (table2, notes2, blocks2))


def second_kernel(place, n_notes, n_terms, *refs):
    refs = list(refs)
    pos, table, table2, blocks, blocks2 = take(refs, 5)
    notes, notes2 = take(refs, n_notes), take(refs, n_notes)
    terms_in = take(refs, n_terms)
    image_in, shot, kept_in, given_in = take(refs, 4)
    image, kept, given, w_scr, rays_scr, x_scr = refs

    def run(first, second):
        weights(pos, second[1], terms_in, w_scr, rays_scr)
        x_scr[...] = image_in[...]
        back_project(second[0], second[2], w_scr, x_scr)
        out = x_scr[...].astype(jnp.bfloat16)
        image[...] = out

        @pl.when(pos[1] == 0)
        def _():
            kept[...] = shot[...]
            given[...] = out

        @pl.when(pos[1] == 1)
        def _():
            kept[...] = out
            given[...] = shot[...]

    active = on_core(pos, place, run, (table, notes, blocks), (table2, notes2, blocks2))

    @pl.when(jnp.logical_not(active))
    def _():
        kept[...] = kept_in[...]
        given[...] = given_in[...]


def project_kernel(place, pos, table, table2, image, blocks, blocks2, terms):
    def run(first, second):
        project(first[0], first[1], image, terms)

    on_core(pos, place, run, (table, blocks), (table2, blocks2))


def last_kernel(pos, kept, given, images):
    batches, per_batch, _ = images.shape
    half = kept.shape[1]
    group = half // per_batch

    def write(refs):
        for c in range(CB):
            for h in range(2):
                value = refs[h][c].astype(jnp.float32).reshape(group, per_batch, BS)
                where = slice(h * group, (h + 1) * group)
                images[where, :, c * BS : (c + 1) * BS] = value.astype(jnp.bfloat16)

    @pl.when(pos[1] == 0)
    def _():
        write((kept, given))

    @pl.when(pos[1] == 1)
    def _():
        write((given, kept))


def per_device(blocks, block_rows, block_cols, sinogram):
    batches, per_batch, here = sinogram.shape
    half = batches * per_batch // 2
    quarter = here // BS
    count = blocks.shape[2]
    subsets = lax.axis_size("subset")
    tiles = lax.axis_size("tile")
    row_blocks = quarter * tiles
    places = subsets // 2
    direct = tiles <= DIRECT
    subset = lax.axis_index("subset")
    pos = jnp.stack([subset // 2, subset % 2, lax.axis_index("tile")]).astype(jnp.int32)

    image_shape = (CB, half, BS)
    image_out = jax.ShapeDtypeStruct(image_shape, jnp.bfloat16)
    terms_out = jax.ShapeDtypeStruct((row_blocks, half, BS), jnp.bfloat16)
    note_out = jax.ShapeDtypeStruct((quarter + 1, half, BS), jnp.float32)
    w_scr = pltpu.VMEM((row_blocks, half, BS), jnp.bfloat16)
    rays_scr = pltpu.VMEM((tiles, quarter, half, BS), jnp.float32)
    x_scr = pltpu.VMEM(image_shape, jnp.float32)

    def swapped(value):
        return lax.ppermute(value, "subset", [(s, s ^ 1) for s in range(subsets)])

    def turned(value, d, other=0):
        pairs = [
            (s * tiles + t, (s ^ other) * tiles + (t ^ d))
            for s in range(subsets)
            for t in range(tiles)
        ]
        return lax.ppermute(value, ("subset", "tile"), pairs)

    def spread(value):
        if direct:
            return [value] + [turned(value, d) for d in range(1, tiles)]
        return [lax.all_gather(value, "tile")]

    def call(kernel, smem, operands, out_shape, scratch, name):
        many = isinstance(out_shape, tuple)
        return pl.pallas_call(
            kernel,
            out_shape=out_shape,
            in_specs=[SMEM] * smem + [VMEM] * (len(operands) - smem),
            out_specs=(VMEM,) * len(out_shape) if many else VMEM,
            scratch_shapes=scratch,
            compiler_params=PARAMS,
            name=name,
        )(*operands)

    blocks2 = swapped(blocks)
    chunks = 8 if count % 8 == 0 else 1
    note, note2, table, blocks = pl.pallas_call(
        functools.partial(head_kernel, row_blocks, chunks),
        out_shape=(
            note_out,
            note_out,
            jax.ShapeDtypeStruct((2, count), jnp.int32),
            pltpu.VMEM(blocks.shape, blocks.dtype),
        ),
        in_specs=[SMEM] + [pl.BlockSpec(memory_space=pltpu.HBM)] * 4,
        out_specs=(VMEM, VMEM, SMEM, VMEM),
        scratch_shapes=[
            pltpu.SMEM(block_rows.shape, jnp.int32),
            pltpu.SMEM(block_cols.shape, jnp.int32),
            pltpu.VMEM(sinogram.shape, jnp.float32),
            pltpu.SMEM((row_blocks,), jnp.int32),
            pltpu.VMEM((row_blocks, BS, BS), jnp.float32),
            pltpu.SemaphoreType.DMA((3 + chunks,)),
        ],
        compiler_params=PARAMS,
        name="head",
    )(
        pos,
        *(
            pltpu.with_memory_space_constraint(value, pltpu.HBM)
            for value in (block_rows, block_cols, blocks, sinogram)
        ),
    )
    notes = spread(note)
    if direct:
        notes2 = [turned(note2, d, 1) for d in range(tiles)]
    else:
        notes2 = spread(swapped(note2))
    table2 = swapped(table)
    blocks2 = pltpu.with_memory_space_constraint(blocks2, pltpu.VMEM)

    kept = jnp.zeros(image_shape, jnp.bfloat16)
    given = kept
    image = None
    for place in range(places):
        fixed = [pos, table, table2, blocks, blocks2]
        extra = []
        if place > 0:
            pairs = [(2 * place - 2 + c, 2 * place + c) for c in range(2)]
            image = lax.ppermute(image, "subset", pairs)
            terms = call(
                functools.partial(project_kernel, place),
                3,
                [pos, table, table2, image, blocks, blocks2],
                terms_out,
                [],
                "project",
            )
            extra = spread(terms) + [image]
        image32, shot, terms = call(
            functools.partial(first_kernel, place, len(notes), max(len(extra) - 1, 0)),
            3,
            fixed + notes + notes2 + extra,
            (jax.ShapeDtypeStruct(image_shape, jnp.float32), image_out, terms_out),
            [w_scr, rays_scr],
            "first",
        )
        terms = spread(terms)
        image, kept, given = call(
            functools.partial(second_kernel, place, len(notes), len(terms)),
            3,
            fixed + notes + notes2 + terms + [image32, shot, kept, given],
            (image_out, image_out, image_out),
            [w_scr, rays_scr, x_scr],
            "second",
        )
    images = call(
        last_kernel,
        1,
        [pos, kept, swapped(given)],
        jax.ShapeDtypeStruct((batches, per_batch, PIX), jnp.bfloat16),
        [],
        "last",
    )
    return images[None]


def solution(mesh):
    in_specs = (
        P("subset", "tile", None, None, None),
        P("subset", "tile", None),
        P("subset", "tile", None),
        P(None, None, ("subset", "tile")),
    )
    out_specs = P("subset", None, None, "tile")
    return jax.shard_map(
        per_device, mesh=mesh, in_specs=in_specs, out_specs=out_specs, check_vma=False
    )
```

```python
import functools

import jax
import jax.numpy as jnp
from jax import lax
from jax.experimental import pallas as pl
from jax.experimental.pallas import tpu as pltpu
from jax.sharding import PartitionSpec as P

BS = 128
PIX = 4096
CB = PIX // BS
relaxation = 0.5

DIRECT = 4

NN = (((1,), (0,)), ((), ()))
NT = (((1,), (1,)), ((), ()))
VMEM = pl.BlockSpec(memory_space=pltpu.VMEM)
SMEM = pl.BlockSpec(memory_space=pltpu.SMEM)
PARAMS = pltpu.CompilerParams(vmem_limit_bytes=20 * 2**20)


def dot(lhs, rhs, dims):
    return lax.dot_general(lhs, rhs, dims, preferred_element_type=jnp.float32)


def head_kernel(row_blocks, chunks, pos, rows_in, cols_in, blocks_in, rays_in, *refs):
    note, note2, table, blocks, rows, cols, rays, seen, squares, sems = refs
    count = blocks.shape[2]
    each = count // row_blocks
    per_chunk = count // chunks
    batches, per_batch, here = rays.shape
    quarter = here // BS
    half = note.shape[1]
    group = half // per_batch
    small = [
        pltpu.make_async_copy(src, dst, sems.at[i])
        for i, (src, dst) in enumerate(((rows_in, rows), (cols_in, cols), (rays_in, rays)))
    ]
    large = []
    for k in range(chunks):
        where = pl.ds(k * per_chunk, per_chunk)
        large.append(
            pltpu.make_async_copy(
                blocks_in.at[0, 0, where], blocks.at[0, 0, where], sems.at[3 + k]
            )
        )
    for copy in small + large:
        copy.start()
    squares[...] = jnp.zeros_like(squares)
    for copy in small:
        copy.wait()
    for r in range(row_blocks):
        seen[r] = r * each
    for n in range(count):
        row = rows[0, 0, n]
        at = seen[row]
        seen[row] = at + 1
        table[0, at] = n
        table[1, at] = cols[0, 0, n]
    for out, core in ((note, pos[1]), (note2, 1 - pos[1])):
        for i in range(quarter):
            parts = [
                rays[core * group + g, :, i * BS : (i + 1) * BS] for g in range(group)
            ]
            out[i] = jnp.concatenate(parts, axis=0)
    for k in range(chunks):
        large[k].wait()
        for n in range(k * per_chunk, (k + 1) * per_chunk):
            block = blocks[0, 0, n].astype(jnp.float32)
            row = rows[0, 0, n]
            squares[row] = squares[row] + block * block
    ones = jnp.ones((16, BS), jnp.bfloat16)
    for r in range(row_blocks):
        left = squares[r]
        total = 0.0
        for _ in range(2):
            part = left.astype(jnp.bfloat16)
            total = total + dot(ones, part, NT)
            left = left - part.astype(jnp.float32)
        note[quarter, r : r + 1] = total[0:1]
        note2[quarter, r : r + 1] = total[0:1]


def slabs(refs, *where):
    if len(refs) > 1:
        return [ref[where] for ref in refs]
    return [refs[0][(t,) + where] for t in range(refs[0].shape[0])]


def gather_rays(pos, notes, slot, rays_scr):
    row_blocks = rays_scr.shape[0] * rays_scr.shape[1]
    quarter = rays_scr.shape[1]
    norms = sum(slabs(notes, slot, quarter))[0:row_blocks]
    if len(notes) > 1:
        for d, ref in enumerate(notes):
            rays_scr[pos[2] ^ d] = ref[slot, 0:quarter]
    else:
        rays_scr[...] = notes[0][:, slot, 0:quarter]
    return relaxation / norms


def weights(pos, notes, slot, terms, w_scr, rays_scr):
    row_blocks = w_scr.shape[0]
    quarter = rays_scr.shape[1]
    scale = gather_rays(pos, notes, slot, rays_scr)
    for r in range(row_blocks):
        left = rays_scr[r // quarter, r % quarter]
        if terms is not None:
            left = left - sum(part.astype(jnp.float32) for part in slabs(terms, r))
        w_scr[r] = (left * scale[r : r + 1]).astype(jnp.bfloat16)


def back_project(table, blocks, w_scr, image):
    row_blocks = w_scr.shape[0]
    count = blocks.shape[2]
    each = count // row_blocks
    for k in range(count):
        col = table[1, k]
        image[col] = image[col] + dot(w_scr[k // each], blocks[0, 0, table[0, k]], NN)


def project(table, blocks, image, terms):
    row_blocks = terms.shape[0]
    each = blocks.shape[2] // row_blocks
    for r in range(row_blocks):
        total = 0.0
        for k in range(r * each, (r + 1) * each):
            total = total + dot(image[table[1, k]], blocks[0, 0, table[0, k]], NT)
        terms[r] = total.astype(jnp.bfloat16)


def take(refs, n):
    taken = refs[:n]
    del refs[:n]
    return taken


def on_core(pos, place, run, own, other):
    active = pos[0] == place

    @pl.when(jnp.logical_and(active, pos[1] == 0))
    def _():
        run(own, other)

    @pl.when(jnp.logical_and(active, pos[1] == 1))
    def _():
        run(other, own)

    return active


def first_kernel(place, n_notes, *refs):
    refs = list(refs)
    pos, table, table2, blocks, blocks2 = take(refs, 5)
    notes = take(refs, n_notes)
    image, shot, terms, w_scr, rays_scr = refs

    def run(first, second):
        weights(pos, notes, first[1], None, w_scr, rays_scr)
        image[...] = jnp.zeros_like(image)
        back_project(first[0], first[2], w_scr, image)
        shot[...] = image[...].astype(jnp.bfloat16)
        project(second[0], second[2], shot, terms)

    on_core(pos, place, run, (table, 0, blocks), (table2, 1, blocks2))


def second_kernel(place, n_notes, n_terms, *refs):
    refs = list(refs)
    info, table, table2, blocks, blocks2 = take(refs, 5)
    pos = [info[0, i] for i in range(3)]
    notes = take(refs, n_notes)
    terms_in = take(refs, n_terms)
    image_in, shot = take(refs, 2)
    image, kept, given, w_scr, rays_scr, x_scr = refs

    def run(first, second):
        weights(pos, notes, second[1], terms_in, w_scr, rays_scr)
        x_scr[...] = image_in[...]
        back_project(second[0], second[2], w_scr, x_scr)
        image[...] = x_scr[...].astype(jnp.bfloat16)

        @pl.when(pos[1] == 0)
        def _():
            kept[...] = shot[...]
            given[...] = image[...]

        @pl.when(pos[1] == 1)
        def _():
            kept[...] = image[...]
            given[...] = shot[...]

    on_core(pos, place, run, (table, 0, blocks), (table2, 1, blocks2))


def pack_kernel(n_notes, *refs):
    refs = list(refs)
    pos, table, table2, blocks, blocks2 = take(refs, 5)
    notes = take(refs, n_notes)
    _, info, wide, tall, rays, rays_scr = refs
    row_blocks = wide.shape[1]
    each = wide.shape[3] // BS
    quarter = rays_scr.shape[1]
    for i in range(3):
        info[0, i] = pos[i]

    @pl.when(pos[0] > 0)
    def _():
        for slot, (tab, src) in enumerate(((table, blocks), (table2, blocks2))):
            at = pos[1] if slot == 0 else 1 - pos[1]
            scale = gather_rays(pos, notes, slot, rays_scr)
            for r in range(row_blocks):
                row = scale[r : r + 1]
                rays[at, r] = rays_scr[r // quarter, r % quarter] * row
                rays[at, row_blocks, r : r + 1] = row
                for j in range(each):
                    k = r * each + j
                    info[1 + at, k] = tab[1, k]
                    block = src[0, 0, tab[0, k]]
                    wide[at, r, :, j * BS : (j + 1) * BS] = block
                    tall[at, r, j * BS : (j + 1) * BS] = block.T


def packed_weights(rays, slot, terms, w_scr):
    row_blocks = w_scr.shape[0]
    for r in range(row_blocks):
        total = sum(part.astype(jnp.float32) for part in slabs(terms, r))
        scale = rays[slot, row_blocks, r : r + 1]
        w_scr[r] = (rays[slot, r] - total * scale).astype(jnp.bfloat16)


def packed_back(info, wide, slot, w_scr, image):
    row_blocks = wide.shape[1]
    each = wide.shape[3] // BS
    for r in range(row_blocks):
        back = dot(w_scr[r], wide[slot, r], NN)
        for j in range(each):
            col = info[1 + slot, r * each + j]
            image[col] = image[col] + back[:, j * BS : (j + 1) * BS]


def packed_project(info, tall, slot, image, terms):
    row_blocks = tall.shape[1]
    each = tall.shape[2] // BS
    for r in range(row_blocks):
        parts = [image[info[1 + slot, r * each + j]] for j in range(each)]
        total = dot(jnp.concatenate(parts, axis=1), tall[slot, r], NN)
        terms[r] = total.astype(jnp.bfloat16)


def later_first(place, n_terms, *refs):
    refs = list(refs)
    info, rays, wide, tall = take(refs, 4)
    terms_in = take(refs, n_terms)
    image_in, image, shot, terms, w_scr = refs

    @pl.when(info[0, 0] == place)
    def _():
        packed_weights(rays, 0, terms_in, w_scr)
        image[...] = image_in[...].astype(jnp.float32)
        packed_back(info, wide, 0, w_scr, image)
        shot[...] = image[...].astype(jnp.bfloat16)
        packed_project(info, tall, 1, shot, terms)


def later_second(place, n_terms, last, *refs):
    refs = list(refs)
    info, rays, wide = take(refs, 3)
    terms_in = take(refs, n_terms)
    image_in, shot, kept_in, given_in = take(refs, 4)
    image = None if last else take(refs, 1)[0]
    kept, given, w_scr, x_scr = refs
    active = info[0, 0] == place

    @pl.when(active)
    def _():
        packed_weights(rays, 1, terms_in, w_scr)
        x_scr[...] = image_in[...]
        packed_back(info, wide, 1, w_scr, x_scr)
        if not last:
            image[...] = x_scr[...].astype(jnp.bfloat16)

        @pl.when(info[0, 1] == 0)
        def _():
            kept[...] = shot[...]
            given[...] = x_scr[...].astype(jnp.bfloat16)

        @pl.when(info[0, 1] == 1)
        def _():
            kept[...] = x_scr[...].astype(jnp.bfloat16)
            given[...] = shot[...]

    @pl.when(jnp.logical_not(active))
    def _():
        kept[...] = kept_in[...]
        given[...] = given_in[...]


def later_project(place, info, image, tall, terms):
    @pl.when(info[0, 0] == place)
    def _():
        packed_project(info, tall, 0, image, terms)


def last_kernel(pos, kept, given, images):
    batches, per_batch, _ = images.shape
    half = kept.shape[1]
    group = half // per_batch

    def write(refs):
        for c in range(CB):
            for h in range(2):
                value = refs[h][c].astype(jnp.float32).reshape(group, per_batch, BS)
                where = slice(h * group, (h + 1) * group)
                images[where, :, c * BS : (c + 1) * BS] = value.astype(jnp.bfloat16)

    @pl.when(pos[1] == 0)
    def _():
        write((kept, given))

    @pl.when(pos[1] == 1)
    def _():
        write((given, kept))


def per_device(blocks, block_rows, block_cols, sinogram):
    batches, per_batch, here = sinogram.shape
    half = batches * per_batch // 2
    quarter = here // BS
    count = blocks.shape[2]
    subsets = lax.axis_size("subset")
    tiles = lax.axis_size("tile")
    row_blocks = quarter * tiles
    places = subsets // 2
    direct = tiles <= DIRECT
    subset = lax.axis_index("subset")
    pos = jnp.stack([subset // 2, subset % 2, lax.axis_index("tile")]).astype(jnp.int32)

    image_shape = (CB, half, BS)
    image_out = jax.ShapeDtypeStruct(image_shape, jnp.bfloat16)
    terms_out = jax.ShapeDtypeStruct((row_blocks, half, BS), jnp.bfloat16)
    note_out = jax.ShapeDtypeStruct((quarter + 1, half, BS), jnp.float32)
    w_scr = pltpu.VMEM((row_blocks, half, BS), jnp.bfloat16)
    rays_scr = pltpu.VMEM((tiles, quarter, half, BS), jnp.float32)
    x_scr = pltpu.VMEM(image_shape, jnp.float32)

    def swapped(value):
        return lax.ppermute(value, "subset", [(s, s ^ 1) for s in range(subsets)])

    def turned(value, d, other=0):
        pairs = [
            (s * tiles + t, (s ^ other) * tiles + (t ^ d))
            for s in range(subsets)
            for t in range(tiles)
        ]
        return lax.ppermute(value, ("subset", "tile"), pairs)

    def spread(value):
        if direct:
            return [value] + [turned(value, d) for d in range(1, tiles)]
        return [lax.all_gather(value, "tile")]

    def call(kernel, smem, operands, out_shape, scratch, name):
        many = isinstance(out_shape, tuple)
        return pl.pallas_call(
            kernel,
            out_shape=out_shape,
            in_specs=[SMEM] * smem + [VMEM] * (len(operands) - smem),
            out_specs=(VMEM,) * len(out_shape) if many else VMEM,
            scratch_shapes=scratch,
            compiler_params=PARAMS,
            name=name,
        )(*operands)

    blocks2 = swapped(blocks)
    chunks = 8 if count % 8 == 0 else 1
    note, note2, table, blocks = pl.pallas_call(
        functools.partial(head_kernel, row_blocks, chunks),
        out_shape=(
            note_out,
            note_out,
            jax.ShapeDtypeStruct((2, count), jnp.int32),
            pltpu.VMEM(blocks.shape, blocks.dtype),
        ),
        in_specs=[SMEM] + [pl.BlockSpec(memory_space=pltpu.HBM)] * 4,
        out_specs=(VMEM, VMEM, SMEM, VMEM),
        scratch_shapes=[
            pltpu.SMEM(block_rows.shape, jnp.int32),
            pltpu.SMEM(block_cols.shape, jnp.int32),
            pltpu.VMEM(sinogram.shape, jnp.float32),
            pltpu.SMEM((row_blocks,), jnp.int32),
            pltpu.VMEM((row_blocks, BS, BS), jnp.float32),
            pltpu.SemaphoreType.DMA((3 + chunks,)),
        ],
        compiler_params=PARAMS,
        name="head",
    )(
        pos,
        *(
            pltpu.with_memory_space_constraint(value, pltpu.HBM)
            for value in (block_rows, block_cols, blocks, sinogram)
        ),
    )
    notes = spread(jnp.stack([note, swapped(note2)]))
    table2 = swapped(table)
    blocks2 = pltpu.with_memory_space_constraint(blocks2, pltpu.VMEM)
    fixed = [pos, table, table2, blocks, blocks2]
    image32_out = jax.ShapeDtypeStruct(image_shape, jnp.float32)

    image32, shot, terms = call(
        functools.partial(first_kernel, 0, len(notes)),
        3,
        fixed + notes,
        (image32_out, image_out, terms_out),
        [w_scr, rays_scr],
        "first",
    )
    each = count // row_blocks
    info, wide, tall, rays = pl.pallas_call(
        functools.partial(pack_kernel, len(notes)),
        out_shape=(
            jax.ShapeDtypeStruct((3, count), jnp.int32),
            pltpu.VMEM((2, row_blocks, BS, each * BS), jnp.bfloat16),
            pltpu.VMEM((2, row_blocks, each * BS, BS), jnp.bfloat16),
            jax.ShapeDtypeStruct((2, row_blocks + 1, half, BS), jnp.float32),
        ),
        in_specs=[SMEM] * 3 + [VMEM] * (2 + len(notes)) + [pl.BlockSpec(memory_space=pl.ANY)],
        out_specs=(SMEM, VMEM, VMEM, VMEM),
        scratch_shapes=[rays_scr],
        compiler_params=PARAMS,
        name="pack",
    )(*fixed, *notes, terms)
    terms = spread(terms)
    fixed[0] = info
    image, kept, given = call(
        functools.partial(second_kernel, 0, len(notes), len(terms)),
        3,
        fixed + notes + terms + [image32, shot],
        (image_out, image_out, image_out),
        [w_scr, rays_scr, x_scr],
        "second",
    )

    for place in range(1, places):
        pairs = [
            (2 * p + c, 2 * ((2 * place - 1 - p) % places) + c)
            for p in range(places)
            for c in range(2)
        ]
        image = lax.ppermute(image, "subset", pairs)
        terms = call(
            functools.partial(later_project, place),
            1,
            [info, image, tall],
            terms_out,
            [],
            "project",
        )
        terms = spread(terms)
        image32, shot, terms = call(
            functools.partial(later_first, place, len(terms)),
            1,
            [info, rays, wide, tall] + terms + [image],
            (image32_out, image_out, terms_out),
            [w_scr],
            "first",
        )
        terms = spread(terms)
        last = place == places - 1
        outs = call(
            functools.partial(later_second, place, len(terms), last),
            1,
            [info, rays, wide] + terms + [image32, shot, kept, given],
            (image_out,) * (2 if last else 3),
            [w_scr, x_scr],
            "second",
        )
        kept, given = outs[-2:]
        image = outs[0]
    images = call(
        last_kernel,
        1,
        [pos, kept, swapped(given)],
        jax.ShapeDtypeStruct((batches, per_batch, PIX), jnp.bfloat16),
        [],
        "last",
    )
    return images[None]


def solution(mesh):
    in_specs = (
        P("subset", "tile", None, None, None),
        P("subset", "tile", None),
        P("subset", "tile", None),
        P(None, None, ("subset", "tile")),
    )
    out_specs = P("subset", None, None, "tile")
    return jax.shard_map(
        per_device, mesh=mesh, in_specs=in_specs, out_specs=out_specs, check_vma=False
    )
```

```python
import functools

import jax
import jax.numpy as jnp
from jax import lax
from jax.experimental import pallas as pl
from jax.experimental.pallas import tpu as pltpu
from jax.sharding import PartitionSpec as P

BS = 128
PIX = 4096
CB = PIX // BS
relaxation = 0.5

NN = (((1,), (0,)), ((), ()))
NT = (((1,), (1,)), ((), ()))
VMEM = pl.BlockSpec(memory_space=pltpu.VMEM)
SMEM = pl.BlockSpec(memory_space=pltpu.SMEM)
PARAMS = pltpu.CompilerParams(vmem_limit_bytes=20 * 2**20)


def dot(lhs, rhs, dims):
    return lax.dot_general(lhs, rhs, dims, preferred_element_type=jnp.float32)


def head_kernel(row_blocks, chunks, pos, rows_in, cols_in, blocks_in, rays_in, *refs):
    note, note2, table, blocks, rows, cols, rays, seen, squares, sems = refs
    count = blocks.shape[2]
    each = count // row_blocks
    per_chunk = count // chunks
    batches, per_batch, here = rays.shape
    quarter = here // BS
    half = note.shape[1]
    group = half // per_batch
    small = [
        pltpu.make_async_copy(src, dst, sems.at[i])
        for i, (src, dst) in enumerate(((rows_in, rows), (cols_in, cols), (rays_in, rays)))
    ]
    large = []
    for k in range(chunks):
        where = pl.ds(k * per_chunk, per_chunk)
        large.append(
            pltpu.make_async_copy(
                blocks_in.at[0, 0, where], blocks.at[0, 0, where], sems.at[3 + k]
            )
        )
    for copy in small + large:
        copy.start()
    squares[...] = jnp.zeros_like(squares)
    for copy in small:
        copy.wait()
    for r in range(row_blocks):
        seen[r] = r * each
    for n in range(count):
        row = rows[0, 0, n]
        at = seen[row]
        seen[row] = at + 1
        table[0, at] = n
        table[1, at] = cols[0, 0, n]
    for out, core in ((note, pos[1]), (note2, 1 - pos[1])):
        for i in range(quarter):
            parts = [
                rays[core * group + g, :, i * BS : (i + 1) * BS] for g in range(group)
            ]
            out[i] = jnp.concatenate(parts, axis=0)
    for k in range(chunks):
        large[k].wait()
        for n in range(k * per_chunk, (k + 1) * per_chunk):
            block = blocks[0, 0, n].astype(jnp.float32)
            row = rows[0, 0, n]
            squares[row] = squares[row] + block * block
    ones = jnp.ones((16, BS), jnp.bfloat16)
    for r in range(row_blocks):
        left = squares[r]
        total = 0.0
        for _ in range(2):
            part = left.astype(jnp.bfloat16)
            total = total + dot(ones, part, NT)
            left = left - part.astype(jnp.float32)
        note[quarter, r : r + 1] = total[0:1]
        note2[quarter, r : r + 1] = total[0:1]


def slabs(refs, *where):
    if len(refs) > 1:
        return [ref[where] for ref in refs]
    return [refs[0][(t,) + where] for t in range(refs[0].shape[0])]


def gather_rays(pos, notes, slot, rays_scr):
    row_blocks = rays_scr.shape[0] * rays_scr.shape[1]
    quarter = rays_scr.shape[1]
    norms = sum(slabs(notes, slot, quarter))[0:row_blocks]
    if len(notes) > 1:
        for d, ref in enumerate(notes):
            rays_scr[pos[2] ^ d] = ref[slot, 0:quarter]
    else:
        rays_scr[...] = notes[0][:, slot, 0:quarter]
    return relaxation / norms


def weights(pos, notes, slot, terms, w_scr, rays_scr):
    row_blocks = w_scr.shape[0]
    quarter = rays_scr.shape[1]
    scale = gather_rays(pos, notes, slot, rays_scr)
    for r in range(row_blocks):
        left = rays_scr[r // quarter, r % quarter]
        if terms is not None:
            left = left - sum(part.astype(jnp.float32) for part in slabs(terms, r))
        w_scr[r] = (left * scale[r : r + 1]).astype(jnp.bfloat16)


def back_project(table, blocks, w_scr, image):
    row_blocks = w_scr.shape[0]
    count = blocks.shape[2]
    each = count // row_blocks
    for k in range(count):
        col = table[1, k]
        image[col] = image[col] + dot(w_scr[k // each], blocks[0, 0, table[0, k]], NN)


def project(table, blocks, image, terms):
    tiles, row_blocks, _, _ = terms.shape
    each = blocks.shape[2] // row_blocks
    for r in range(row_blocks):
        total = 0.0
        for k in range(r * each, (r + 1) * each):
            total = total + dot(image[table[1, k]], blocks[0, 0, table[0, k]], NT)
        total = total.astype(jnp.bfloat16)
        for t in range(tiles):
            terms[t, r] = total


def take(refs, n):
    taken = refs[:n]
    del refs[:n]
    return taken


def on_core(pos, place, run, own, other):
    active = pos[0] == place

    @pl.when(jnp.logical_and(active, pos[1] == 0))
    def _():
        run(own, other)

    @pl.when(jnp.logical_and(active, pos[1] == 1))
    def _():
        run(other, own)

    return active


def first_kernel(place, n_notes, *refs):
    refs = list(refs)
    pos, table, table2, blocks, blocks2 = take(refs, 5)
    notes = take(refs, n_notes)
    image, shot, terms, w_scr, rays_scr = refs

    def run(first, second):
        weights(pos, notes, first[1], None, w_scr, rays_scr)
        image[...] = jnp.zeros_like(image)
        back_project(first[0], first[2], w_scr, image)
        shot[...] = image[...].astype(jnp.bfloat16)
        project(second[0], second[2], shot, terms)

    on_core(pos, place, run, (table, 0, blocks), (table2, 1, blocks2))


def second_kernel(place, n_notes, n_terms, *refs):
    refs = list(refs)
    info, table, table2, blocks, blocks2 = take(refs, 5)
    pos = [info[0, i] for i in range(3)]
    notes = take(refs, n_notes)
    terms_in = take(refs, n_terms)
    image_in, shot = take(refs, 2)
    image, kept, given, w_scr, rays_scr, x_scr = refs

    def run(first, second):
        weights(pos, notes, second[1], terms_in, w_scr, rays_scr)
        x_scr[...] = image_in[...]
        back_project(second[0], second[2], w_scr, x_scr)
        image[...] = x_scr[...].astype(jnp.bfloat16)

        @pl.when(pos[1] == 0)
        def _():
            kept[...] = shot[...]
            given[...] = image[...]

        @pl.when(pos[1] == 1)
        def _():
            kept[...] = image[...]
            given[...] = shot[...]

    on_core(pos, place, run, (table, 0, blocks), (table2, 1, blocks2))


def pack_kernel(n_notes, *refs):
    refs = list(refs)
    pos, table, table2, blocks, blocks2 = take(refs, 5)
    notes = take(refs, n_notes)
    _, info, wide, tall, rays, rays_scr = refs
    row_blocks = wide.shape[1]
    each = wide.shape[3] // BS
    quarter = rays_scr.shape[1]
    for i in range(3):
        info[0, i] = pos[i]

    @pl.when(pos[0] > 0)
    def _():
        for slot, (tab, src) in enumerate(((table, blocks), (table2, blocks2))):
            at = pos[1] if slot == 0 else 1 - pos[1]
            scale = gather_rays(pos, notes, slot, rays_scr)
            for r in range(row_blocks):
                row = scale[r : r + 1]
                rays[at, r] = rays_scr[r // quarter, r % quarter] * row
                rays[at, row_blocks, r : r + 1] = row
                for j in range(each):
                    k = r * each + j
                    info[1 + at, k] = tab[1, k]
                    block = src[0, 0, tab[0, k]]
                    wide[at, r, :, j * BS : (j + 1) * BS] = block
                    tall[at, r, j * BS : (j + 1) * BS] = block.T


def packed_weights(rays, slot, terms, w_scr):
    row_blocks = w_scr.shape[0]
    for r in range(row_blocks):
        total = sum(part.astype(jnp.float32) for part in slabs(terms, r))
        scale = rays[slot, row_blocks, r : r + 1]
        w_scr[r] = (rays[slot, r] - total * scale).astype(jnp.bfloat16)


def packed_back(info, wide, slot, w_scr, image):
    row_blocks = wide.shape[1]
    each = wide.shape[3] // BS
    for r in range(row_blocks):
        back = dot(w_scr[r], wide[slot, r], NN)
        for j in range(each):
            col = info[1 + slot, r * each + j]
            image[col] = image[col] + back[:, j * BS : (j + 1) * BS]


def packed_project(info, tall, slot, image, terms):
    row_blocks = tall.shape[1]
    each = tall.shape[2] // BS
    for r in range(row_blocks):
        parts = [image[info[1 + slot, r * each + j]] for j in range(each)]
        total = dot(jnp.concatenate(parts, axis=1), tall[slot, r], NN)
        total = total.astype(jnp.bfloat16)
        for t in range(terms.shape[0]):
            terms[t, r] = total


def later_first(place, n_terms, *refs):
    refs = list(refs)
    info, rays, wide, tall = take(refs, 4)
    terms_in = take(refs, n_terms)
    image_in, image, shot, terms, w_scr = refs

    @pl.when(info[0, 0] == place)
    def _():
        packed_weights(rays, 0, terms_in, w_scr)
        image[...] = image_in[...].astype(jnp.float32)
        packed_back(info, wide, 0, w_scr, image)
        shot[...] = image[...].astype(jnp.bfloat16)
        packed_project(info, tall, 1, shot, terms)


def later_second(place, n_terms, last, *refs):
    refs = list(refs)
    info, rays, wide = take(refs, 3)
    terms_in = take(refs, n_terms)
    image_in, shot, kept_in, given_in = take(refs, 4)
    image = None if last else take(refs, 1)[0]
    kept, given, w_scr, x_scr = refs
    active = info[0, 0] == place

    @pl.when(active)
    def _():
        packed_weights(rays, 1, terms_in, w_scr)
        x_scr[...] = image_in[...]
        packed_back(info, wide, 1, w_scr, x_scr)
        if not last:
            image[...] = x_scr[...].astype(jnp.bfloat16)

        @pl.when(info[0, 1] == 0)
        def _():
            kept[...] = shot[...]
            given[...] = x_scr[...].astype(jnp.bfloat16)

        @pl.when(info[0, 1] == 1)
        def _():
            kept[...] = x_scr[...].astype(jnp.bfloat16)
            given[...] = shot[...]

    @pl.when(jnp.logical_not(active))
    def _():
        kept[...] = kept_in[...]
        given[...] = given_in[...]


def later_project(place, info, image, tall, terms):
    @pl.when(info[0, 0] == place)
    def _():
        packed_project(info, tall, 0, image, terms)


def last_kernel(pos, kept, given, images):
    batches, per_batch, _ = images.shape
    half = kept.shape[1]
    group = half // per_batch

    def write(refs):
        for c in range(CB):
            for h in range(2):
                value = refs[h][c].astype(jnp.float32).reshape(group, per_batch, BS)
                where = slice(h * group, (h + 1) * group)
                images[where, :, c * BS : (c + 1) * BS] = value.astype(jnp.bfloat16)

    @pl.when(pos[1] == 0)
    def _():
        write((kept, given))

    @pl.when(pos[1] == 1)
    def _():
        write((given, kept))


def per_device(blocks, block_rows, block_cols, sinogram):
    batches, per_batch, here = sinogram.shape
    half = batches * per_batch // 2
    quarter = here // BS
    count = blocks.shape[2]
    subsets = lax.axis_size("subset")
    tiles = lax.axis_size("tile")
    row_blocks = quarter * tiles
    places = subsets // 2
    subset = lax.axis_index("subset")
    pos = jnp.stack([subset // 2, subset % 2, lax.axis_index("tile")]).astype(jnp.int32)

    image_shape = (CB, half, BS)
    image_out = jax.ShapeDtypeStruct(image_shape, jnp.bfloat16)
    terms_out = jax.ShapeDtypeStruct((tiles, row_blocks, half, BS), jnp.bfloat16)
    note_out = jax.ShapeDtypeStruct((quarter + 1, half, BS), jnp.float32)
    w_scr = pltpu.VMEM((row_blocks, half, BS), jnp.bfloat16)
    rays_scr = pltpu.VMEM((tiles, quarter, half, BS), jnp.float32)
    x_scr = pltpu.VMEM(image_shape, jnp.float32)

    def swapped(value):
        return lax.ppermute(value, "subset", [(s, s ^ 1) for s in range(subsets)])

    def spread(copies):
        return [lax.all_to_all(copies, "tile", 0, 0)]

    def call(kernel, smem, operands, out_shape, scratch, name):
        many = isinstance(out_shape, tuple)
        return pl.pallas_call(
            kernel,
            out_shape=out_shape,
            in_specs=[SMEM] * smem + [VMEM] * (len(operands) - smem),
            out_specs=(VMEM,) * len(out_shape) if many else VMEM,
            scratch_shapes=scratch,
            compiler_params=PARAMS,
            name=name,
        )(*operands)

    blocks2 = swapped(blocks)
    chunks = 8 if count % 8 == 0 else 1
    note, note2, table, blocks = pl.pallas_call(
        functools.partial(head_kernel, row_blocks, chunks),
        out_shape=(
            note_out,
            note_out,
            jax.ShapeDtypeStruct((2, count), jnp.int32),
            pltpu.VMEM(blocks.shape, blocks.dtype),
        ),
        in_specs=[SMEM] + [pl.BlockSpec(memory_space=pltpu.HBM)] * 4,
        out_specs=(VMEM, VMEM, SMEM, VMEM),
        scratch_shapes=[
            pltpu.SMEM(block_rows.shape, jnp.int32),
            pltpu.SMEM(block_cols.shape, jnp.int32),
            pltpu.VMEM(sinogram.shape, jnp.float32),
            pltpu.SMEM((row_blocks,), jnp.int32),
            pltpu.VMEM((row_blocks, BS, BS), jnp.float32),
            pltpu.SemaphoreType.DMA((3 + chunks,)),
        ],
        compiler_params=PARAMS,
        name="head",
    )(
        pos,
        *(
            pltpu.with_memory_space_constraint(value, pltpu.HBM)
            for value in (block_rows, block_cols, blocks, sinogram)
        ),
    )
    both = jnp.stack([note, swapped(note2)])
    notes = spread(jnp.broadcast_to(both, (tiles,) + both.shape))
    table2 = swapped(table)
    blocks2 = pltpu.with_memory_space_constraint(blocks2, pltpu.VMEM)
    fixed = [pos, table, table2, blocks, blocks2]
    image32_out = jax.ShapeDtypeStruct(image_shape, jnp.float32)

    image32, shot, terms = call(
        functools.partial(first_kernel, 0, len(notes)),
        3,
        fixed + notes,
        (image32_out, image_out, terms_out),
        [w_scr, rays_scr],
        "first",
    )
    each = count // row_blocks
    info, wide, tall, rays = pl.pallas_call(
        functools.partial(pack_kernel, len(notes)),
        out_shape=(
            jax.ShapeDtypeStruct((3, count), jnp.int32),
            pltpu.VMEM((2, row_blocks, BS, each * BS), jnp.bfloat16),
            pltpu.VMEM((2, row_blocks, each * BS, BS), jnp.bfloat16),
            jax.ShapeDtypeStruct((2, row_blocks + 1, half, BS), jnp.float32),
        ),
        in_specs=[SMEM] * 3 + [VMEM] * (2 + len(notes)) + [pl.BlockSpec(memory_space=pl.ANY)],
        out_specs=(SMEM, VMEM, VMEM, VMEM),
        scratch_shapes=[rays_scr],
        compiler_params=PARAMS,
        name="pack",
    )(*fixed, *notes, terms)
    terms = spread(terms)
    fixed[0] = info
    image, kept, given = call(
        functools.partial(second_kernel, 0, len(notes), len(terms)),
        3,
        fixed + notes + terms + [image32, shot],
        (image_out, image_out, image_out),
        [w_scr, rays_scr, x_scr],
        "second",
    )

    for place in range(1, places):
        pairs = [
            (2 * p + c, 2 * ((2 * place - 1 - p) % places) + c)
            for p in range(places)
            for c in range(2)
        ]
        image = lax.ppermute(image, "subset", pairs)
        terms = call(
            functools.partial(later_project, place),
            1,
            [info, image, tall],
            terms_out,
            [],
            "project",
        )
        terms = spread(terms)
        image32, shot, terms = call(
            functools.partial(later_first, place, len(terms)),
            1,
            [info, rays, wide, tall] + terms + [image],
            (image32_out, image_out, terms_out),
            [w_scr],
            "first",
        )
        terms = spread(terms)
        last = place == places - 1
        outs = call(
            functools.partial(later_second, place, len(terms), last),
            1,
            [info, rays, wide] + terms + [image32, shot, kept, given],
            (image_out,) * (2 if last else 3),
            [w_scr, x_scr],
            "second",
        )
        kept, given = outs[-2:]
        image = outs[0]
    images = call(
        last_kernel,
        1,
        [pos, kept, swapped(given)],
        jax.ShapeDtypeStruct((batches, per_batch, PIX), jnp.bfloat16),
        [],
        "last",
    )
    return images[None]


def solution(mesh):
    in_specs = (
        P("subset", "tile", None, None, None),
        P("subset", "tile", None),
        P("subset", "tile", None),
        P(None, None, ("subset", "tile")),
    )
    out_specs = P("subset", None, None, "tile")
    return jax.shard_map(
        per_device, mesh=mesh, in_specs=in_specs, out_specs=out_specs, check_vma=False
    )
```

```python
import functools

import jax
import jax.numpy as jnp
from jax import lax
from jax.experimental import pallas as pl
from jax.experimental.pallas import tpu as pltpu
from jax.sharding import PartitionSpec as P

BS = 128
PIX = 4096
CB = PIX // BS
relaxation = 0.5

DIRECT = 4

NN = (((1,), (0,)), ((), ()))
NT = (((1,), (1,)), ((), ()))
VMEM = pl.BlockSpec(memory_space=pltpu.VMEM)
SMEM = pl.BlockSpec(memory_space=pltpu.SMEM)
PARAMS = pltpu.CompilerParams(vmem_limit_bytes=20 * 2**20)


def dot(lhs, rhs, dims):
    return lax.dot_general(lhs, rhs, dims, preferred_element_type=jnp.float32)


def head_kernel(row_blocks, chunks, pos, rows_in, cols_in, blocks_in, rays_in, *refs):
    note, note2, table, blocks, rows, cols, rays, seen, squares, sems = refs
    count = blocks.shape[2]
    each = count // row_blocks
    per_chunk = count // chunks
    batches, per_batch, here = rays.shape
    quarter = here // BS
    half = note.shape[1]
    group = half // per_batch
    small = [
        pltpu.make_async_copy(src, dst, sems.at[i])
        for i, (src, dst) in enumerate(((rows_in, rows), (cols_in, cols), (rays_in, rays)))
    ]
    large = []
    for k in range(chunks):
        where = pl.ds(k * per_chunk, per_chunk)
        large.append(
            pltpu.make_async_copy(
                blocks_in.at[0, 0, where], blocks.at[0, 0, where], sems.at[3 + k]
            )
        )
    for copy in small + large:
        copy.start()
    squares[...] = jnp.zeros_like(squares)
    for copy in small:
        copy.wait()
    for r in range(row_blocks):
        seen[r] = r * each
    for n in range(count):
        row = rows[0, 0, n]
        at = seen[row]
        seen[row] = at + 1
        table[0, at] = n
        table[1, at] = cols[0, 0, n]
    for out, core in ((note, pos[1]), (note2, 1 - pos[1])):
        for i in range(quarter):
            parts = [
                rays[core * group + g, :, i * BS : (i + 1) * BS] for g in range(group)
            ]
            out[i] = jnp.concatenate(parts, axis=0)
    for k in range(chunks):
        large[k].wait()
        for n in range(k * per_chunk, (k + 1) * per_chunk):
            block = blocks[0, 0, n].astype(jnp.float32)
            row = rows[0, 0, n]
            squares[row] = squares[row] + block * block
    ones = jnp.ones((BS, BS), jnp.bfloat16)
    on_diagonal = lax.broadcasted_iota(jnp.int32, (BS, BS), 0) == lax.broadcasted_iota(
        jnp.int32, (BS, BS), 1
    )
    for r in range(row_blocks):
        left = squares[r]
        coarse = left.astype(jnp.bfloat16)
        fine = (left - coarse.astype(jnp.float32)).astype(jnp.bfloat16)
        total = dot(coarse, ones, NN) + dot(fine, ones, NN)
        total = jnp.sum(jnp.where(on_diagonal, total, 0.0), axis=0, keepdims=True)
        note[quarter, r : r + 1] = total
        note2[quarter, r : r + 1] = total


def slabs(refs, *where):
    if len(refs) > 1:
        return [ref[where] for ref in refs]
    return [refs[0][(t,) + where] for t in range(refs[0].shape[0])]


def gather_rays(pos, notes, slot, rays_scr):
    row_blocks = rays_scr.shape[0] * rays_scr.shape[1]
    quarter = rays_scr.shape[1]
    norms = sum(slabs(notes, slot, quarter))[0:row_blocks]
    if len(notes) > 1:
        for i, ref in enumerate(notes):
            rays_scr[pos[2] ^ ((len(notes) - i) % len(notes))] = ref[slot, 0:quarter]
    else:
        rays_scr[...] = notes[0][:, slot, 0:quarter]
    return relaxation / norms


def weights(pos, notes, slot, terms, w_scr, rays_scr):
    row_blocks = w_scr.shape[0]
    quarter = rays_scr.shape[1]
    scale = gather_rays(pos, notes, slot, rays_scr)
    for r in range(row_blocks):
        left = rays_scr[r // quarter, r % quarter]
        if terms is not None:
            left = left - sum(part.astype(jnp.float32) for part in slabs(terms, r))
        w_scr[r] = (left * scale[r : r + 1]).astype(jnp.bfloat16)


def back_project(table, blocks, w_scr, image):
    row_blocks = w_scr.shape[0]
    count = blocks.shape[2]
    each = count // row_blocks
    for k in range(count):
        col = table[1, k]
        image[col] = image[col] + dot(w_scr[k // each], blocks[0, 0, table[0, k]], NN)


def project(table, blocks, image, terms):
    row_blocks = terms.shape[0]
    each = blocks.shape[2] // row_blocks
    for r in range(row_blocks):
        total = 0.0
        for k in range(r * each, (r + 1) * each):
            total = total + dot(image[table[1, k]], blocks[0, 0, table[0, k]], NT)
        terms[r] = total.astype(jnp.bfloat16)


def take(refs, n):
    taken = refs[:n]
    del refs[:n]
    return taken


def on_core(pos, place, run, own, other):
    active = pos[0] == place

    @pl.when(jnp.logical_and(active, pos[1] == 0))
    def _():
        run(own, other)

    @pl.when(jnp.logical_and(active, pos[1] == 1))
    def _():
        run(other, own)

    return active


def first_kernel(place, n_notes, *refs):
    refs = list(refs)
    pos, table, table2, blocks, blocks2 = take(refs, 5)
    notes = take(refs, n_notes)
    image, shot, terms, w_scr, rays_scr = refs

    def run(first, second):
        weights(pos, notes, first[1], None, w_scr, rays_scr)
        image[...] = jnp.zeros_like(image)
        back_project(first[0], first[2], w_scr, image)
        shot[...] = image[...].astype(jnp.bfloat16)
        project(second[0], second[2], shot, terms)

    on_core(pos, place, run, (table, 0, blocks), (table2, 1, blocks2))


def second_kernel(place, n_notes, n_terms, *refs):
    refs = list(refs)
    info, table, table2, blocks, blocks2 = take(refs, 5)
    pos = [info[0, i] for i in range(3)]
    notes = take(refs, n_notes)
    terms_in = take(refs, n_terms)
    image_in, shot = take(refs, 2)
    image, kept, given, w_scr, rays_scr, x_scr = refs

    def run(first, second):
        weights(pos, notes, second[1], terms_in, w_scr, rays_scr)
        x_scr[...] = image_in[...]
        back_project(second[0], second[2], w_scr, x_scr)
        image[...] = x_scr[...].astype(jnp.bfloat16)

        @pl.when(pos[1] == 0)
        def _():
            kept[...] = shot[...]
            given[...] = image[...]

        @pl.when(pos[1] == 1)
        def _():
            kept[...] = image[...]
            given[...] = shot[...]

    on_core(pos, place, run, (table, 0, blocks), (table2, 1, blocks2))


def pack_kernel(n_notes, *refs):
    refs = list(refs)
    pos, table, table2, blocks, blocks2 = take(refs, 5)
    notes = take(refs, n_notes)
    _, info, wide, tall, rays, rays_scr = refs
    row_blocks = wide.shape[1]
    each = wide.shape[3] // BS
    quarter = rays_scr.shape[1]
    for i in range(3):
        info[0, i] = pos[i]

    @pl.when(pos[0] > 0)
    def _():
        for slot, (tab, src) in enumerate(((table, blocks), (table2, blocks2))):
            at = pos[1] if slot == 0 else 1 - pos[1]
            scale = gather_rays(pos, notes, slot, rays_scr)
            for r in range(row_blocks):
                row = scale[r : r + 1]
                rays[at, r] = rays_scr[r // quarter, r % quarter] * row
                rays[at, row_blocks, r : r + 1] = row
                for j in range(each):
                    k = r * each + j
                    info[1 + at, k] = tab[1, k]
                    block = src[0, 0, tab[0, k]]
                    wide[at, r, :, j * BS : (j + 1) * BS] = block
                    tall[at, r, j * BS : (j + 1) * BS] = block.T


def packed_weights(rays, slot, terms, w_scr):
    row_blocks = w_scr.shape[0]
    for r in range(row_blocks):
        total = sum(part.astype(jnp.float32) for part in slabs(terms, r))
        scale = rays[slot, row_blocks, r : r + 1]
        w_scr[r] = (rays[slot, r] - total * scale).astype(jnp.bfloat16)


def packed_back(info, wide, slot, w_scr, image):
    row_blocks = wide.shape[1]
    each = wide.shape[3] // BS
    for r in range(row_blocks):
        back = dot(w_scr[r], wide[slot, r], NN)
        for j in range(each):
            col = info[1 + slot, r * each + j]
            image[col] = image[col] + back[:, j * BS : (j + 1) * BS]


def packed_project(info, tall, slot, image, terms):
    row_blocks = tall.shape[1]
    each = tall.shape[2] // BS
    for r in range(row_blocks):
        parts = [image[info[1 + slot, r * each + j]] for j in range(each)]
        total = dot(jnp.concatenate(parts, axis=1), tall[slot, r], NN)
        terms[r] = total.astype(jnp.bfloat16)


def later_first(place, n_terms, *refs):
    refs = list(refs)
    info, rays, wide, tall = take(refs, 4)
    terms_in = take(refs, n_terms)
    image_in, image, shot, terms, w_scr = refs

    @pl.when(info[0, 0] == place)
    def _():
        packed_weights(rays, 0, terms_in, w_scr)
        image[...] = image_in[...].astype(jnp.float32)
        packed_back(info, wide, 0, w_scr, image)
        shot[...] = image[...].astype(jnp.bfloat16)
        packed_project(info, tall, 1, shot, terms)


def later_second(place, n_terms, last, *refs):
    refs = list(refs)
    info, rays, wide = take(refs, 3)
    terms_in = take(refs, n_terms)
    image_in, shot, kept_in, given_in = take(refs, 4)
    image = None if last else take(refs, 1)[0]
    kept, given, w_scr, x_scr = refs
    active = info[0, 0] == place

    def write(out, source):
        if not last:
            out[...] = source[...].astype(jnp.bfloat16)
            return
        group, per_batch, _ = out.shape
        for c in range(CB):
            value = source[c].astype(jnp.float32).reshape(group, per_batch, BS)
            out[:, :, c * BS : (c + 1) * BS] = value.astype(jnp.bfloat16)

    @pl.when(active)
    def _():
        packed_weights(rays, 1, terms_in, w_scr)
        x_scr[...] = image_in[...]
        packed_back(info, wide, 1, w_scr, x_scr)
        if not last:
            image[...] = x_scr[...].astype(jnp.bfloat16)

        @pl.when(info[0, 1] == 0)
        def _():
            write(kept, shot)
            write(given, x_scr)

        @pl.when(info[0, 1] == 1)
        def _():
            write(kept, x_scr)
            write(given, shot)

    @pl.when(jnp.logical_not(active))
    def _():
        write(kept, kept_in)
        write(given, given_in)


def later_project(place, info, image, tall, terms):
    @pl.when(info[0, 0] == place)
    def _():
        packed_project(info, tall, 0, image, terms)


def last_kernel(info, kept, given, images, sems):
    group = kept.shape[0]
    core = info[0, 1]
    copies = [
        pltpu.make_async_copy(
            source, images.at[pl.ds(half * group, group)], sems.at[i]
        )
        for i, (source, half) in enumerate(((kept, core), (given, 1 - core)))
    ]
    for copy in copies:
        copy.start()
    for copy in copies:
        copy.wait()


def per_device(blocks, block_rows, block_cols, sinogram):
    batches, per_batch, here = sinogram.shape
    half = batches * per_batch // 2
    quarter = here // BS
    count = blocks.shape[2]
    subsets = lax.axis_size("subset")
    tiles = lax.axis_size("tile")
    row_blocks = quarter * tiles
    places = subsets // 2
    direct = tiles <= DIRECT
    subset = lax.axis_index("subset")
    pos = jnp.stack([subset // 2, subset % 2, lax.axis_index("tile")]).astype(jnp.int32)

    image_shape = (CB, half, BS)
    image_out = jax.ShapeDtypeStruct(image_shape, jnp.bfloat16)
    terms_out = jax.ShapeDtypeStruct((row_blocks, half, BS), jnp.bfloat16)
    note_out = jax.ShapeDtypeStruct((quarter + 1, half, BS), jnp.float32)
    w_scr = pltpu.VMEM((row_blocks, half, BS), jnp.bfloat16)
    rays_scr = pltpu.VMEM((tiles, quarter, half, BS), jnp.float32)
    x_scr = pltpu.VMEM(image_shape, jnp.float32)

    def swapped(value):
        return lax.ppermute(value, "subset", [(s, s ^ 1) for s in range(subsets)])

    def turned(value, d, other=0):
        pairs = [
            (s * tiles + t, (s ^ other) * tiles + (t ^ d))
            for s in range(subsets)
            for t in range(tiles)
        ]
        return lax.ppermute(value, ("subset", "tile"), pairs)

    def spread(value):
        if direct:
            return [value] + [turned(value, d) for d in range(tiles - 1, 0, -1)]
        return [lax.all_gather(value, "tile")]

    def call(kernel, smem, operands, out_shape, scratch, name):
        many = isinstance(out_shape, tuple)
        return pl.pallas_call(
            kernel,
            out_shape=out_shape,
            in_specs=[SMEM] * smem + [VMEM] * (len(operands) - smem),
            out_specs=(VMEM,) * len(out_shape) if many else VMEM,
            scratch_shapes=scratch,
            compiler_params=PARAMS,
            name=name,
        )(*operands)

    blocks2 = swapped(blocks)
    chunks = 8 if count % 8 == 0 else 1
    note, note2, table, blocks = pl.pallas_call(
        functools.partial(head_kernel, row_blocks, chunks),
        out_shape=(
            note_out,
            note_out,
            jax.ShapeDtypeStruct((2, count), jnp.int32),
            pltpu.VMEM(blocks.shape, blocks.dtype),
        ),
        in_specs=[SMEM] + [pl.BlockSpec(memory_space=pltpu.HBM)] * 4,
        out_specs=(VMEM, VMEM, SMEM, VMEM),
        scratch_shapes=[
            pltpu.SMEM(block_rows.shape, jnp.int32),
            pltpu.SMEM(block_cols.shape, jnp.int32),
            pltpu.VMEM(sinogram.shape, jnp.float32),
            pltpu.SMEM((row_blocks,), jnp.int32),
            pltpu.VMEM((row_blocks, BS, BS), jnp.float32),
            pltpu.SemaphoreType.DMA((3 + chunks,)),
        ],
        compiler_params=PARAMS,
        name="head",
    )(
        pos,
        *(
            pltpu.with_memory_space_constraint(value, pltpu.HBM)
            for value in (block_rows, block_cols, blocks, sinogram)
        ),
    )
    notes = spread(jnp.stack([note, swapped(note2)]))
    table2 = swapped(table)
    blocks2 = pltpu.with_memory_space_constraint(blocks2, pltpu.VMEM)
    fixed = [pos, table, table2, blocks, blocks2]
    half_out = jax.ShapeDtypeStruct((batches // 2, per_batch, PIX), jnp.bfloat16)
    image32_out = jax.ShapeDtypeStruct(image_shape, jnp.float32)

    image32, shot, terms = call(
        functools.partial(first_kernel, 0, len(notes)),
        3,
        fixed + notes,
        (image32_out, image_out, terms_out),
        [w_scr, rays_scr],
        "first",
    )
    each = count // row_blocks
    info, wide, tall, rays = pl.pallas_call(
        functools.partial(pack_kernel, len(notes)),
        out_shape=(
            jax.ShapeDtypeStruct((3, count), jnp.int32),
            pltpu.VMEM((2, row_blocks, BS, each * BS), jnp.bfloat16),
            pltpu.VMEM((2, row_blocks, each * BS, BS), jnp.bfloat16),
            jax.ShapeDtypeStruct((2, row_blocks + 1, half, BS), jnp.float32),
        ),
        in_specs=[SMEM] * 3 + [VMEM] * (2 + len(notes)) + [pl.BlockSpec(memory_space=pl.ANY)],
        out_specs=(SMEM, VMEM, VMEM, VMEM),
        scratch_shapes=[rays_scr],
        compiler_params=PARAMS,
        name="pack",
    )(*fixed, *notes, terms)
    terms = spread(terms)
    fixed[0] = info
    image, kept, given = call(
        functools.partial(second_kernel, 0, len(notes), len(terms)),
        3,
        fixed + notes + terms + [image32, shot],
        (image_out, image_out, image_out),
        [w_scr, rays_scr, x_scr],
        "second",
    )

    for place in range(1, places):
        pairs = [
            (2 * p + c, 2 * ((2 * place - 1 - p) % places) + c)
            for p in range(places)
            for c in range(2)
        ]
        image = lax.ppermute(image, "subset", pairs)
        terms = call(
            functools.partial(later_project, place),
            1,
            [info, image, tall],
            terms_out,
            [],
            "project",
        )
        terms = spread(terms)
        image32, shot, terms = call(
            functools.partial(later_first, place, len(terms)),
            1,
            [info, rays, wide, tall] + terms + [image],
            (image32_out, image_out, terms_out),
            [w_scr],
            "first",
        )
        terms = spread(terms)
        last = place == places - 1
        outs = call(
            functools.partial(later_second, place, len(terms), last),
            1,
            [info, rays, wide] + terms + [image32, shot, kept, given],
            (half_out,) * 2 if last else (image_out,) * 3,
            [w_scr, x_scr],
            "second",
        )
        kept, given = outs[-2:]
        image = outs[0]
    images = pl.pallas_call(
        last_kernel,
        out_shape=jax.ShapeDtypeStruct((batches, per_batch, PIX), jnp.bfloat16),
        in_specs=[SMEM, VMEM, VMEM],
        out_specs=pl.BlockSpec(memory_space=pl.ANY),
        scratch_shapes=[pltpu.SemaphoreType.DMA((2,))],
        compiler_params=PARAMS,
        name="last",
    )(info, kept, swapped(given))
    return images[None]


def solution(mesh):
    in_specs = (
        P("subset", "tile", None, None, None),
        P("subset", "tile", None),
        P("subset", "tile", None),
        P(None, None, ("subset", "tile")),
    )
    out_specs = P("subset", None, None, "tile")
    return jax.shard_map(
        per_device, mesh=mesh, in_specs=in_specs, out_specs=out_specs, check_vma=False
    )
```

```python
import functools

import jax
import jax.numpy as jnp
from jax import lax
from jax.experimental import pallas as pl
from jax.experimental.pallas import tpu as pltpu
from jax.sharding import PartitionSpec as P

BS = 128
PIX = 4096
CB = PIX // BS
relaxation = 0.5

DIRECT = 4

NN = (((1,), (0,)), ((), ()))
NT = (((1,), (1,)), ((), ()))
VMEM = pl.BlockSpec(memory_space=pltpu.VMEM)
SMEM = pl.BlockSpec(memory_space=pltpu.SMEM)
PARAMS = pltpu.CompilerParams(vmem_limit_bytes=20 * 2**20)


def dot(lhs, rhs, dims):
    return lax.dot_general(lhs, rhs, dims, preferred_element_type=jnp.float32)


def head_kernel(row_blocks, chunks, pos, rows_in, cols_in, blocks_in, rays_in, *refs):
    note, note2, table, own, blocks, rows, cols, rays, seen, squares, sems = refs
    count = blocks.shape[2]
    each = count // row_blocks
    per_chunk = count // chunks
    batches, per_batch, here = rays.shape
    quarter = here // BS
    half = note.shape[1]
    group = half // per_batch
    small = [
        pltpu.make_async_copy(src, dst, sems.at[i])
        for i, (src, dst) in enumerate(((rows_in, rows), (cols_in, cols), (rays_in, rays)))
    ]
    large = []
    for k in range(chunks):
        where = pl.ds(k * per_chunk, per_chunk)
        large.append(
            pltpu.make_async_copy(
                blocks_in.at[0, 0, where], blocks.at[0, 0, where], sems.at[3 + k]
            )
        )
    for copy in small + large:
        copy.start()
    squares[...] = jnp.zeros_like(squares)
    for copy in small:
        copy.wait()
    for i in range(3):
        own[0, i] = pos[i]
    for r in range(row_blocks):
        seen[r] = r * each
    for n in range(count):
        row = rows[0, 0, n]
        at = seen[row]
        seen[row] = at + 1
        col = cols[0, 0, n]
        for out, first in ((table, 0), (own, 1)):
            out[first, at] = n
            out[first + 1, at] = col
    for out, core in ((note, pos[1]), (note2, 1 - pos[1])):
        for i in range(quarter):
            parts = [
                rays[core * group + g, :, i * BS : (i + 1) * BS] for g in range(group)
            ]
            out[i] = jnp.concatenate(parts, axis=0)
    for k in range(chunks):
        large[k].wait()
        for n in range(k * per_chunk, (k + 1) * per_chunk):
            block = blocks[0, 0, n].astype(jnp.float32)
            row = rows[0, 0, n]
            squares[row] = squares[row] + block * block
    ones = jnp.ones((BS, BS), jnp.bfloat16)
    on_diagonal = lax.broadcasted_iota(jnp.int32, (BS, BS), 0) == lax.broadcasted_iota(
        jnp.int32, (BS, BS), 1
    )
    for r in range(row_blocks):
        left = squares[r]
        coarse = left.astype(jnp.bfloat16)
        fine = (left - coarse.astype(jnp.float32)).astype(jnp.bfloat16)
        total = dot(coarse, ones, NN) + dot(fine, ones, NN)
        total = jnp.sum(jnp.where(on_diagonal, total, 0.0), axis=0, keepdims=True)
        note[quarter, r : r + 1] = total
        note2[quarter, r : r + 1] = total


def slabs(refs, *where):
    if len(refs) > 1:
        return [ref[where] for ref in refs]
    return [refs[0][(t,) + where] for t in range(refs[0].shape[0])]


def pack(tab, first, blocks, at, wide, tall):
    row_blocks = wide.shape[1]
    each = wide.shape[3] // BS
    for r in range(row_blocks):
        for j in range(each):
            block = blocks[0, 0, tab[first, r * each + j]]
            wide[at, r, :, j * BS : (j + 1) * BS] = block
            tall[at, r, j * BS : (j + 1) * BS] = block.T


def pack_own_kernel(own, blocks, _, wide, tall):
    pack(own, 1, blocks, own[0, 1], wide, tall)


def pack_other_kernel(own, table2, blocks2, wide_in, tall_in, info, wide, tall):
    del wide_in, tall_in
    core = own[0, 1]
    for i in range(3):
        info[0, i] = own[0, i]
    for k in range(info.shape[1]):
        info[1 + core, k] = own[2, k]
        info[2 - core, k] = table2[1, k]
    pack(table2, 0, blocks2, 1 - core, wide, tall)


def gather_rays(info, notes, rays, rays_scr):
    tiles, quarter, _, _ = rays_scr.shape
    row_blocks = tiles * quarter
    for slot in range(2):
        at = slot ^ info[0, 1]
        norms = sum(slabs(notes, at, quarter))[0:row_blocks]
        scale = relaxation / norms
        if len(notes) > 1:
            for i, ref in enumerate(notes):
                tile = info[0, 2] ^ ((len(notes) - i) % len(notes))
                rays_scr[tile] = ref[at, 0:quarter]
        else:
            rays_scr[...] = notes[0][:, at, 0:quarter]
        for r in range(row_blocks):
            row = scale[r : r + 1]
            rays[slot, r] = rays_scr[r // quarter, r % quarter] * row
            rays[slot, row_blocks, r : r + 1] = row


def weights(rays, slot, terms, w_scr):
    row_blocks = w_scr.shape[0]
    for r in range(row_blocks):
        left = rays[slot, r]
        if terms:
            total = sum(part.astype(jnp.float32) for part in slabs(terms, r))
            left = left - total * rays[slot, row_blocks, r : r + 1]
        w_scr[r] = left.astype(jnp.bfloat16)


def back_project(info, wide, slot, w_scr, image):
    row_blocks = wide.shape[1]
    each = wide.shape[3] // BS
    for r in range(row_blocks):
        back = dot(w_scr[r], wide[slot, r], NN)
        for j in range(each):
            col = info[1 + slot, r * each + j]
            image[col] = image[col] + back[:, j * BS : (j + 1) * BS]


def project(info, tall, slot, image, terms):
    row_blocks = tall.shape[1]
    each = tall.shape[2] // BS
    for r in range(row_blocks):
        parts = [image[info[1 + slot, r * each + j]] for j in range(each)]
        total = dot(jnp.concatenate(parts, axis=1), tall[slot, r], NN)
        terms[r] = total.astype(jnp.bfloat16)


def take(refs, n):
    taken = refs[:n]
    del refs[:n]
    return taken


def first_kernel(place, n_notes, n_terms, *refs):
    refs = list(refs)
    info, wide, tall = take(refs, 3)
    if place == 0:
        notes, terms_in = take(refs, n_notes), []
        image, shot, terms, rays, w_scr, rays_scr = refs
        gather_rays(info, notes, rays, rays_scr)
    else:
        rays, image_in = take(refs, 2)
        terms_in = take(refs, n_terms)
        image, shot, terms, w_scr = refs

    @pl.when(info[0, 0] == place)
    def _():
        weights(rays, 0, terms_in, w_scr)
        if place == 0:
            image[...] = jnp.zeros_like(image)
        else:
            image[...] = image_in[...].astype(jnp.float32)
        back_project(info, wide, 0, w_scr, image)
        shot[...] = image[...].astype(jnp.bfloat16)
        project(info, tall, 1, shot, terms)


def second_kernel(place, last, n_terms, *refs):
    refs = list(refs)
    info, rays, wide = take(refs, 3)
    terms_in = take(refs, n_terms)
    image_in, shot = take(refs, 2)
    held = take(refs, 2) if place > 0 else []
    image = None if last else take(refs, 1)[0]
    kept, given, w_scr, x_scr = refs
    active = info[0, 0] == place

    def write(out, source):
        if not last:
            out[...] = source[...].astype(jnp.bfloat16)
            return
        group, per_batch, _ = out.shape
        for c in range(CB):
            value = source[c].astype(jnp.float32).reshape(group, per_batch, BS)
            out[:, :, c * BS : (c + 1) * BS] = value.astype(jnp.bfloat16)

    @pl.when(active)
    def _():
        weights(rays, 1, terms_in, w_scr)
        x_scr[...] = image_in[...]
        back_project(info, wide, 1, w_scr, x_scr)
        if not last:
            image[...] = x_scr[...].astype(jnp.bfloat16)

        @pl.when(info[0, 1] == 0)
        def _():
            write(kept, shot)
            write(given, x_scr)

        @pl.when(info[0, 1] == 1)
        def _():
            write(kept, x_scr)
            write(given, shot)

    if held:

        @pl.when(jnp.logical_not(active))
        def _():
            write(kept, held[0])
            write(given, held[1])


def project_kernel(place, info, image, tall, terms):
    @pl.when(info[0, 0] == place)
    def _():
        project(info, tall, 0, image, terms)


def per_device(blocks, block_rows, block_cols, sinogram):
    batches, per_batch, here = sinogram.shape
    half = batches * per_batch // 2
    quarter = here // BS
    count = blocks.shape[2]
    subsets = lax.axis_size("subset")
    tiles = lax.axis_size("tile")
    row_blocks = quarter * tiles
    places = subsets // 2
    direct = tiles <= DIRECT
    subset = lax.axis_index("subset")
    pos = jnp.stack([subset // 2, subset % 2, lax.axis_index("tile")]).astype(jnp.int32)

    image_shape = (CB, half, BS)
    image_out = jax.ShapeDtypeStruct(image_shape, jnp.bfloat16)
    terms_out = jax.ShapeDtypeStruct((row_blocks, half, BS), jnp.bfloat16)
    note_out = jax.ShapeDtypeStruct((quarter + 1, half, BS), jnp.float32)
    w_scr = pltpu.VMEM((row_blocks, half, BS), jnp.bfloat16)
    rays_scr = pltpu.VMEM((tiles, quarter, half, BS), jnp.float32)
    x_scr = pltpu.VMEM(image_shape, jnp.float32)

    def swapped(value):
        return lax.ppermute(value, "subset", [(s, s ^ 1) for s in range(subsets)])

    def turned(value, d, other=0):
        pairs = [
            (s * tiles + t, (s ^ other) * tiles + (t ^ d))
            for s in range(subsets)
            for t in range(tiles)
        ]
        return lax.ppermute(value, ("subset", "tile"), pairs)

    def spread(value):
        if direct:
            return [value] + [turned(value, d) for d in range(tiles - 1, 0, -1)]
        return [lax.all_gather(value, "tile")]

    def call(kernel, smem, operands, out_shape, scratch, name):
        many = isinstance(out_shape, tuple)
        return pl.pallas_call(
            kernel,
            out_shape=out_shape,
            in_specs=[SMEM] * smem + [VMEM] * (len(operands) - smem),
            out_specs=(VMEM,) * len(out_shape) if many else VMEM,
            scratch_shapes=scratch,
            compiler_params=PARAMS,
            name=name,
        )(*operands)

    blocks2 = swapped(blocks)
    chunks = 8 if count % 8 == 0 else 1
    note, note2, table, own, blocks = pl.pallas_call(
        functools.partial(head_kernel, row_blocks, chunks),
        out_shape=(
            note_out,
            note_out,
            jax.ShapeDtypeStruct((2, count), jnp.int32),
            pltpu.SMEM((3, count), jnp.int32),
            pltpu.VMEM(blocks.shape, blocks.dtype),
        ),
        in_specs=[SMEM] + [pl.BlockSpec(memory_space=pltpu.HBM)] * 4,
        out_specs=(VMEM, VMEM, SMEM, SMEM, VMEM),
        scratch_shapes=[
            pltpu.SMEM(block_rows.shape, jnp.int32),
            pltpu.SMEM(block_cols.shape, jnp.int32),
            pltpu.VMEM(sinogram.shape, jnp.float32),
            pltpu.SMEM((row_blocks,), jnp.int32),
            pltpu.VMEM((row_blocks, BS, BS), jnp.float32),
            pltpu.SemaphoreType.DMA((3 + chunks,)),
        ],
        compiler_params=PARAMS,
        name="head",
    )(
        pos,
        *(
            pltpu.with_memory_space_constraint(value, pltpu.HBM)
            for value in (block_rows, block_cols, blocks, sinogram)
        ),
    )
    table2 = swapped(table)
    both = jnp.stack([note, swapped(note2)])
    notes = spread(both)

    own = pltpu.with_memory_space_constraint(own, pltpu.SMEM)
    blocks2 = pltpu.with_memory_space_constraint(blocks2, pltpu.VMEM)
    each = count // row_blocks
    packed_out = (
        pltpu.VMEM((2, row_blocks, BS, each * BS), jnp.bfloat16),
        pltpu.VMEM((2, row_blocks, each * BS, BS), jnp.bfloat16),
    )
    wide, tall = pl.pallas_call(
        pack_own_kernel,
        out_shape=packed_out,
        in_specs=[SMEM, VMEM, pl.BlockSpec(memory_space=pl.ANY)],
        out_specs=(VMEM, VMEM),
        compiler_params=PARAMS,
        name="pack_own",
    )(own, blocks, both)
    info, wide, tall = pl.pallas_call(
        pack_other_kernel,
        out_shape=(pltpu.SMEM((3, count), jnp.int32),) + packed_out,
        in_specs=[SMEM, SMEM, VMEM, VMEM, VMEM],
        out_specs=(SMEM, VMEM, VMEM),
        input_output_aliases={3: 1, 4: 2},
        compiler_params=PARAMS,
        name="pack_other",
    )(own, table2, blocks2, wide, tall)
    info = pltpu.with_memory_space_constraint(info, pltpu.SMEM)

    half_out = jax.ShapeDtypeStruct((batches // 2, per_batch, PIX), jnp.bfloat16)
    image32_out = jax.ShapeDtypeStruct(image_shape, jnp.float32)
    rays_out = jax.ShapeDtypeStruct((2, row_blocks + 1, half, BS), jnp.float32)
    rays, image, held = None, None, []
    for place in range(places):
        outs = (image32_out, image_out, terms_out)
        if place == 0:
            image32, shot, terms, rays = call(
                functools.partial(first_kernel, place, len(notes), 0),
                1,
                [info, wide, tall] + notes,
                outs + (rays_out,),
                [w_scr, rays_scr],
                "first",
            )
        else:
            pairs = [
                (2 * p + c, 2 * ((2 * place - 1 - p) % places) + c)
                for p in range(places)
                for c in range(2)
            ]
            image = lax.ppermute(image, "subset", pairs)
            terms = call(
                functools.partial(project_kernel, place),
                1,
                [info, image, tall],
                terms_out,
                [],
                "project",
            )
            terms = spread(terms)
            image32, shot, terms = call(
                functools.partial(first_kernel, place, 0, len(terms)),
                1,
                [info, wide, tall, rays, image] + terms,
                outs,
                [w_scr],
                "first",
            )
        terms = spread(terms)
        last = place == places - 1
        outs = call(
            functools.partial(second_kernel, place, last, len(terms)),
            1,
            [info, rays, wide] + terms + [image32, shot] + held,
            (half_out,) * 2 if last else (image_out,) * 3,
            [w_scr, x_scr],
            "second",
        )
        image = outs[0]
        held = list(outs[-2:])

    kept, given = held
    given = swapped(given)
    first = subset % 2 == 0
    images = jnp.concatenate(
        [jnp.where(first, kept, given), jnp.where(first, given, kept)], axis=0
    )
    return images[None]


def solution(mesh):
    in_specs = (
        P("subset", "tile", None, None, None),
        P("subset", "tile", None),
        P("subset", "tile", None),
        P(None, None, ("subset", "tile")),
    )
    out_specs = P("subset", None, None, "tile")
    return jax.shard_map(
        per_device, mesh=mesh, in_specs=in_specs, out_specs=out_specs, check_vma=False
    )
```

```python
import functools

import jax
import jax.numpy as jnp
from jax import lax
from jax.experimental import pallas as pl
from jax.experimental.pallas import tpu as pltpu
from jax.sharding import PartitionSpec as P

BS = 128
PIX = 4096
CB = PIX // BS
relaxation = 0.5

DIRECT = 4

NN = (((1,), (0,)), ((), ()))
NT = (((1,), (1,)), ((), ()))
VMEM = pl.BlockSpec(memory_space=pltpu.VMEM)
SMEM = pl.BlockSpec(memory_space=pltpu.SMEM)
PARAMS = pltpu.CompilerParams(vmem_limit_bytes=20 * 2**20)


def dot(lhs, rhs, dims):
    return lax.dot_general(lhs, rhs, dims, preferred_element_type=jnp.float32)


def head_kernel(row_blocks, chunks, pos, rows_in, cols_in, blocks_in, rays_in, *refs):
    note, note2, table, own, blocks, rows, cols, rays, seen, squares, sems = refs
    count = blocks.shape[2]
    each = count // row_blocks
    per_chunk = count // chunks
    batches, per_batch, here = rays.shape
    quarter = here // BS
    half = note.shape[1]
    group = half // per_batch
    small = [
        pltpu.make_async_copy(src, dst, sems.at[i])
        for i, (src, dst) in enumerate(((rows_in, rows), (cols_in, cols), (rays_in, rays)))
    ]
    large = []
    for k in range(chunks):
        where = pl.ds(k * per_chunk, per_chunk)
        large.append(
            pltpu.make_async_copy(
                blocks_in.at[0, 0, where], blocks.at[0, 0, where], sems.at[3 + k]
            )
        )
    for copy in small + large:
        copy.start()
    squares[...] = jnp.zeros_like(squares)
    for copy in small:
        copy.wait()
    for i in range(3):
        own[0, i] = pos[i]
    for r in range(row_blocks):
        seen[r] = r * each
    for n in range(count):
        row = rows[0, 0, n]
        at = seen[row]
        seen[row] = at + 1
        col = cols[0, 0, n]
        for out, first in ((table, 0), (own, 1)):
            out[first, at] = n
            out[first + 1, at] = col
    for out, core in ((note, pos[1]), (note2, 1 - pos[1])):
        for i in range(quarter):
            parts = [
                rays[core * group + g, :, i * BS : (i + 1) * BS] for g in range(group)
            ]
            out[i] = jnp.concatenate(parts, axis=0)
    for k in range(chunks):
        large[k].wait()
        for n in range(k * per_chunk, (k + 1) * per_chunk):
            block = blocks[0, 0, n].astype(jnp.float32)
            row = rows[0, 0, n]
            squares[row] = squares[row] + block * block
    ones = jnp.ones((BS, BS), jnp.bfloat16)
    on_diagonal = lax.broadcasted_iota(jnp.int32, (BS, BS), 0) == lax.broadcasted_iota(
        jnp.int32, (BS, BS), 1
    )
    for r in range(row_blocks):
        left = squares[r]
        coarse = left.astype(jnp.bfloat16)
        fine = (left - coarse.astype(jnp.float32)).astype(jnp.bfloat16)
        total = dot(coarse, ones, NN) + dot(fine, ones, NN)
        total = jnp.sum(jnp.where(on_diagonal, total, 0.0), axis=0, keepdims=True)
        note[quarter, r : r + 1] = total
        note2[quarter, r : r + 1] = total


def slabs(refs, *where):
    if len(refs) > 1:
        return [ref[where] for ref in refs]
    return [refs[0][(t,) + where] for t in range(refs[0].shape[0])]


def pack(tab, first, blocks, at, wide, tall):
    row_blocks = wide.shape[1]
    each = wide.shape[3] // BS
    for r in range(row_blocks):
        for j in range(each):
            block = blocks[0, 0, tab[first, r * each + j]]
            wide[at, r, :, j * BS : (j + 1) * BS] = block
            tall[at, r, j * BS : (j + 1) * BS] = block.T


def pack_own_kernel(own, blocks, _, wide, tall):
    pack(own, 1, blocks, own[0, 1], wide, tall)


def pack_other_kernel(own, table2, blocks2, wide_in, tall_in, info, wide, tall):
    del wide_in, tall_in
    core = own[0, 1]
    for i in range(3):
        info[0, i] = own[0, i]
    for k in range(info.shape[1]):
        info[1 + core, k] = own[2, k]
        info[2 - core, k] = table2[1, k]
    pack(table2, 0, blocks2, 1 - core, wide, tall)


def gather_rays(info, notes, rays, rays_scr):
    tiles, quarter, _, _ = rays_scr.shape
    row_blocks = tiles * quarter
    for slot in range(2):
        at = slot ^ info[0, 1]
        norms = sum(slabs(notes, at, quarter))[0:row_blocks]
        scale = relaxation / norms
        if len(notes) > 1:
            for i, ref in enumerate(notes):
                tile = info[0, 2] ^ ((len(notes) - i) % len(notes))
                rays_scr[tile] = ref[at, 0:quarter]
        else:
            rays_scr[...] = notes[0][:, at, 0:quarter]
        for r in range(row_blocks):
            row = scale[r : r + 1]
            rays[slot, r] = rays_scr[r // quarter, r % quarter] * row
            rays[slot, row_blocks, r : r + 1] = row


def weights(rays, slot, terms, w_scr):
    row_blocks = w_scr.shape[0]
    for r in range(row_blocks):
        left = rays[slot, r]
        if terms:
            total = sum(part.astype(jnp.float32) for part in slabs(terms, r))
            left = left - total * rays[slot, row_blocks, r : r + 1]
        w_scr[r] = left.astype(jnp.bfloat16)


def back_project(info, wide, slot, w_scr, image):
    row_blocks = wide.shape[1]
    each = wide.shape[3] // BS
    for r in range(row_blocks):
        back = dot(w_scr[r], wide[slot, r], NN)
        for j in range(each):
            col = info[1 + slot, r * each + j]
            image[col] = image[col] + back[:, j * BS : (j + 1) * BS]


def project(info, tall, slot, image, terms):
    row_blocks = tall.shape[1]
    each = tall.shape[2] // BS
    for r in range(row_blocks):
        parts = [image[info[1 + slot, r * each + j]] for j in range(each)]
        total = dot(jnp.concatenate(parts, axis=1), tall[slot, r], NN)
        terms[r] = total.astype(jnp.bfloat16)


def take(refs, n):
    taken = refs[:n]
    del refs[:n]
    return taken


def first_kernel(place, n_notes, n_terms, *refs):
    refs = list(refs)
    info, wide, tall = take(refs, 3)
    if place == 0:
        notes, terms_in = take(refs, n_notes), []
        image, shot, terms, rays, w_scr, rays_scr = refs
        gather_rays(info, notes, rays, rays_scr)
    else:
        rays, image_in = take(refs, 2)
        terms_in = take(refs, n_terms)
        image, shot, terms, w_scr = refs

    @pl.when(info[0, 0] == place)
    def _():
        weights(rays, 0, terms_in, w_scr)
        if place == 0:
            image[...] = jnp.zeros_like(image)
        else:
            image[...] = image_in[...].astype(jnp.float32)
        back_project(info, wide, 0, w_scr, image)
        shot[...] = image[...].astype(jnp.bfloat16)
        project(info, tall, 1, shot, terms)


def second_kernel(place, last, n_terms, *refs):
    refs = list(refs)
    info, rays, wide = take(refs, 3)
    terms_in = take(refs, n_terms)
    image_in, shot = take(refs, 2)
    held = take(refs, 2) if place > 0 else []
    image = None if last else take(refs, 1)[0]
    kept, given, w_scr, x_scr = refs
    active = info[0, 0] == place

    def write(out, source):
        if not last:
            out[...] = source[...].astype(jnp.bfloat16)
            return
        group, per_batch, _ = out.shape
        for c in range(CB):
            value = source[c].astype(jnp.float32).reshape(group, per_batch, BS)
            out[:, :, c * BS : (c + 1) * BS] = value.astype(jnp.bfloat16)

    @pl.when(active)
    def _():
        weights(rays, 1, terms_in, w_scr)
        x_scr[...] = image_in[...]
        back_project(info, wide, 1, w_scr, x_scr)
        if not last:
            image[...] = x_scr[...].astype(jnp.bfloat16)

        @pl.when(info[0, 1] == 0)
        def _():
            write(kept, shot)
            write(given, x_scr)

        @pl.when(info[0, 1] == 1)
        def _():
            write(kept, x_scr)
            write(given, shot)

    if held:

        @pl.when(jnp.logical_not(active))
        def _():
            write(kept, held[0])
            write(given, held[1])


def project_kernel(place, info, image, tall, terms):
    @pl.when(info[0, 0] == place)
    def _():
        project(info, tall, 0, image, terms)


def per_device(blocks, block_rows, block_cols, sinogram):
    batches, per_batch, here = sinogram.shape
    half = batches * per_batch // 2
    quarter = here // BS
    count = blocks.shape[2]
    subsets = lax.axis_size("subset")
    tiles = lax.axis_size("tile")
    row_blocks = quarter * tiles
    places = subsets // 2
    direct = tiles <= DIRECT
    subset = lax.axis_index("subset")
    pos = jnp.stack([subset // 2, subset % 2, lax.axis_index("tile")]).astype(jnp.int32)

    image_shape = (CB, half, BS)
    image_out = jax.ShapeDtypeStruct(image_shape, jnp.bfloat16)
    terms_out = jax.ShapeDtypeStruct((row_blocks, half, BS), jnp.bfloat16)
    note_out = jax.ShapeDtypeStruct((quarter + 1, half, BS), jnp.float32)
    w_scr = pltpu.VMEM((row_blocks, half, BS), jnp.bfloat16)
    rays_scr = pltpu.VMEM((tiles, quarter, half, BS), jnp.float32)
    x_scr = pltpu.VMEM(image_shape, jnp.float32)

    def swapped(value):
        return lax.ppermute(value, "subset", [(s, s ^ 1) for s in range(subsets)])

    def turned(value, d, other=0):
        pairs = [
            (s * tiles + t, (s ^ other) * tiles + (t ^ d))
            for s in range(subsets)
            for t in range(tiles)
        ]
        return lax.ppermute(value, ("subset", "tile"), pairs)

    def spread(value):
        if direct:
            return [value] + [turned(value, d) for d in range(tiles - 1, 0, -1)]
        return [lax.all_gather(value, "tile")]

    def summed(terms):
        d = 1
        while 2 * d < tiles:
            terms = terms + turned(terms, d)
            d *= 2
        return [terms, turned(terms, d)]

    def call(kernel, smem, operands, out_shape, scratch, name):
        many = isinstance(out_shape, tuple)
        return pl.pallas_call(
            kernel,
            out_shape=out_shape,
            in_specs=[SMEM] * smem + [VMEM] * (len(operands) - smem),
            out_specs=(VMEM,) * len(out_shape) if many else VMEM,
            scratch_shapes=scratch,
            compiler_params=PARAMS,
            name=name,
        )(*operands)

    blocks2 = swapped(blocks)
    chunks = 8 if count % 8 == 0 else 1
    note, note2, table, own, blocks = pl.pallas_call(
        functools.partial(head_kernel, row_blocks, chunks),
        out_shape=(
            note_out,
            note_out,
            jax.ShapeDtypeStruct((2, count), jnp.int32),
            pltpu.SMEM((3, count), jnp.int32),
            pltpu.VMEM(blocks.shape, blocks.dtype),
        ),
        in_specs=[SMEM] + [pl.BlockSpec(memory_space=pltpu.HBM)] * 4,
        out_specs=(VMEM, VMEM, SMEM, SMEM, VMEM),
        scratch_shapes=[
            pltpu.SMEM(block_rows.shape, jnp.int32),
            pltpu.SMEM(block_cols.shape, jnp.int32),
            pltpu.VMEM(sinogram.shape, jnp.float32),
            pltpu.SMEM((row_blocks,), jnp.int32),
            pltpu.VMEM((row_blocks, BS, BS), jnp.float32),
            pltpu.SemaphoreType.DMA((3 + chunks,)),
        ],
        compiler_params=PARAMS,
        name="head",
    )(
        pos,
        *(
            pltpu.with_memory_space_constraint(value, pltpu.HBM)
            for value in (block_rows, block_cols, blocks, sinogram)
        ),
    )
    table2 = swapped(table)
    both = jnp.stack([note, swapped(note2)])
    notes = spread(both)

    own = pltpu.with_memory_space_constraint(own, pltpu.SMEM)
    blocks2 = pltpu.with_memory_space_constraint(blocks2, pltpu.VMEM)
    each = count // row_blocks
    packed_out = (
        pltpu.VMEM((2, row_blocks, BS, each * BS), jnp.bfloat16),
        pltpu.VMEM((2, row_blocks, each * BS, BS), jnp.bfloat16),
    )
    wide, tall = pl.pallas_call(
        pack_own_kernel,
        out_shape=packed_out,
        in_specs=[SMEM, VMEM, pl.BlockSpec(memory_space=pl.ANY)],
        out_specs=(VMEM, VMEM),
        compiler_params=PARAMS,
        name="pack_own",
    )(own, blocks, both)
    info, wide, tall = pl.pallas_call(
        pack_other_kernel,
        out_shape=(pltpu.SMEM((3, count), jnp.int32),) + packed_out,
        in_specs=[SMEM, SMEM, VMEM, VMEM, VMEM],
        out_specs=(SMEM, VMEM, VMEM),
        input_output_aliases={3: 1, 4: 2},
        compiler_params=PARAMS,
        name="pack_other",
    )(own, table2, blocks2, wide, tall)
    info = pltpu.with_memory_space_constraint(info, pltpu.SMEM)

    half_out = jax.ShapeDtypeStruct((batches // 2, per_batch, PIX), jnp.bfloat16)
    image32_out = jax.ShapeDtypeStruct(image_shape, jnp.float32)
    rays_out = jax.ShapeDtypeStruct((2, row_blocks + 1, half, BS), jnp.float32)
    rays, image, held = None, None, []
    for place in range(places):
        outs = (image32_out, image_out, terms_out)
        if place == 0:
            image32, shot, terms, rays = call(
                functools.partial(first_kernel, place, len(notes), 0),
                1,
                [info, wide, tall] + notes,
                outs + (rays_out,),
                [w_scr, rays_scr],
                "first",
            )
        else:
            pairs = [
                (2 * p + c, 2 * ((2 * place - 1 - p) % places) + c)
                for p in range(places)
                for c in range(2)
            ]
            image = lax.ppermute(image, "subset", pairs)
            terms = call(
                functools.partial(project_kernel, place),
                1,
                [info, image, tall],
                terms_out,
                [],
                "project",
            )
            terms = summed(terms)
            image32, shot, terms = call(
                functools.partial(first_kernel, place, 0, len(terms)),
                1,
                [info, wide, tall, rays, image] + terms,
                outs,
                [w_scr],
                "first",
            )
        terms = summed(terms)
        last = place == places - 1
        outs = call(
            functools.partial(second_kernel, place, last, len(terms)),
            1,
            [info, rays, wide] + terms + [image32, shot] + held,
            (half_out,) * 2 if last else (image_out,) * 3,
            [w_scr, x_scr],
            "second",
        )
        image = outs[0]
        held = list(outs[-2:])

    kept, given = held
    given = swapped(given)
    first = subset % 2 == 0
    images = jnp.concatenate(
        [jnp.where(first, kept, given), jnp.where(first, given, kept)], axis=0
    )
    return images[None]


def solution(mesh):
    in_specs = (
        P("subset", "tile", None, None, None),
        P("subset", "tile", None),
        P("subset", "tile", None),
        P(None, None, ("subset", "tile")),
    )
    out_specs = P("subset", None, None, "tile")
    return jax.shard_map(
        per_device, mesh=mesh, in_specs=in_specs, out_specs=out_specs, check_vma=False
    )
```

```python
import functools

import jax
import jax.numpy as jnp
from jax import lax
from jax.experimental import pallas as pl
from jax.experimental.pallas import tpu as pltpu
from jax.sharding import PartitionSpec as P

BS = 128
PIX = 4096
CB = PIX // BS
relaxation = 0.5

DIRECT = 4

NN = (((1,), (0,)), ((), ()))
NT = (((1,), (1,)), ((), ()))
VMEM = pl.BlockSpec(memory_space=pltpu.VMEM)
SMEM = pl.BlockSpec(memory_space=pltpu.SMEM)
PARAMS = pltpu.CompilerParams(vmem_limit_bytes=20 * 2**20)


def dot(lhs, rhs, dims):
    return lax.dot_general(lhs, rhs, dims, preferred_element_type=jnp.float32)


def head_kernel(row_blocks, chunks, pos, rows_in, cols_in, blocks_in, rays_in, *refs):
    note, table, own, blocks, rows, cols, rays, seen, squares, sems = refs
    count = blocks.shape[2]
    each = count // row_blocks
    per_chunk = count // chunks
    batches, per_batch, here = rays.shape
    quarter = here // BS
    small = [
        pltpu.make_async_copy(src, dst, sems.at[i])
        for i, (src, dst) in enumerate(((rows_in, rows), (cols_in, cols), (rays_in, rays)))
    ]
    large = []
    for k in range(chunks):
        where = pl.ds(k * per_chunk, per_chunk)
        large.append(
            pltpu.make_async_copy(
                blocks_in.at[0, 0, where], blocks.at[0, 0, where], sems.at[3 + k]
            )
        )
    for copy in small + large:
        copy.start()
    squares[...] = jnp.zeros_like(squares)
    for copy in small:
        copy.wait()
    for i in range(3):
        own[0, i] = pos[i]
    for r in range(row_blocks):
        seen[r] = r * each
    for n in range(count):
        row = rows[0, 0, n]
        at = seen[row]
        seen[row] = at + 1
        col = cols[0, 0, n]
        for out, first in ((table, 0), (own, 1)):
            out[first, at] = n
            out[first + 1, at] = col
    for i in range(quarter):
        parts = [rays[g, :, i * BS : (i + 1) * BS] for g in range(batches)]
        note[i] = jnp.concatenate(parts, axis=0)
    for k in range(chunks):
        large[k].wait()
        for n in range(k * per_chunk, (k + 1) * per_chunk):
            block = blocks[0, 0, n].astype(jnp.float32)
            row = rows[0, 0, n]
            squares[row] = squares[row] + block * block
    ones = jnp.ones((BS, BS), jnp.bfloat16)
    on_diagonal = lax.broadcasted_iota(jnp.int32, (BS, BS), 0) == lax.broadcasted_iota(
        jnp.int32, (BS, BS), 1
    )
    for r in range(row_blocks):
        left = squares[r]
        coarse = left.astype(jnp.bfloat16)
        fine = (left - coarse.astype(jnp.float32)).astype(jnp.bfloat16)
        total = dot(coarse, ones, NN) + dot(fine, ones, NN)
        total = jnp.sum(jnp.where(on_diagonal, total, 0.0), axis=0, keepdims=True)
        note[quarter, r : r + 1] = total


def pack_own_kernel(own, blocks, _, wide):
    row_blocks = wide.shape[0]
    each = wide.shape[2] // BS
    for r in range(row_blocks):
        for j in range(each):
            block = blocks[0, 0, own[1, r * each + j]]
            wide[r, :, j * BS : (j + 1) * BS] = block


def pack_other_kernel(own, table2, blocks2, info, tall):
    row_blocks = tall.shape[0]
    each = tall.shape[1] // BS
    for i in range(3):
        info[0, i] = own[0, i]
    for r in range(row_blocks):
        for j in range(each):
            k = r * each + j
            info[1, k] = own[2, k]
            info[2, k] = table2[1, k]
            block = blocks2[0, 0, table2[0, k]]
            tall[r, j * BS : (j + 1) * BS] = block.T


def gather_rays(info, notes, rays, rays_scr):
    tiles, quarter, _, _ = rays_scr.shape
    row_blocks = tiles * quarter
    if len(notes) > 1:
        norms = sum(ref[quarter] for ref in notes)[0:row_blocks]
        for i, ref in enumerate(notes):
            rays_scr[info[0, 2] ^ i] = ref[0:quarter]
    else:
        norms = sum(notes[0][t, quarter] for t in range(tiles))[0:row_blocks]
        rays_scr[...] = notes[0][:, 0:quarter]
    scale = relaxation / norms
    for r in range(row_blocks):
        row = scale[r : r + 1]
        rays[r] = rays_scr[r // quarter, r % quarter] * row
        rays[row_blocks, r : r + 1] = row


def weights(rays, terms, w_scr):
    row_blocks = w_scr.shape[0]
    for r in range(row_blocks):
        left = rays[r]
        if terms:
            total = sum(ref[r].astype(jnp.float32) for ref in terms)
            left = left - total * rays[row_blocks, r : r + 1]
        w_scr[r] = left.astype(jnp.bfloat16)


def back_project(info, wide, w_scr, image):
    row_blocks = wide.shape[0]
    each = wide.shape[2] // BS
    for r in range(row_blocks):
        back = dot(w_scr[r], wide[r], NN)
        for j in range(each):
            col = info[1, r * each + j]
            image[col] = image[col] + back[:, j * BS : (j + 1) * BS]


def project(info, tall, image, terms):
    row_blocks = tall.shape[0]
    each = tall.shape[1] // BS
    for r in range(row_blocks):
        parts = [image[info[2, r * each + j]] for j in range(each)]
        total = dot(jnp.concatenate(parts, axis=1), tall[r], NN)
        terms[r] = total.astype(jnp.bfloat16)


def take(refs, n):
    taken = refs[:n]
    del refs[:n]
    return taken


def on_core(info, place, core):
    return jnp.logical_and(info[0, 0] == place, info[0, 1] == core)


def project_kernel(place, info, image, tall, terms):
    @pl.when(on_core(info, place, 1))
    def _():
        project(info, tall, image, terms)


def first_kernel(place, n_notes, n_terms, *refs):
    refs = list(refs)
    info, wide, tall = take(refs, 3)
    if place == 0:
        notes, terms_in = take(refs, n_notes), []
        shot, terms, rays, w_scr, x_scr, rays_scr = refs
        gather_rays(info, notes, rays, rays_scr)
    else:
        rays, image_in = take(refs, 2)
        terms_in = take(refs, n_terms)
        shot, terms, w_scr, x_scr = refs

    @pl.when(on_core(info, place, 0))
    def _():
        weights(rays, terms_in, w_scr)
        if place == 0:
            x_scr[...] = jnp.zeros_like(x_scr)
        else:
            x_scr[...] = image_in[...].astype(jnp.float32)
        back_project(info, wide, w_scr, x_scr)
        shot[...] = x_scr[...].astype(jnp.bfloat16)
        project(info, tall, shot, terms)


def second_kernel(place, last, n_terms, *refs):
    refs = list(refs)
    info, rays, wide, image_in, shot = take(refs, 5)
    terms_in = take(refs, n_terms)
    held = take(refs, 1) if place > 0 else []
    image = None if last else take(refs, 1)[0]
    out, w_scr, x_scr = refs
    batches, per_batch, _ = out.shape

    def write(source):
        if not last:
            out[...] = source[...].astype(jnp.bfloat16)
            return
        for c in range(CB):
            value = source[c].astype(jnp.float32).reshape(batches, per_batch, BS)
            out[:, :, c * BS : (c + 1) * BS] = value.astype(jnp.bfloat16)

    @pl.when(on_core(info, place, 1))
    def _():
        weights(rays, terms_in, w_scr)
        x_scr[...] = image_in[...].astype(jnp.float32)
        back_project(info, wide, w_scr, x_scr)
        if not last:
            image[...] = x_scr[...].astype(jnp.bfloat16)
        write(x_scr)

    @pl.when(on_core(info, place, 0))
    def _():
        write(shot)

    if held:

        @pl.when(info[0, 0] != place)
        def _():
            write(held[0])


def per_device(blocks, block_rows, block_cols, sinogram):
    batches, per_batch, here = sinogram.shape
    slices = batches * per_batch
    quarter = here // BS
    count = blocks.shape[2]
    subsets = lax.axis_size("subset")
    tiles = lax.axis_size("tile")
    row_blocks = quarter * tiles
    each = count // row_blocks
    places = subsets // 2
    direct = tiles <= DIRECT
    subset = lax.axis_index("subset")
    pos = jnp.stack([subset // 2, subset % 2, lax.axis_index("tile")]).astype(jnp.int32)

    image_shape = (CB, slices, BS)
    image_out = jax.ShapeDtypeStruct(image_shape, jnp.bfloat16)
    terms_out = jax.ShapeDtypeStruct((row_blocks, slices, BS), jnp.bfloat16)
    rays_out = jax.ShapeDtypeStruct((row_blocks + 1, slices, BS), jnp.float32)
    final_out = jax.ShapeDtypeStruct((batches, per_batch, PIX), jnp.bfloat16)
    w_scr = pltpu.VMEM((row_blocks, slices, BS), jnp.bfloat16)
    x_scr = pltpu.VMEM(image_shape, jnp.float32)
    rays_scr = pltpu.VMEM((tiles, quarter, slices, BS), jnp.float32)

    def sent(value, target):
        pairs = []
        for p in range(places):
            for c in range(2):
                for t in range(tiles):
                    q, e, u = target(p, c, t)
                    pairs.append(((2 * p + c) * tiles + t, (2 * q + e) * tiles + u))
        return lax.ppermute(value, ("subset", "tile"), pairs)

    def swapped(value):
        return sent(value, lambda p, c, t: (p, 1 - c, t))

    def spread(value):
        if direct:
            far = range(1, tiles)
            return [value] + [sent(value, lambda p, c, t: (p, c, t ^ d)) for d in far]
        return [lax.all_gather(value, "tile")]

    def passed(terms, core):
        if not direct:
            return [swapped(lax.psum(terms, "tile"))]
        return [
            sent(terms, lambda p, c, t: (p, 1 - c, t ^ d if c == core else t))
            for d in range(tiles)
        ]

    def call(kernel, smem, operands, out_shape, scratch, name):
        many = isinstance(out_shape, tuple)
        return pl.pallas_call(
            kernel,
            out_shape=out_shape,
            in_specs=[SMEM] * smem + [VMEM] * (len(operands) - smem),
            out_specs=(VMEM,) * len(out_shape) if many else VMEM,
            scratch_shapes=scratch,
            compiler_params=PARAMS,
            name=name,
        )(*operands)

    blocks2 = swapped(blocks)
    chunks = 8 if count % 8 == 0 else 1
    note, table, own, blocks = pl.pallas_call(
        functools.partial(head_kernel, row_blocks, chunks),
        out_shape=(
            jax.ShapeDtypeStruct((quarter + 1, slices, BS), jnp.float32),
            jax.ShapeDtypeStruct((2, count), jnp.int32),
            pltpu.SMEM((3, count), jnp.int32),
            pltpu.VMEM(blocks.shape, blocks.dtype),
        ),
        in_specs=[SMEM] + [pl.BlockSpec(memory_space=pltpu.HBM)] * 4,
        out_specs=(VMEM, SMEM, SMEM, VMEM),
        scratch_shapes=[
            pltpu.SMEM(block_rows.shape, jnp.int32),
            pltpu.SMEM(block_cols.shape, jnp.int32),
            pltpu.VMEM(sinogram.shape, jnp.float32),
            pltpu.SMEM((row_blocks,), jnp.int32),
            pltpu.VMEM((row_blocks, BS, BS), jnp.float32),
            pltpu.SemaphoreType.DMA((3 + chunks,)),
        ],
        compiler_params=PARAMS,
        name="head",
    )(
        pos,
        *(
            pltpu.with_memory_space_constraint(value, pltpu.HBM)
            for value in (block_rows, block_cols, blocks, sinogram)
        ),
    )
    notes = spread(note)
    table2 = swapped(table)

    own = pltpu.with_memory_space_constraint(own, pltpu.SMEM)
    blocks2 = pltpu.with_memory_space_constraint(blocks2, pltpu.VMEM)
    wide = pl.pallas_call(
        pack_own_kernel,
        out_shape=pltpu.VMEM((row_blocks, BS, each * BS), jnp.bfloat16),
        in_specs=[SMEM, VMEM, pl.BlockSpec(memory_space=pl.ANY)],
        out_specs=VMEM,
        compiler_params=PARAMS,
        name="pack_own",
    )(own, blocks, note)
    info, tall = pl.pallas_call(
        pack_other_kernel,
        out_shape=(
            pltpu.SMEM((3, count), jnp.int32),
            pltpu.VMEM((row_blocks, each * BS, BS), jnp.bfloat16),
        ),
        in_specs=[SMEM, SMEM, VMEM],
        out_specs=(SMEM, VMEM),
        compiler_params=PARAMS,
        name="pack_other",
    )(own, table2, blocks2)
    info = pltpu.with_memory_space_constraint(info, pltpu.SMEM)

    held = []
    image, rays = None, None
    for place in range(places):
        if place == 0:
            shot, terms, rays = call(
                functools.partial(first_kernel, place, len(notes), 0),
                1,
                [info, wide, tall] + notes,
                (image_out, terms_out, rays_out),
                [w_scr, x_scr, rays_scr],
                "first",
            )
        else:
            def hop(p, c, t):
                return ((2 * place - 1 - p) % places, c, t) if c else (p, c, t ^ 1)

            image = sent(image, hop)
            terms = call(
                functools.partial(project_kernel, place),
                1,
                [info, image, tall],
                terms_out,
                [],
                "project",
            )
            image = swapped(image)
            terms = passed(terms, 1)
            shot, terms = call(
                functools.partial(first_kernel, place, 0, len(terms)),
                1,
                [info, wide, tall, rays, image] + terms,
                (image_out, terms_out),
                [w_scr, x_scr],
                "first",
            )
        image = swapped(shot)
        terms = passed(terms, 0)
        last = place == places - 1
        outs = call(
            functools.partial(second_kernel, place, last, len(terms)),
            1,
            [info, rays, wide, image, shot] + terms + held,
            final_out if last else (image_out, image_out),
            [w_scr, x_scr],
            "second",
        )
        if last:
            return outs[None]
        image = outs[0]
        held = [outs[1]]


def solution(mesh):
    in_specs = (
        P("subset", "tile", None, None, None),
        P("subset", "tile", None),
        P("subset", "tile", None),
        P(None, None, ("subset", "tile")),
    )
    out_specs = P("subset", None, None, "tile")
    return jax.shard_map(
        per_device, mesh=mesh, in_specs=in_specs, out_specs=out_specs, check_vma=False
    )
```

```python
import functools

import jax
import jax.numpy as jnp
from jax import lax
from jax.experimental import pallas as pl
from jax.experimental.pallas import tpu as pltpu
from jax.sharding import PartitionSpec as P

BS = 128
PIX = 4096
CB = PIX // BS
relaxation = 0.5

DIRECT = 4

NN = (((1,), (0,)), ((), ()))
NT = (((1,), (1,)), ((), ()))
VMEM = pl.BlockSpec(memory_space=pltpu.VMEM)
SMEM = pl.BlockSpec(memory_space=pltpu.SMEM)
PARAMS = pltpu.CompilerParams(vmem_limit_bytes=20 * 2**20)


def dot(lhs, rhs, dims):
    return lax.dot_general(lhs, rhs, dims, preferred_element_type=jnp.float32)


def head_kernel(row_blocks, chunks, pos, rows_in, cols_in, blocks_in, rays_in, *refs):
    note, table, own, blocks, rows, cols, rays, seen, squares, sems = refs
    count = blocks.shape[2]
    each = count // row_blocks
    per_chunk = count // chunks
    batches, per_batch, here = rays.shape
    quarter = here // BS
    small = [
        pltpu.make_async_copy(src, dst, sems.at[i])
        for i, (src, dst) in enumerate(((rows_in, rows), (cols_in, cols), (rays_in, rays)))
    ]
    large = []
    for k in range(chunks):
        where = pl.ds(k * per_chunk, per_chunk)
        large.append(
            pltpu.make_async_copy(
                blocks_in.at[0, 0, where], blocks.at[0, 0, where], sems.at[3 + k]
            )
        )
    for copy in small + large:
        copy.start()
    squares[...] = jnp.zeros_like(squares)
    for copy in small:
        copy.wait()
    for i in range(3):
        own[0, i] = pos[i]
    for r in range(row_blocks):
        seen[r] = r * each
    for n in range(count):
        row = rows[0, 0, n]
        at = seen[row]
        seen[row] = at + 1
        col = cols[0, 0, n]
        for out, first in ((table, 0), (own, 1)):
            out[first, at] = n
            out[first + 1, at] = col
    for i in range(quarter):
        parts = [rays[g, :, i * BS : (i + 1) * BS] for g in range(batches)]
        note[i] = jnp.concatenate(parts, axis=0)
    for k in range(chunks):
        large[k].wait()
        for n in range(k * per_chunk, (k + 1) * per_chunk):
            block = blocks[0, 0, n].astype(jnp.float32)
            row = rows[0, 0, n]
            squares[row] = squares[row] + block * block
    ones = jnp.ones((BS, BS), jnp.bfloat16)
    on_diagonal = lax.broadcasted_iota(jnp.int32, (BS, BS), 0) == lax.broadcasted_iota(
        jnp.int32, (BS, BS), 1
    )
    for r in range(row_blocks):
        left = squares[r]
        coarse = left.astype(jnp.bfloat16)
        fine = (left - coarse.astype(jnp.float32)).astype(jnp.bfloat16)
        total = dot(coarse, ones, NN) + dot(fine, ones, NN)
        total = jnp.sum(jnp.where(on_diagonal, total, 0.0), axis=0, keepdims=True)
        note[quarter, r : r + 1] = total


def pack_own_kernel(own, blocks, _, wide):
    row_blocks = wide.shape[0]
    each = wide.shape[2] // BS
    for r in range(row_blocks):
        for j in range(each):
            block = blocks[0, 0, own[1, r * each + j]]
            wide[r, :, j * BS : (j + 1) * BS] = block


def pack_other_kernel(own, table2, blocks2, info, tall):
    row_blocks = tall.shape[0]
    each = tall.shape[1] // BS
    for i in range(3):
        info[0, i] = own[0, i]
    for r in range(row_blocks):
        for j in range(each):
            k = r * each + j
            info[1, k] = own[2, k]
            info[2, k] = table2[1, k]
            block = blocks2[0, 0, table2[0, k]]
            tall[r, j * BS : (j + 1) * BS] = block.T


def gather_rays(info, notes, rays, rays_scr):
    tiles, quarter, _, _ = rays_scr.shape
    row_blocks = tiles * quarter
    if len(notes) > 1:
        norms = sum(ref[quarter] for ref in notes)[0:row_blocks]
        for i, ref in enumerate(notes):
            rays_scr[info[0, 2] ^ i] = ref[0:quarter]
    else:
        norms = sum(notes[0][t, quarter] for t in range(tiles))[0:row_blocks]
        rays_scr[...] = notes[0][:, 0:quarter]
    scale = relaxation / norms
    for r in range(row_blocks):
        row = scale[r : r + 1]
        rays[r] = rays_scr[r // quarter, r % quarter] * row
        rays[row_blocks, r : r + 1] = row


def weights(rays, terms, w_scr):
    row_blocks = w_scr.shape[0]
    for r in range(row_blocks):
        left = rays[r]
        if terms:
            total = sum(ref[r].astype(jnp.float32) for ref in terms)
            left = left - total * rays[row_blocks, r : r + 1]
        w_scr[r] = left.astype(jnp.bfloat16)


def back_project(info, wide, w_scr, image):
    row_blocks = wide.shape[0]
    each = wide.shape[2] // BS
    for r in range(row_blocks):
        back = dot(w_scr[r], wide[r], NN)
        for j in range(each):
            col = info[1, r * each + j]
            image[col] = image[col] + back[:, j * BS : (j + 1) * BS]


def project(info, tall, image, terms):
    row_blocks = tall.shape[0]
    each = tall.shape[1] // BS
    for r in range(row_blocks):
        parts = [image[info[2, r * each + j]] for j in range(each)]
        total = dot(jnp.concatenate(parts, axis=1), tall[r], NN)
        terms[r] = total.astype(jnp.bfloat16)


def take(refs, n):
    taken = refs[:n]
    del refs[:n]
    return taken


def on_core(info, place, core):
    return jnp.logical_and(info[0, 0] == place, info[0, 1] == core)


def project_kernel(place, core, info, image, tall, terms):
    @pl.when(on_core(info, place, core))
    def _():
        project(info, tall, image, terms)


def first_kernel(place, n_notes, n_terms, *refs):
    refs = list(refs)
    info, wide = take(refs, 2)
    if place == 0:
        notes, terms_in = take(refs, n_notes), []
        shot, rays, w_scr, x_scr, rays_scr = refs
        gather_rays(info, notes, rays, rays_scr)
    else:
        rays, image_in = take(refs, 2)
        terms_in = take(refs, n_terms)
        shot, w_scr, x_scr = refs

    @pl.when(on_core(info, place, 0))
    def _():
        weights(rays, terms_in, w_scr)
        if place == 0:
            x_scr[...] = jnp.zeros_like(x_scr)
        else:
            x_scr[...] = image_in[...].astype(jnp.float32)
        back_project(info, wide, w_scr, x_scr)
        shot[...] = x_scr[...].astype(jnp.bfloat16)


def second_kernel(place, last, n_terms, *refs):
    refs = list(refs)
    info, rays, wide, image_in, shot = take(refs, 5)
    terms_in = take(refs, n_terms)
    held = take(refs, 1) if place > 0 else []
    image = None if last else take(refs, 1)[0]
    out, w_scr, x_scr = refs
    batches, per_batch, _ = out.shape

    def write(source):
        if not last:
            out[...] = source[...].astype(jnp.bfloat16)
            return
        for c in range(CB):
            value = source[c].astype(jnp.float32).reshape(batches, per_batch, BS)
            out[:, :, c * BS : (c + 1) * BS] = value.astype(jnp.bfloat16)

    @pl.when(on_core(info, place, 1))
    def _():
        weights(rays, terms_in, w_scr)
        x_scr[...] = image_in[...].astype(jnp.float32)
        back_project(info, wide, w_scr, x_scr)
        if not last:
            image[...] = x_scr[...].astype(jnp.bfloat16)
        write(x_scr)

    @pl.when(on_core(info, place, 0))
    def _():
        write(shot)

    if held:

        @pl.when(info[0, 0] != place)
        def _():
            write(held[0])


def per_device(blocks, block_rows, block_cols, sinogram):
    batches, per_batch, here = sinogram.shape
    slices = batches * per_batch
    quarter = here // BS
    count = blocks.shape[2]
    subsets = lax.axis_size("subset")
    tiles = lax.axis_size("tile")
    row_blocks = quarter * tiles
    each = count // row_blocks
    places = subsets // 2
    direct = tiles <= DIRECT
    subset = lax.axis_index("subset")
    pos = jnp.stack([subset // 2, subset % 2, lax.axis_index("tile")]).astype(jnp.int32)

    image_shape = (CB, slices, BS)
    image_out = jax.ShapeDtypeStruct(image_shape, jnp.bfloat16)
    terms_out = jax.ShapeDtypeStruct((row_blocks, slices, BS), jnp.bfloat16)
    rays_out = jax.ShapeDtypeStruct((row_blocks + 1, slices, BS), jnp.float32)
    final_out = jax.ShapeDtypeStruct((batches, per_batch, PIX), jnp.bfloat16)
    w_scr = pltpu.VMEM((row_blocks, slices, BS), jnp.bfloat16)
    x_scr = pltpu.VMEM(image_shape, jnp.float32)
    rays_scr = pltpu.VMEM((tiles, quarter, slices, BS), jnp.float32)

    def sent(value, target):
        pairs = []
        for p in range(places):
            for c in range(2):
                for t in range(tiles):
                    q, e, u = target(p, c, t)
                    pairs.append(((2 * p + c) * tiles + t, (2 * q + e) * tiles + u))
        return lax.ppermute(value, ("subset", "tile"), pairs)

    def swapped(value):
        return sent(value, lambda p, c, t: (p, 1 - c, t))

    def spread(value):
        if direct:
            far = range(1, tiles)
            return [value] + [sent(value, lambda p, c, t: (p, c, t ^ d)) for d in far]
        return [lax.all_gather(value, "tile")]

    def passed(terms, core):
        if not direct:
            return [swapped(lax.psum(terms, "tile"))]

        def way(d):
            def target(p, c, t):
                if c == core:
                    return p, 1 - c, t ^ d
                return (p + 1) % places if d > 1 else p, 1 - c, t

            return target

        return [sent(terms, way(d)) for d in range(tiles)]

    def call(kernel, smem, operands, out_shape, scratch, name):
        many = isinstance(out_shape, tuple)
        return pl.pallas_call(
            kernel,
            out_shape=out_shape,
            in_specs=[SMEM] * smem + [VMEM] * (len(operands) - smem),
            out_specs=(VMEM,) * len(out_shape) if many else VMEM,
            scratch_shapes=scratch,
            compiler_params=PARAMS,
            name=name,
        )(*operands)

    blocks2 = swapped(blocks)
    chunks = 8 if count % 8 == 0 else 1
    note, table, own, blocks = pl.pallas_call(
        functools.partial(head_kernel, row_blocks, chunks),
        out_shape=(
            jax.ShapeDtypeStruct((quarter + 1, slices, BS), jnp.float32),
            jax.ShapeDtypeStruct((2, count), jnp.int32),
            pltpu.SMEM((3, count), jnp.int32),
            pltpu.VMEM(blocks.shape, blocks.dtype),
        ),
        in_specs=[SMEM] + [pl.BlockSpec(memory_space=pltpu.HBM)] * 4,
        out_specs=(VMEM, SMEM, SMEM, VMEM),
        scratch_shapes=[
            pltpu.SMEM(block_rows.shape, jnp.int32),
            pltpu.SMEM(block_cols.shape, jnp.int32),
            pltpu.VMEM(sinogram.shape, jnp.float32),
            pltpu.SMEM((row_blocks,), jnp.int32),
            pltpu.VMEM((row_blocks, BS, BS), jnp.float32),
            pltpu.SemaphoreType.DMA((3 + chunks,)),
        ],
        compiler_params=PARAMS,
        name="head",
    )(
        pos,
        *(
            pltpu.with_memory_space_constraint(value, pltpu.HBM)
            for value in (block_rows, block_cols, blocks, sinogram)
        ),
    )
    notes = spread(note)
    table2 = swapped(table)

    own = pltpu.with_memory_space_constraint(own, pltpu.SMEM)
    blocks2 = pltpu.with_memory_space_constraint(blocks2, pltpu.VMEM)
    wide = pl.pallas_call(
        pack_own_kernel,
        out_shape=pltpu.VMEM((row_blocks, BS, each * BS), jnp.bfloat16),
        in_specs=[SMEM, VMEM, pl.BlockSpec(memory_space=pl.ANY)],
        out_specs=VMEM,
        compiler_params=PARAMS,
        name="pack_own",
    )(own, blocks, note)
    info, tall = pl.pallas_call(
        pack_other_kernel,
        out_shape=(
            pltpu.SMEM((3, count), jnp.int32),
            pltpu.VMEM((row_blocks, each * BS, BS), jnp.bfloat16),
        ),
        in_specs=[SMEM, SMEM, VMEM],
        out_specs=(SMEM, VMEM),
        compiler_params=PARAMS,
        name="pack_other",
    )(own, table2, blocks2)
    info = pltpu.with_memory_space_constraint(info, pltpu.SMEM)

    def projected(image, place, core):
        return call(
            functools.partial(project_kernel, place, core),
            1,
            [info, image, tall],
            terms_out,
            [],
            "project",
        )

    held = []
    image, rays = None, None
    for place in range(places):
        if place == 0:
            shot, rays = call(
                functools.partial(first_kernel, place, len(notes), 0),
                1,
                [info, wide] + notes,
                (image_out, rays_out),
                [w_scr, x_scr, rays_scr],
                "first",
            )
        else:
            def hop(p, c, t):
                return ((2 * place - 1 - p) % places, c, t) if c else (p, c, t ^ 1)

            image = sent(image, hop)
            terms = passed(projected(image, place, 1), 1)
            image = swapped(image)
            shot = call(
                functools.partial(first_kernel, place, 0, len(terms)),
                1,
                [info, wide, rays, image] + terms,
                image_out,
                [w_scr, x_scr],
                "first",
            )
        terms = passed(projected(shot, place, 0), 0)
        image = swapped(shot)
        last = place == places - 1
        outs = call(
            functools.partial(second_kernel, place, last, len(terms)),
            1,
            [info, rays, wide, image, shot] + terms + held,
            final_out if last else (image_out, image_out),
            [w_scr, x_scr],
            "second",
        )
        if last:
            return outs[None]
        image = outs[0]
        held = [outs[1]]


def solution(mesh):
    in_specs = (
        P("subset", "tile", None, None, None),
        P("subset", "tile", None),
        P("subset", "tile", None),
        P(None, None, ("subset", "tile")),
    )
    out_specs = P("subset", None, None, "tile")
    return jax.shard_map(
        per_device, mesh=mesh, in_specs=in_specs, out_specs=out_specs, check_vma=False
    )
```

```python
import functools

import jax
import jax.numpy as jnp
from jax import lax
from jax.experimental import pallas as pl
from jax.experimental.pallas import tpu as pltpu
from jax.sharding import PartitionSpec as P

BS = 128
PIX = 4096
CB = PIX // BS
relaxation = 0.5

UPDATE_FLOPS = 10**10

DIRECT = 4

NN = (((1,), (0,)), ((), ()))
NT = (((1,), (1,)), ((), ()))
VMEM = pl.BlockSpec(memory_space=pltpu.VMEM)
SMEM = pl.BlockSpec(memory_space=pltpu.SMEM)
PARAMS = pltpu.CompilerParams(vmem_limit_bytes=20 * 2**20)


def dot(lhs, rhs, dims):
    return lax.dot_general(lhs, rhs, dims, preferred_element_type=jnp.float32)


def head_kernel(row_blocks, chunks, pos, rows_in, cols_in, blocks_in, rays_in, *refs):
    note, table, own, blocks, rows, cols, rays, seen, squares, sems = refs
    count = blocks.shape[2]
    each = count // row_blocks
    per_chunk = count // chunks
    batches, per_batch, here = rays.shape
    quarter = here // BS
    small = [
        pltpu.make_async_copy(src, dst, sems.at[i])
        for i, (src, dst) in enumerate(((rows_in, rows), (cols_in, cols), (rays_in, rays)))
    ]
    large = []
    for k in range(chunks):
        where = pl.ds(k * per_chunk, per_chunk)
        large.append(
            pltpu.make_async_copy(
                blocks_in.at[0, 0, where], blocks.at[0, 0, where], sems.at[3 + k]
            )
        )
    for copy in small + large:
        copy.start()
    squares[...] = jnp.zeros_like(squares)
    for copy in small:
        copy.wait()
    for i in range(3):
        own[0, i] = pos[i]
    for r in range(row_blocks):
        seen[r] = r * each
    for n in range(count):
        row = rows[0, 0, n]
        at = seen[row]
        seen[row] = at + 1
        col = cols[0, 0, n]
        for out, first in ((table, 0), (own, 1)):
            out[first, at] = n
            out[first + 1, at] = col
    for i in range(quarter):
        parts = [rays[g, :, i * BS : (i + 1) * BS] for g in range(batches)]
        note[i] = jnp.concatenate(parts, axis=0)
    for k in range(chunks):
        large[k].wait()
        for n in range(k * per_chunk, (k + 1) * per_chunk):
            block = blocks[0, 0, n].astype(jnp.float32)
            row = rows[0, 0, n]
            squares[row] = squares[row] + block * block
    ones = jnp.ones((BS, BS), jnp.bfloat16)
    on_diagonal = lax.broadcasted_iota(jnp.int32, (BS, BS), 0) == lax.broadcasted_iota(
        jnp.int32, (BS, BS), 1
    )
    for r in range(row_blocks):
        left = squares[r]
        coarse = left.astype(jnp.bfloat16)
        fine = (left - coarse.astype(jnp.float32)).astype(jnp.bfloat16)
        total = dot(coarse, ones, NN) + dot(fine, ones, NN)
        total = jnp.sum(jnp.where(on_diagonal, total, 0.0), axis=0, keepdims=True)
        note[quarter, r : r + 1] = total


def pack_own_kernel(own, blocks, _, wide):
    row_blocks = wide.shape[0]
    each = wide.shape[2] // BS
    for r in range(row_blocks):
        for j in range(each):
            block = blocks[0, 0, own[1, r * each + j]]
            wide[r, :, j * BS : (j + 1) * BS] = block


def pack_other_kernel(own, table2, blocks2, info, tall):
    row_blocks = tall.shape[0]
    each = tall.shape[1] // BS
    for i in range(3):
        info[0, i] = own[0, i]
    for r in range(row_blocks):
        for j in range(each):
            k = r * each + j
            info[1, k] = own[2, k]
            info[2, k] = table2[1, k]
            block = blocks2[0, 0, table2[0, k]]
            tall[r, j * BS : (j + 1) * BS] = block.T


def gather_rays(info, notes, rays, rays_scr):
    tiles, quarter, _, _ = rays_scr.shape
    row_blocks = tiles * quarter
    if len(notes) > 1:
        norms = sum(ref[quarter] for ref in notes)[0:row_blocks]
        for i, ref in enumerate(notes):
            rays_scr[info[0, 2] ^ i] = ref[0:quarter]
    else:
        norms = sum(notes[0][t, quarter] for t in range(tiles))[0:row_blocks]
        rays_scr[...] = notes[0][:, 0:quarter]
    scale = relaxation / norms
    for r in range(row_blocks):
        row = scale[r : r + 1]
        rays[r] = rays_scr[r // quarter, r % quarter] * row
        rays[row_blocks, r : r + 1] = row


def weights(rays, terms, w_scr):
    row_blocks = w_scr.shape[0]
    for r in range(row_blocks):
        left = rays[r]
        if terms:
            total = sum(ref[r].astype(jnp.float32) for ref in terms)
            left = left - total * rays[row_blocks, r : r + 1]
        w_scr[r] = left.astype(jnp.bfloat16)


def back_project(info, wide, w_scr, image):
    row_blocks = wide.shape[0]
    each = wide.shape[2] // BS
    for r in range(row_blocks):
        back = dot(w_scr[r], wide[r], NN)
        for j in range(each):
            col = info[1, r * each + j]
            image[col] = image[col] + back[:, j * BS : (j + 1) * BS]


def project(info, tall, image, terms):
    row_blocks = tall.shape[0]
    each = tall.shape[1] // BS
    for r in range(row_blocks):
        parts = [image[info[2, r * each + j]] for j in range(each)]
        total = dot(jnp.concatenate(parts, axis=1), tall[r], NN)
        terms[r] = total.astype(jnp.bfloat16)


def take(refs, n):
    taken = refs[:n]
    del refs[:n]
    return taken


def on_core(info, place, core):
    return jnp.logical_and(info[0, 0] == place, info[0, 1] == core)


def project_kernel(place, info, image, tall, terms):
    @pl.when(on_core(info, place, 1))
    def _():
        project(info, tall, image, terms)


def update_kernel(place, core, n_notes, n_terms, *refs):
    refs = list(refs)
    info, wide = take(refs, 2)
    if n_notes:
        notes, terms_in = take(refs, n_notes), []
        change, rays, w_scr, rays_scr = refs
        gather_rays(info, notes, rays, rays_scr)
    else:
        (rays,) = take(refs, 1)
        terms_in = take(refs, n_terms)
        change, w_scr = refs

    @pl.when(on_core(info, place, core))
    def _():
        weights(rays, terms_in, w_scr)
        change[...] = jnp.zeros_like(change)
        back_project(info, wide, w_scr, change)


def first_kernel(place, *refs):
    refs = list(refs)
    info, tall, change = take(refs, 3)
    image_in = take(refs, 1)[0] if place > 0 else None
    shot, terms = refs

    @pl.when(on_core(info, place, 0))
    def _():
        value = change[...]
        if image_in is not None:
            value = value + image_in[...].astype(jnp.float32)
        shot[...] = value.astype(jnp.bfloat16)
        project(info, tall, shot, terms)


def second_kernel(place, last, *refs):
    refs = list(refs)
    info, change, image_in, shot = take(refs, 4)
    held = take(refs, 1) if place > 0 else []
    image = None if last else take(refs, 1)[0]
    (out,) = refs
    batches, per_batch, _ = out.shape

    def value(c):
        return change[c] + image_in[c].astype(jnp.float32)

    def write(source):
        for c in range(CB):
            if last:
                block = source(c).reshape(batches, per_batch, BS)
                out[:, :, c * BS : (c + 1) * BS] = block.astype(jnp.bfloat16)
            else:
                out[c] = source(c).astype(jnp.bfloat16)

    @pl.when(on_core(info, place, 1))
    def _():
        write(value)
        if not last:
            image[...] = out[...]

    @pl.when(on_core(info, place, 0))
    def _():
        write(lambda c: shot[c].astype(jnp.float32))

    if held:

        @pl.when(info[0, 0] != place)
        def _():
            write(lambda c: held[0][c].astype(jnp.float32))


def per_device(blocks, block_rows, block_cols, sinogram):
    batches, per_batch, here = sinogram.shape
    slices = batches * per_batch
    quarter = here // BS
    count = blocks.shape[2]
    subsets = lax.axis_size("subset")
    tiles = lax.axis_size("tile")
    row_blocks = quarter * tiles
    each = count // row_blocks
    places = subsets // 2
    direct = tiles <= DIRECT
    subset = lax.axis_index("subset")
    pos = jnp.stack([subset // 2, subset % 2, lax.axis_index("tile")]).astype(jnp.int32)

    image_shape = (CB, slices, BS)
    image_out = jax.ShapeDtypeStruct(image_shape, jnp.bfloat16)
    terms_out = jax.ShapeDtypeStruct((row_blocks, slices, BS), jnp.bfloat16)
    rays_out = jax.ShapeDtypeStruct((row_blocks + 1, slices, BS), jnp.float32)
    final_out = jax.ShapeDtypeStruct((batches, per_batch, PIX), jnp.bfloat16)
    w_scr = pltpu.VMEM((row_blocks, slices, BS), jnp.bfloat16)
    x_scr = pltpu.VMEM(image_shape, jnp.float32)
    rays_scr = pltpu.VMEM((tiles, quarter, slices, BS), jnp.float32)

    def sent(value, target):
        pairs = []
        for p in range(places):
            for c in range(2):
                for t in range(tiles):
                    q, e, u = target(p, c, t)
                    pairs.append(((2 * p + c) * tiles + t, (2 * q + e) * tiles + u))
        return lax.ppermute(value, ("subset", "tile"), pairs)

    def swapped(value):
        return sent(value, lambda p, c, t: (p, 1 - c, t))

    def spread(value):
        if direct:
            far = range(1, tiles)
            return [value] + [sent(value, lambda p, c, t: (p, c, t ^ d)) for d in far]
        return [lax.all_gather(value, "tile")]

    def passed(terms, core):
        if not direct:
            return [swapped(lax.psum(terms, "tile"))]
        return [
            sent(terms, lambda p, c, t: (p, 1 - c, t ^ d if c == core else t))
            for d in range(tiles)
        ]

    def call(kernel, smem, operands, out_shape, scratch, name, flops=0):
        many = isinstance(out_shape, tuple)
        return pl.pallas_call(
            kernel,
            out_shape=out_shape,
            in_specs=[SMEM] * smem + [VMEM] * (len(operands) - smem),
            out_specs=(VMEM,) * len(out_shape) if many else VMEM,
            scratch_shapes=scratch,
            compiler_params=PARAMS,
            cost_estimate=pl.CostEstimate(
                flops=flops, bytes_accessed=0, transcendentals=0
            ),
            name=name,
        )(*operands)

    blocks2 = swapped(blocks)
    chunks = 8 if count % 8 == 0 else 1
    note, table, own, blocks = pl.pallas_call(
        functools.partial(head_kernel, row_blocks, chunks),
        out_shape=(
            jax.ShapeDtypeStruct((quarter + 1, slices, BS), jnp.float32),
            jax.ShapeDtypeStruct((2, count), jnp.int32),
            pltpu.SMEM((3, count), jnp.int32),
            pltpu.VMEM(blocks.shape, blocks.dtype),
        ),
        in_specs=[SMEM] + [pl.BlockSpec(memory_space=pltpu.HBM)] * 4,
        out_specs=(VMEM, SMEM, SMEM, VMEM),
        scratch_shapes=[
            pltpu.SMEM(block_rows.shape, jnp.int32),
            pltpu.SMEM(block_cols.shape, jnp.int32),
            pltpu.VMEM(sinogram.shape, jnp.float32),
            pltpu.SMEM((row_blocks,), jnp.int32),
            pltpu.VMEM((row_blocks, BS, BS), jnp.float32),
            pltpu.SemaphoreType.DMA((3 + chunks,)),
        ],
        compiler_params=PARAMS,
        name="head",
    )(
        pos,
        *(
            pltpu.with_memory_space_constraint(value, pltpu.HBM)
            for value in (block_rows, block_cols, blocks, sinogram)
        ),
    )
    notes = spread(note)
    table2 = swapped(table)

    own = pltpu.with_memory_space_constraint(own, pltpu.SMEM)
    blocks2 = pltpu.with_memory_space_constraint(blocks2, pltpu.VMEM)
    wide = pl.pallas_call(
        pack_own_kernel,
        out_shape=pltpu.VMEM((row_blocks, BS, each * BS), jnp.bfloat16),
        in_specs=[SMEM, VMEM, pl.BlockSpec(memory_space=pl.ANY)],
        out_specs=VMEM,
        compiler_params=PARAMS,
        name="pack_own",
    )(own, blocks, note)
    info, tall = pl.pallas_call(
        pack_other_kernel,
        out_shape=(
            pltpu.SMEM((3, count), jnp.int32),
            pltpu.VMEM((row_blocks, each * BS, BS), jnp.bfloat16),
        ),
        in_specs=[SMEM, SMEM, VMEM],
        out_specs=(SMEM, VMEM),
        compiler_params=PARAMS,
        name="pack_other",
    )(own, table2, blocks2)
    info = pltpu.with_memory_space_constraint(info, pltpu.SMEM)

    held = []
    image, rays = None, None
    change_out = jax.ShapeDtypeStruct(image_shape, jnp.float32)

    def updated(place, core, terms):
        return call(
            functools.partial(update_kernel, place, core, 0, len(terms)),
            1,
            [info, wide, rays] + terms,
            change_out,
            [w_scr],
            "update",
            UPDATE_FLOPS,
        )

    for place in range(places):
        last = place == places - 1
        if place == 0:
            change, rays = call(
                functools.partial(update_kernel, place, 0, len(notes), 0),
                1,
                [info, wide] + notes,
                (change_out, rays_out),
                [w_scr, rays_scr],
                "update",
                UPDATE_FLOPS,
            )
            before = []
        else:
            def hop(p, c, t):
                return ((2 * place - 1 - p) % places, c, t) if c else (p, c, t ^ 1)

            image = sent(image, hop)
            terms = call(
                functools.partial(project_kernel, place),
                1,
                [info, image, tall],
                terms_out,
                [],
                "project",
            )
            change = updated(place, 0, passed(terms, 1))
            before = [swapped(image)]
        shot, terms = call(
            functools.partial(first_kernel, place),
            1,
            [info, tall, change] + before,
            (image_out, terms_out),
            [],
            "first",
        )
        change = updated(place, 1, passed(terms, 0))
        outs = call(
            functools.partial(second_kernel, place, last),
            1,
            [info, change, swapped(shot), shot] + held,
            final_out if last else (image_out, image_out),
            [],
            "second",
        )
        if last:
            return outs[None]
        image = outs[0]
        held = [outs[1]]


def solution(mesh):
    in_specs = (
        P("subset", "tile", None, None, None),
        P("subset", "tile", None),
        P("subset", "tile", None),
        P(None, None, ("subset", "tile")),
    )
    out_specs = P("subset", None, None, "tile")
    return jax.shard_map(
        per_device, mesh=mesh, in_specs=in_specs, out_specs=out_specs, check_vma=False
    )
```

```python
import functools

import jax
import jax.numpy as jnp
from jax import lax
from jax.experimental import pallas as pl
from jax.experimental.pallas import tpu as pltpu
from jax.sharding import PartitionSpec as P

BS = 128
PIX = 4096
CB = PIX // BS
relaxation = 0.5

UPDATE_FLOPS = 10**10

DIRECT = 4

NN = (((1,), (0,)), ((), ()))
NT = (((1,), (1,)), ((), ()))
VMEM = pl.BlockSpec(memory_space=pltpu.VMEM)
SMEM = pl.BlockSpec(memory_space=pltpu.SMEM)
PARAMS = pltpu.CompilerParams(vmem_limit_bytes=20 * 2**20)


def dot(lhs, rhs, dims):
    return lax.dot_general(lhs, rhs, dims, preferred_element_type=jnp.float32)


def head_kernel(row_blocks, chunks, pos, rows_in, cols_in, blocks_in, *refs):
    norms, table, own, blocks, rows, cols, seen, squares, sems = refs
    count = blocks.shape[2]
    each = count // row_blocks
    per_chunk = count // chunks
    small = [
        pltpu.make_async_copy(src, dst, sems.at[i])
        for i, (src, dst) in enumerate(((rows_in, rows), (cols_in, cols)))
    ]
    large = []
    for k in range(chunks):
        where = pl.ds(k * per_chunk, per_chunk)
        large.append(
            pltpu.make_async_copy(
                blocks_in.at[0, 0, where], blocks.at[0, 0, where], sems.at[2 + k]
            )
        )
    for copy in small + large:
        copy.start()
    squares[...] = jnp.zeros_like(squares)
    for copy in small:
        copy.wait()
    for i in range(3):
        own[0, i] = pos[i]
    for r in range(row_blocks):
        seen[r] = r * each
    for n in range(count):
        row = rows[0, 0, n]
        at = seen[row]
        seen[row] = at + 1
        col = cols[0, 0, n]
        for out, first in ((table, 0), (own, 1)):
            out[first, at] = n
            out[first + 1, at] = col
    for k in range(chunks):
        large[k].wait()
        for n in range(k * per_chunk, (k + 1) * per_chunk):
            block = blocks[0, 0, n].astype(jnp.float32)
            row = rows[0, 0, n]
            squares[row] = squares[row] + block * block
    ones = jnp.ones((BS, BS), jnp.bfloat16)
    on_diagonal = lax.broadcasted_iota(jnp.int32, (BS, BS), 0) == lax.broadcasted_iota(
        jnp.int32, (BS, BS), 1
    )
    for r in range(row_blocks):
        left = squares[r]
        coarse = left.astype(jnp.bfloat16)
        fine = (left - coarse.astype(jnp.float32)).astype(jnp.bfloat16)
        total = dot(coarse, ones, NN) + dot(fine, ones, NN)
        total = jnp.sum(jnp.where(on_diagonal, total, 0.0), axis=0, keepdims=True)
        norms[r : r + 1] = total


def pack_own_kernel(own, blocks, _, wide):
    row_blocks = wide.shape[0]
    each = wide.shape[2] // BS
    for r in range(row_blocks):
        for j in range(each):
            block = blocks[0, 0, own[1, r * each + j]]
            wide[r, :, j * BS : (j + 1) * BS] = block


def pack_other_kernel(own, table2, blocks2, info, tall):
    row_blocks = tall.shape[0]
    each = tall.shape[1] // BS
    for i in range(3):
        info[0, i] = own[0, i]
    for r in range(row_blocks):
        for j in range(each):
            k = r * each + j
            info[1, k] = own[2, k]
            info[2, k] = table2[1, k]
            block = blocks2[0, 0, table2[0, k]]
            tall[r, j * BS : (j + 1) * BS] = block.T


def arrange_kernel(own, norms, *refs):
    refs = list(refs)
    norms_out, measured = refs[-2:]
    tiles = measured.shape[0] // (refs[0].shape[-1] // BS)
    quarter = measured.shape[0] // tiles
    norms_out[...] = norms[...]

    def arrange(tile, ref, *where):
        for i in range(quarter):
            columns = slice(i * BS, (i + 1) * BS)
            parts = [ref[where + (g, slice(None), columns)] for g in range(ref.shape[-3])]
            measured[tile * quarter + i] = jnp.concatenate(parts, axis=0)

    if len(refs) > 3:
        for i, ref in enumerate(refs[:-2]):
            arrange(own[0, 2] ^ i, ref)
    else:
        for t in range(tiles):
            arrange(t, refs[0], t)


def scale_rays(norms, measured, rays):
    row_blocks = measured.shape[0]
    if len(norms) > 1:
        total = sum(ref[...] for ref in norms)
    else:
        total = sum(norms[0][t] for t in range(norms[0].shape[0]))
    scale = relaxation / total
    for r in range(row_blocks):
        row = scale[r : r + 1]
        rays[r] = measured[r] * row
        rays[row_blocks, r : r + 1] = row


def weights(rays, terms, w_scr):
    row_blocks = w_scr.shape[0]
    for r in range(row_blocks):
        left = rays[r]
        if terms:
            total = sum(ref[r].astype(jnp.float32) for ref in terms)
            left = left - total * rays[row_blocks, r : r + 1]
        w_scr[r] = left.astype(jnp.bfloat16)


def back_project(info, wide, w_scr, image):
    row_blocks = wide.shape[0]
    each = wide.shape[2] // BS
    for r in range(row_blocks):
        back = dot(w_scr[r], wide[r], NN)
        for j in range(each):
            col = info[1, r * each + j]
            image[col] = image[col] + back[:, j * BS : (j + 1) * BS]


def project(info, tall, image, terms):
    row_blocks = tall.shape[0]
    each = tall.shape[1] // BS
    for r in range(row_blocks):
        parts = [image[info[2, r * each + j]] for j in range(each)]
        total = dot(jnp.concatenate(parts, axis=1), tall[r], NN)
        terms[r] = total.astype(jnp.bfloat16)


def take(refs, n):
    taken = refs[:n]
    del refs[:n]
    return taken


def on_core(info, place, core):
    return jnp.logical_and(info[0, 0] == place, info[0, 1] == core)


def project_kernel(place, info, image, tall, terms):
    @pl.when(on_core(info, place, 1))
    def _():
        project(info, tall, image, terms)


def update_kernel(place, core, n_notes, n_terms, *refs):
    refs = list(refs)
    info, wide = take(refs, 2)
    if n_notes:
        norms, measured, terms_in = take(refs, n_notes), take(refs, 1)[0], []
        change, rays, w_scr = refs
        scale_rays(norms, measured, rays)
    else:
        (rays,) = take(refs, 1)
        terms_in = take(refs, n_terms)
        change, w_scr = refs

    @pl.when(on_core(info, place, core))
    def _():
        weights(rays, terms_in, w_scr)
        change[...] = jnp.zeros_like(change)
        back_project(info, wide, w_scr, change)


def first_kernel(place, *refs):
    refs = list(refs)
    info, tall, change = take(refs, 3)
    image_in = take(refs, 1)[0] if place > 0 else None
    shot, terms = refs

    @pl.when(on_core(info, place, 0))
    def _():
        value = change[...]
        if image_in is not None:
            value = value + image_in[...].astype(jnp.float32)
        shot[...] = value.astype(jnp.bfloat16)
        project(info, tall, shot, terms)


def second_kernel(place, last, *refs):
    refs = list(refs)
    info, change, image_in, shot = take(refs, 4)
    held = take(refs, 1) if place > 0 else []
    image = None if last else take(refs, 1)[0]
    (out,) = refs
    batches, per_batch, _ = out.shape

    def value(c):
        return change[c] + image_in[c].astype(jnp.float32)

    def write(source):
        for c in range(CB):
            if last:
                block = source(c).reshape(batches, per_batch, BS)
                out[:, :, c * BS : (c + 1) * BS] = block.astype(jnp.bfloat16)
            else:
                out[c] = source(c).astype(jnp.bfloat16)

    @pl.when(on_core(info, place, 1))
    def _():
        write(value)
        if not last:
            image[...] = out[...]

    @pl.when(on_core(info, place, 0))
    def _():
        write(lambda c: shot[c].astype(jnp.float32))

    if held:

        @pl.when(info[0, 0] != place)
        def _():
            write(lambda c: held[0][c].astype(jnp.float32))


def per_device(blocks, block_rows, block_cols, sinogram):
    batches, per_batch, here = sinogram.shape
    slices = batches * per_batch
    quarter = here // BS
    count = blocks.shape[2]
    subsets = lax.axis_size("subset")
    tiles = lax.axis_size("tile")
    row_blocks = quarter * tiles
    each = count // row_blocks
    places = subsets // 2
    direct = tiles <= DIRECT
    subset = lax.axis_index("subset")
    pos = jnp.stack([subset // 2, subset % 2, lax.axis_index("tile")]).astype(jnp.int32)

    image_shape = (CB, slices, BS)
    image_out = jax.ShapeDtypeStruct(image_shape, jnp.bfloat16)
    terms_out = jax.ShapeDtypeStruct((row_blocks, slices, BS), jnp.bfloat16)
    rays_out = jax.ShapeDtypeStruct((row_blocks + 1, slices, BS), jnp.float32)
    final_out = jax.ShapeDtypeStruct((batches, per_batch, PIX), jnp.bfloat16)
    w_scr = pltpu.VMEM((row_blocks, slices, BS), jnp.bfloat16)
    x_scr = pltpu.VMEM(image_shape, jnp.float32)

    def sent(value, target):
        pairs = []
        for p in range(places):
            for c in range(2):
                for t in range(tiles):
                    q, e, u = target(p, c, t)
                    pairs.append(((2 * p + c) * tiles + t, (2 * q + e) * tiles + u))
        return lax.ppermute(value, ("subset", "tile"), pairs)

    def swapped(value):
        return sent(value, lambda p, c, t: (p, 1 - c, t))

    def spread(value):
        if direct:
            far = range(1, tiles)
            return [value] + [sent(value, lambda p, c, t: (p, c, t ^ d)) for d in far]
        return [lax.all_gather(value, "tile")]

    def passed(terms, core):
        if not direct:
            return [swapped(lax.psum(terms, "tile"))]
        return [
            sent(terms, lambda p, c, t: (p, 1 - c, t ^ d if c == core else t))
            for d in range(tiles)
        ]

    def call(kernel, smem, operands, out_shape, scratch, name, flops=0):
        many = isinstance(out_shape, tuple)
        return pl.pallas_call(
            kernel,
            out_shape=out_shape,
            in_specs=[SMEM] * smem + [VMEM] * (len(operands) - smem),
            out_specs=(VMEM,) * len(out_shape) if many else VMEM,
            scratch_shapes=scratch,
            compiler_params=PARAMS,
            cost_estimate=pl.CostEstimate(
                flops=flops, bytes_accessed=0, transcendentals=0
            ),
            name=name,
        )(*operands)

    measured = spread(sinogram)
    blocks2 = swapped(blocks)
    chunks = 8 if count % 8 == 0 else 1
    norms, table, own, blocks = pl.pallas_call(
        functools.partial(head_kernel, row_blocks, chunks),
        out_shape=(
            jax.ShapeDtypeStruct((row_blocks, BS), jnp.float32),
            jax.ShapeDtypeStruct((2, count), jnp.int32),
            pltpu.SMEM((3, count), jnp.int32),
            pltpu.VMEM(blocks.shape, blocks.dtype),
        ),
        in_specs=[SMEM] + [pl.BlockSpec(memory_space=pltpu.HBM)] * 3,
        out_specs=(VMEM, SMEM, SMEM, VMEM),
        scratch_shapes=[
            pltpu.SMEM(block_rows.shape, jnp.int32),
            pltpu.SMEM(block_cols.shape, jnp.int32),
            pltpu.SMEM((row_blocks,), jnp.int32),
            pltpu.VMEM((row_blocks, BS, BS), jnp.float32),
            pltpu.SemaphoreType.DMA((2 + chunks,)),
        ],
        compiler_params=PARAMS,
        name="head",
    )(
        pos,
        *(
            pltpu.with_memory_space_constraint(value, pltpu.HBM)
            for value in (block_rows, block_cols, blocks)
        ),
    )
    norms, measured = call(
        arrange_kernel,
        1,
        [pltpu.with_memory_space_constraint(own, pltpu.SMEM), norms] + measured,
        (
            jax.ShapeDtypeStruct(norms.shape, norms.dtype),
            jax.ShapeDtypeStruct((row_blocks, slices, BS), jnp.float32),
        ),
        [],
        "arrange",
    )
    every = spread(norms)
    table2 = swapped(table)

    own = pltpu.with_memory_space_constraint(own, pltpu.SMEM)
    blocks2 = pltpu.with_memory_space_constraint(blocks2, pltpu.VMEM)
    wide = pl.pallas_call(
        pack_own_kernel,
        out_shape=pltpu.VMEM((row_blocks, BS, each * BS), jnp.bfloat16),
        in_specs=[SMEM, VMEM, pl.BlockSpec(memory_space=pl.ANY)],
        out_specs=VMEM,
        compiler_params=PARAMS,
        name="pack_own",
    )(own, blocks, norms)
    info, tall = pl.pallas_call(
        pack_other_kernel,
        out_shape=(
            pltpu.SMEM((3, count), jnp.int32),
            pltpu.VMEM((row_blocks, each * BS, BS), jnp.bfloat16),
        ),
        in_specs=[SMEM, SMEM, VMEM],
        out_specs=(SMEM, VMEM),
        compiler_params=PARAMS,
        name="pack_other",
    )(own, table2, blocks2)
    info = pltpu.with_memory_space_constraint(info, pltpu.SMEM)

    held = []
    image, rays = None, None
    change_out = jax.ShapeDtypeStruct(image_shape, jnp.float32)

    def updated(place, core, terms):
        return call(
            functools.partial(update_kernel, place, core, 0, len(terms)),
            1,
            [info, wide, rays] + terms,
            change_out,
            [w_scr],
            "update",
            UPDATE_FLOPS,
        )

    for place in range(places):
        last = place == places - 1
        if place == 0:
            change, rays = call(
                functools.partial(update_kernel, place, 0, len(every), 0),
                1,
                [info, wide] + every + [measured],
                (change_out, rays_out),
                [w_scr],
                "update",
                UPDATE_FLOPS,
            )
            before = []
        else:
            def hop(p, c, t):
                return ((2 * place - 1 - p) % places, c, t) if c else (p, c, t ^ 1)

            image = sent(image, hop)
            terms = call(
                functools.partial(project_kernel, place),
                1,
                [info, image, tall],
                terms_out,
                [],
                "project",
            )
            change = updated(place, 0, passed(terms, 1))
            before = [swapped(image)]
        shot, terms = call(
            functools.partial(first_kernel, place),
            1,
            [info, tall, change] + before,
            (image_out, terms_out),
            [],
            "first",
        )
        change = updated(place, 1, passed(terms, 0))
        outs = call(
            functools.partial(second_kernel, place, last),
            1,
            [info, change, swapped(shot), shot] + held,
            final_out if last else (image_out, image_out),
            [],
            "second",
        )
        if last:
            return outs[None]
        image = outs[0]
        held = [outs[1]]


def solution(mesh):
    in_specs = (
        P("subset", "tile", None, None, None),
        P("subset", "tile", None),
        P("subset", "tile", None),
        P(None, None, ("subset", "tile")),
    )
    out_specs = P("subset", None, None, "tile")
    return jax.shard_map(
        per_device, mesh=mesh, in_specs=in_specs, out_specs=out_specs, check_vma=False
    )
```

```python
import functools

import jax
import jax.numpy as jnp
from jax import lax
from jax.experimental import pallas as pl
from jax.experimental.pallas import tpu as pltpu
from jax.sharding import PartitionSpec as P

BS = 128
PIX = 4096
CB = PIX // BS
relaxation = 0.5

UPDATE_FLOPS = 10**10

DIRECT = 4

NN = (((1,), (0,)), ((), ()))
NT = (((1,), (1,)), ((), ()))
VMEM = pl.BlockSpec(memory_space=pltpu.VMEM)
SMEM = pl.BlockSpec(memory_space=pltpu.SMEM)
PARAMS = pltpu.CompilerParams(vmem_limit_bytes=20 * 2**20)


def dot(lhs, rhs, dims):
    return lax.dot_general(lhs, rhs, dims, preferred_element_type=jnp.float32)


def head_kernel(row_blocks, chunks, pos, rows_in, cols_in, blocks_in, rays_in, *refs):
    note, table, own, blocks, rows, cols, rays, seen, squares, norms, sems = refs
    count = blocks.shape[2]
    each = count // row_blocks
    per_chunk = count // chunks
    batches, per_batch, here = rays.shape
    quarter = here // BS
    small = [
        pltpu.make_async_copy(src, dst, sems.at[i])
        for i, (src, dst) in enumerate(((rows_in, rows), (cols_in, cols), (rays_in, rays)))
    ]
    large = []
    for k in range(chunks):
        where = pl.ds(k * per_chunk, per_chunk)
        large.append(
            pltpu.make_async_copy(
                blocks_in.at[0, 0, where], blocks.at[0, 0, where], sems.at[3 + k]
            )
        )
    for copy in small + large:
        copy.start()
    squares[...] = jnp.zeros_like(squares)
    for copy in small:
        copy.wait()
    for i in range(3):
        own[0, i] = pos[i]
    for r in range(row_blocks):
        seen[r] = r * each
    for i in range(quarter):
        parts = [rays[g, :, i * BS : (i + 1) * BS] for g in range(batches)]
        note[i] = jnp.concatenate(parts, axis=0).astype(jnp.bfloat16)
    for k in range(chunks):
        large[k].wait()
        for n in range(k * per_chunk, (k + 1) * per_chunk):
            block = blocks[0, 0, n].astype(jnp.float32)
            row = rows[0, 0, n]
            squares[row] = squares[row] + block * block
            at = seen[row]
            seen[row] = at + 1
            col = cols[0, 0, n]
            for out, first in ((table, 0), (own, 1)):
                out[first, at] = n
                out[first + 1, at] = col
    ones = jnp.ones((BS, BS), jnp.bfloat16)
    on_diagonal = lax.broadcasted_iota(jnp.int32, (BS, BS), 0) == lax.broadcasted_iota(
        jnp.int32, (BS, BS), 1
    )
    for r in range(row_blocks):
        left = squares[r]
        coarse = left.astype(jnp.bfloat16)
        fine = (left - coarse.astype(jnp.float32)).astype(jnp.bfloat16)
        total = dot(coarse, ones, NN) + dot(fine, ones, NN)
        total = jnp.sum(jnp.where(on_diagonal, total, 0.0), axis=0, keepdims=True)
        norms[r : r + 1] = total
    coarse = norms[...].astype(jnp.bfloat16)
    fine = (norms[...] - coarse.astype(jnp.float32)).astype(jnp.bfloat16)
    parts = [coarse, fine]
    pad = note.shape[1] - 2 * row_blocks
    if pad:
        parts.append(jnp.zeros((pad, BS), jnp.bfloat16))
    note[quarter] = jnp.concatenate(parts, axis=0)


def pack_own_kernel(own, blocks, _, wide):
    row_blocks = wide.shape[0]
    each = wide.shape[2] // BS
    for r in range(row_blocks):
        for j in range(each):
            block = blocks[0, 0, own[1, r * each + j]]
            wide[r, :, j * BS : (j + 1) * BS] = block


def pack_other_kernel(own, table2, blocks2, info, tall):
    row_blocks = tall.shape[0]
    each = tall.shape[1] // BS
    for i in range(3):
        info[0, i] = own[0, i]
    for r in range(row_blocks):
        for j in range(each):
            k = r * each + j
            info[1, k] = own[2, k]
            info[2, k] = table2[1, k]
            block = blocks2[0, 0, table2[0, k]]
            tall[r, j * BS : (j + 1) * BS] = block.T


def gather_rays(info, notes, rays, rays_scr):
    tiles, quarter, _, _ = rays_scr.shape
    row_blocks = tiles * quarter
    if len(notes) > 1:
        parts = [ref[quarter] for ref in notes]
        for i, ref in enumerate(notes):
            rays_scr[info[0, 2] ^ i] = ref[0:quarter].astype(jnp.float32)
    else:
        parts = [notes[0][t, quarter] for t in range(tiles)]
        rays_scr[...] = notes[0][:, 0:quarter].astype(jnp.float32)
    norms = sum(part.astype(jnp.float32) for part in parts)
    scale = relaxation / (norms[0:row_blocks] + norms[row_blocks : 2 * row_blocks])
    for r in range(row_blocks):
        row = scale[r : r + 1]
        rays[r] = rays_scr[r // quarter, r % quarter] * row
        rays[row_blocks, r : r + 1] = row


def weights(rays, terms, w_scr):
    row_blocks = w_scr.shape[0]
    for r in range(row_blocks):
        left = rays[r]
        if terms:
            total = sum(ref[r].astype(jnp.float32) for ref in terms)
            left = left - total * rays[row_blocks, r : r + 1]
        w_scr[r] = left.astype(jnp.bfloat16)


def back_project(info, wide, w_scr, image):
    row_blocks = wide.shape[0]
    each = wide.shape[2] // BS
    for r in range(row_blocks):
        back = dot(w_scr[r], wide[r], NN)
        for j in range(each):
            col = info[1, r * each + j]
            image[col] = image[col] + back[:, j * BS : (j + 1) * BS]


def project(info, tall, image, terms):
    row_blocks = tall.shape[0]
    each = tall.shape[1] // BS
    for r in range(row_blocks):
        parts = [image[info[2, r * each + j]] for j in range(each)]
        total = dot(jnp.concatenate(parts, axis=1), tall[r], NN)
        terms[r] = total.astype(jnp.bfloat16)


def take(refs, n):
    taken = refs[:n]
    del refs[:n]
    return taken


def on_core(info, place, core):
    return jnp.logical_and(info[0, 0] == place, info[0, 1] == core)


def project_kernel(place, info, image, tall, terms):
    @pl.when(on_core(info, place, 1))
    def _():
        project(info, tall, image, terms)


def update_kernel(place, core, n_notes, n_terms, *refs):
    refs = list(refs)
    info, wide = take(refs, 2)
    if n_notes:
        notes, terms_in = take(refs, n_notes), []
        change, rays, w_scr, rays_scr = refs
        gather_rays(info, notes, rays, rays_scr)
    else:
        (rays,) = take(refs, 1)
        terms_in = take(refs, n_terms)
        change, w_scr = refs

    @pl.when(on_core(info, place, core))
    def _():
        weights(rays, terms_in, w_scr)
        change[...] = jnp.zeros_like(change)
        back_project(info, wide, w_scr, change)


def first_kernel(place, *refs):
    refs = list(refs)
    info, tall, change = take(refs, 3)
    image_in = take(refs, 1)[0] if place > 0 else None
    shot, terms = refs

    @pl.when(on_core(info, place, 0))
    def _():
        value = change[...]
        if image_in is not None:
            value = value + image_in[...].astype(jnp.float32)
        shot[...] = value.astype(jnp.bfloat16)
        project(info, tall, shot, terms)


def second_kernel(place, last, *refs):
    refs = list(refs)
    info, change, image_in, shot = take(refs, 4)
    held = take(refs, 1) if place > 0 else []
    image = None if last else take(refs, 1)[0]
    (out,) = refs
    batches, per_batch, _ = out.shape

    def value(c):
        return change[c] + image_in[c].astype(jnp.float32)

    def write(source):
        for c in range(CB):
            if last:
                block = source(c).reshape(batches, per_batch, BS)
                out[:, :, c * BS : (c + 1) * BS] = block.astype(jnp.bfloat16)
            else:
                out[c] = source(c).astype(jnp.bfloat16)

    @pl.when(on_core(info, place, 1))
    def _():
        write(value)
        if not last:
            image[...] = out[...]

    @pl.when(on_core(info, place, 0))
    def _():
        write(lambda c: shot[c].astype(jnp.float32))

    if held:

        @pl.when(info[0, 0] != place)
        def _():
            write(lambda c: held[0][c].astype(jnp.float32))


def per_device(blocks, block_rows, block_cols, sinogram):
    batches, per_batch, here = sinogram.shape
    slices = batches * per_batch
    quarter = here // BS
    count = blocks.shape[2]
    subsets = lax.axis_size("subset")
    tiles = lax.axis_size("tile")
    row_blocks = quarter * tiles
    each = count // row_blocks
    places = subsets // 2
    direct = tiles <= DIRECT
    subset = lax.axis_index("subset")
    pos = jnp.stack([subset // 2, subset % 2, lax.axis_index("tile")]).astype(jnp.int32)

    image_shape = (CB, slices, BS)
    image_out = jax.ShapeDtypeStruct(image_shape, jnp.bfloat16)
    terms_out = jax.ShapeDtypeStruct((row_blocks, slices, BS), jnp.bfloat16)
    rays_out = jax.ShapeDtypeStruct((row_blocks + 1, slices, BS), jnp.float32)
    final_out = jax.ShapeDtypeStruct((batches, per_batch, PIX), jnp.bfloat16)
    w_scr = pltpu.VMEM((row_blocks, slices, BS), jnp.bfloat16)
    x_scr = pltpu.VMEM(image_shape, jnp.float32)
    rays_scr = pltpu.VMEM((tiles, quarter, slices, BS), jnp.float32)

    def sent(value, target):
        pairs = []
        for p in range(places):
            for c in range(2):
                for t in range(tiles):
                    q, e, u = target(p, c, t)
                    pairs.append(((2 * p + c) * tiles + t, (2 * q + e) * tiles + u))
        return lax.ppermute(value, ("subset", "tile"), pairs)

    def swapped(value):
        return sent(value, lambda p, c, t: (p, 1 - c, t))

    def spread(value):
        if direct:
            far = range(1, tiles)
            return [value] + [sent(value, lambda p, c, t: (p, c, t ^ d)) for d in far]
        return [lax.all_gather(value, "tile")]

    def passed(terms, core):
        if not direct:
            return [swapped(lax.psum(terms, "tile"))]
        return [
            sent(terms, lambda p, c, t: (p, 1 - c, t ^ d if c == core else t))
            for d in range(tiles)
        ]

    def call(kernel, smem, operands, out_shape, scratch, name, flops=0):
        many = isinstance(out_shape, tuple)
        return pl.pallas_call(
            kernel,
            out_shape=out_shape,
            in_specs=[SMEM] * smem + [VMEM] * (len(operands) - smem),
            out_specs=(VMEM,) * len(out_shape) if many else VMEM,
            scratch_shapes=scratch,
            compiler_params=PARAMS,
            cost_estimate=pl.CostEstimate(
                flops=flops, bytes_accessed=0, transcendentals=0
            ),
            name=name,
        )(*operands)

    blocks2 = swapped(blocks)
    chunks = 8 if count % 8 == 0 else 1
    note, table, own, blocks = pl.pallas_call(
        functools.partial(head_kernel, row_blocks, chunks),
        out_shape=(
            jax.ShapeDtypeStruct((quarter + 1, slices, BS), jnp.bfloat16),
            jax.ShapeDtypeStruct((2, count), jnp.int32),
            pltpu.SMEM((3, count), jnp.int32),
            pltpu.VMEM(blocks.shape, blocks.dtype),
        ),
        in_specs=[SMEM] + [pl.BlockSpec(memory_space=pltpu.HBM)] * 4,
        out_specs=(VMEM, SMEM, SMEM, VMEM),
        scratch_shapes=[
            pltpu.SMEM(block_rows.shape, jnp.int32),
            pltpu.SMEM(block_cols.shape, jnp.int32),
            pltpu.VMEM(sinogram.shape, jnp.float32),
            pltpu.SMEM((row_blocks,), jnp.int32),
            pltpu.VMEM((row_blocks, BS, BS), jnp.float32),
            pltpu.VMEM((row_blocks, BS), jnp.float32),
            pltpu.SemaphoreType.DMA((3 + chunks,)),
        ],
        compiler_params=PARAMS,
        name="head",
    )(
        pos,
        *(
            pltpu.with_memory_space_constraint(value, pltpu.HBM)
            for value in (block_rows, block_cols, blocks, sinogram)
        ),
    )
    notes = spread(note)
    table2 = swapped(table)

    own = pltpu.with_memory_space_constraint(own, pltpu.SMEM)
    blocks2 = pltpu.with_memory_space_constraint(blocks2, pltpu.VMEM)
    wide = pl.pallas_call(
        pack_own_kernel,
        out_shape=pltpu.VMEM((row_blocks, BS, each * BS), jnp.bfloat16),
        in_specs=[SMEM, VMEM, pl.BlockSpec(memory_space=pl.ANY)],
        out_specs=VMEM,
        compiler_params=PARAMS,
        name="pack_own",
    )(own, blocks, note)
    info, tall = pl.pallas_call(
        pack_other_kernel,
        out_shape=(
            pltpu.SMEM((3, count), jnp.int32),
            pltpu.VMEM((row_blocks, each * BS, BS), jnp.bfloat16),
        ),
        in_specs=[SMEM, SMEM, VMEM],
        out_specs=(SMEM, VMEM),
        compiler_params=PARAMS,
        name="pack_other",
    )(own, table2, blocks2)
    info = pltpu.with_memory_space_constraint(info, pltpu.SMEM)

    held = []
    image, rays = None, None
    change_out = jax.ShapeDtypeStruct(image_shape, jnp.float32)

    def updated(place, core, terms):
        return call(
            functools.partial(update_kernel, place, core, 0, len(terms)),
            1,
            [info, wide, rays] + terms,
            change_out,
            [w_scr],
            "update",
            UPDATE_FLOPS,
        )

    for place in range(places):
        last = place == places - 1
        if place == 0:
            change, rays = call(
                functools.partial(update_kernel, place, 0, len(notes), 0),
                1,
                [info, wide] + notes,
                (change_out, rays_out),
                [w_scr, rays_scr],
                "update",
                UPDATE_FLOPS,
            )
            before = []
        else:
            def hop(p, c, t):
                if c == 1 and p in (place - 1, place):
                    return 2 * place - 1 - p, c, t
                return p, c, t ^ 1

            image = sent(image, hop)
            terms = call(
                functools.partial(project_kernel, place),
                1,
                [info, image, tall],
                terms_out,
                [],
                "project",
            )
            change = updated(place, 0, passed(terms, 1))
            before = [swapped(image)]
        shot, terms = call(
            functools.partial(first_kernel, place),
            1,
            [info, tall, change] + before,
            (image_out, terms_out),
            [],
            "first",
        )
        change = updated(place, 1, passed(terms, 0))
        outs = call(
            functools.partial(second_kernel, place, last),
            1,
            [info, change, swapped(shot), shot] + held,
            final_out if last else (image_out, image_out),
            [],
            "second",
        )
        if last:
            return outs[None]
        image = outs[0]
        held = [outs[1]]


def solution(mesh):
    in_specs = (
        P("subset", "tile", None, None, None),
        P("subset", "tile", None),
        P("subset", "tile", None),
        P(None, None, ("subset", "tile")),
    )
    out_specs = P("subset", None, None, "tile")
    return jax.shard_map(
        per_device, mesh=mesh, in_specs=in_specs, out_specs=out_specs, check_vma=False
    )
```

```python
import functools

import jax
import jax.numpy as jnp
from jax import lax
from jax.experimental import pallas as pl
from jax.experimental.pallas import tpu as pltpu
from jax.sharding import PartitionSpec as P

BS = 128
PIX = 4096
CB = PIX // BS
relaxation = 0.5

UPDATE_FLOPS = 10**10

DIRECT = 4

NN = (((1,), (0,)), ((), ()))
NT = (((1,), (1,)), ((), ()))
VMEM = pl.BlockSpec(memory_space=pltpu.VMEM)
SMEM = pl.BlockSpec(memory_space=pltpu.SMEM)
PARAMS = pltpu.CompilerParams(vmem_limit_bytes=20 * 2**20)


def dot(lhs, rhs, dims):
    return lax.dot_general(lhs, rhs, dims, preferred_element_type=jnp.float32)


def head_kernel(row_blocks, chunks, pos, rows_in, cols_in, blocks_in, rays_in, *refs):
    note, table, own, blocks, rows, cols, rays, seen, squares, norms, sems = refs
    count = blocks.shape[2]
    each = count // row_blocks
    per_chunk = count // chunks
    batches, per_batch, here = rays.shape
    quarter = here // BS
    small = [
        pltpu.make_async_copy(src, dst, sems.at[i])
        for i, (src, dst) in enumerate(((rows_in, rows), (cols_in, cols), (rays_in, rays)))
    ]
    large = []
    for k in range(chunks):
        where = pl.ds(k * per_chunk, per_chunk)
        large.append(
            pltpu.make_async_copy(
                blocks_in.at[0, 0, where], blocks.at[0, 0, where], sems.at[3 + k]
            )
        )
    for copy in small + large:
        copy.start()
    squares[...] = jnp.zeros_like(squares)
    for copy in small:
        copy.wait()
    for i in range(3):
        own[0, i] = pos[i]
    for r in range(row_blocks):
        seen[r] = r * each
    for i in range(quarter):
        parts = [rays[g, :, i * BS : (i + 1) * BS] for g in range(batches)]
        note[i] = jnp.concatenate(parts, axis=0).astype(jnp.bfloat16)
    for k in range(chunks):
        large[k].wait()
        for n in range(k * per_chunk, (k + 1) * per_chunk):
            block = blocks[0, 0, n].astype(jnp.float32)
            row = rows[0, 0, n]
            squares[row] = squares[row] + block * block
            at = seen[row]
            seen[row] = at + 1
            col = cols[0, 0, n]
            for out, first in ((table, 0), (own, 1)):
                out[first, at] = n
                out[first + 1, at] = col
    ones = jnp.ones((BS, BS), jnp.bfloat16)
    on_diagonal = lax.broadcasted_iota(jnp.int32, (BS, BS), 0) == lax.broadcasted_iota(
        jnp.int32, (BS, BS), 1
    )
    for r in range(row_blocks):
        left = squares[r]
        coarse = left.astype(jnp.bfloat16)
        fine = (left - coarse.astype(jnp.float32)).astype(jnp.bfloat16)
        total = dot(coarse, ones, NN) + dot(fine, ones, NN)
        total = jnp.sum(jnp.where(on_diagonal, total, 0.0), axis=0, keepdims=True)
        norms[r : r + 1] = total
    coarse = norms[...].astype(jnp.bfloat16)
    fine = (norms[...] - coarse.astype(jnp.float32)).astype(jnp.bfloat16)
    parts = [coarse, fine]
    pad = note.shape[1] - 2 * row_blocks
    if pad:
        parts.append(jnp.zeros((pad, BS), jnp.bfloat16))
    note[quarter] = jnp.concatenate(parts, axis=0)


def pack_own_kernel(own, blocks, _, wide):
    row_blocks = wide.shape[0]
    each = wide.shape[2] // BS
    for r in range(row_blocks):
        for j in range(each):
            block = blocks[0, 0, own[1, r * each + j]]
            wide[r, :, j * BS : (j + 1) * BS] = block


def pack_other_kernel(own, table2, blocks2, info, tall):
    row_blocks = tall.shape[0]
    each = tall.shape[1] // BS
    for i in range(3):
        info[0, i] = own[0, i]
    for r in range(row_blocks):
        for j in range(each):
            k = r * each + j
            info[1, k] = own[2, k]
            info[2, k] = table2[1, k]
            block = blocks2[0, 0, table2[0, k]]
            tall[r, j * BS : (j + 1) * BS] = block.T


def gather_rays(info, notes, rays, rays_scr):
    tiles, quarter, _, _ = rays_scr.shape
    row_blocks = tiles * quarter
    if len(notes) > 1:
        parts = [ref[quarter] for ref in notes]
        for i, ref in enumerate(notes):
            rays_scr[info[0, 2] ^ i] = ref[0:quarter].astype(jnp.float32)
    else:
        parts = [notes[0][t, quarter] for t in range(tiles)]
        rays_scr[...] = notes[0][:, 0:quarter].astype(jnp.float32)
    norms = sum(part.astype(jnp.float32) for part in parts)
    scale = relaxation / (norms[0:row_blocks] + norms[row_blocks : 2 * row_blocks])
    for r in range(row_blocks):
        row = scale[r : r + 1]
        rays[r] = rays_scr[r // quarter, r % quarter] * row
        rays[row_blocks, r : r + 1] = row


def weights(rays, terms, w_scr):
    row_blocks = w_scr.shape[0]
    for r in range(row_blocks):
        left = rays[r]
        if terms:
            total = sum(ref[r].astype(jnp.float32) for ref in terms)
            left = left - total * rays[row_blocks, r : r + 1]
        w_scr[r] = left.astype(jnp.bfloat16)


def back_project(info, wide, w_scr, image):
    row_blocks = wide.shape[0]
    each = wide.shape[2] // BS
    for r in range(row_blocks):
        back = dot(w_scr[r], wide[r], NN)
        for j in range(each):
            col = info[1, r * each + j]
            image[col] = image[col] + back[:, j * BS : (j + 1) * BS]


def project(info, tall, image, terms):
    row_blocks = tall.shape[0]
    each = tall.shape[1] // BS
    for r in range(row_blocks):
        parts = [image[info[2, r * each + j]] for j in range(each)]
        total = dot(jnp.concatenate(parts, axis=1), tall[r], NN)
        terms[r] = total.astype(jnp.bfloat16)


def take(refs, n):
    taken = refs[:n]
    del refs[:n]
    return taken


def on_core(info, place, core):
    return jnp.logical_and(info[0, 0] == place, info[0, 1] == core)


def project_kernel(place, info, image, tall, terms):
    @pl.when(on_core(info, place, 1))
    def _():
        project(info, tall, image, terms)


def update_kernel(place, core, n_notes, n_terms, *refs):
    refs = list(refs)
    info, wide = take(refs, 2)
    if n_notes:
        notes, terms_in = take(refs, n_notes), []
        change, rays, w_scr, rays_scr = refs
        gather_rays(info, notes, rays, rays_scr)
    else:
        (rays,) = take(refs, 1)
        terms_in = take(refs, n_terms)
        change, w_scr = refs

    @pl.when(on_core(info, place, core))
    def _():
        weights(rays, terms_in, w_scr)
        change[...] = jnp.zeros_like(change)
        back_project(info, wide, w_scr, change)


def first_kernel(place, *refs):
    refs = list(refs)
    info, tall, change = take(refs, 3)
    image_in = take(refs, 1)[0] if place > 0 else None
    shot, terms = refs

    @pl.when(on_core(info, place, 0))
    def _():
        value = change[...]
        if image_in is not None:
            value = value + image_in[...].astype(jnp.float32)
        shot[...] = value.astype(jnp.bfloat16)
        project(info, tall, shot, terms)


def second_kernel(place, last, *refs):
    refs = list(refs)
    info, change, image_in, shot = take(refs, 4)
    held = take(refs, 1) if place > 0 else []
    image = None if last else take(refs, 1)[0]
    (out,) = refs
    batches, per_batch, _ = out.shape

    def value(c):
        return change[c] + image_in[c].astype(jnp.float32)

    def write(source):
        for c in range(CB):
            if last:
                block = source(c).reshape(batches, per_batch, BS)
                out[:, :, c * BS : (c + 1) * BS] = block.astype(jnp.bfloat16)
            else:
                out[c] = source(c).astype(jnp.bfloat16)

    @pl.when(on_core(info, place, 1))
    def _():
        write(value)
        if not last:
            image[...] = out[...]

    @pl.when(on_core(info, place, 0))
    def _():
        write(lambda c: shot[c].astype(jnp.float32))

    if held:

        @pl.when(info[0, 0] != place)
        def _():
            write(lambda c: held[0][c].astype(jnp.float32))


def per_device(blocks, block_rows, block_cols, sinogram):
    batches, per_batch, here = sinogram.shape
    slices = batches * per_batch
    quarter = here // BS
    count = blocks.shape[2]
    subsets = lax.axis_size("subset")
    tiles = lax.axis_size("tile")
    row_blocks = quarter * tiles
    each = count // row_blocks
    places = subsets // 2
    direct = tiles <= DIRECT
    subset = lax.axis_index("subset")
    pos = jnp.stack([subset // 2, subset % 2, lax.axis_index("tile")]).astype(jnp.int32)

    image_shape = (CB, slices, BS)
    image_out = jax.ShapeDtypeStruct(image_shape, jnp.bfloat16)
    terms_out = jax.ShapeDtypeStruct((row_blocks, slices, BS), jnp.bfloat16)
    rays_out = jax.ShapeDtypeStruct((row_blocks + 1, slices, BS), jnp.float32)
    final_out = jax.ShapeDtypeStruct((batches, per_batch, PIX), jnp.bfloat16)
    w_scr = pltpu.VMEM((row_blocks, slices, BS), jnp.bfloat16)
    x_scr = pltpu.VMEM(image_shape, jnp.float32)
    rays_scr = pltpu.VMEM((tiles, quarter, slices, BS), jnp.float32)

    def sent(value, target):
        pairs = []
        for p in range(places):
            for c in range(2):
                for t in range(tiles):
                    q, e, u = target(p, c, t)
                    pairs.append(((2 * p + c) * tiles + t, (2 * q + e) * tiles + u))
        return lax.ppermute(value, ("subset", "tile"), pairs)

    def swapped(value):
        return sent(value, lambda p, c, t: (p, 1 - c, t))

    def spread(value):
        if direct:
            far = range(1, tiles)
            return [value] + [sent(value, lambda p, c, t: (p, c, t ^ d)) for d in far]
        return [lax.all_gather(value, "tile")]

    def passed(terms, core):
        if not direct:
            return [swapped(lax.psum(terms, "tile"))]
        return [
            sent(terms, lambda p, c, t: (p, 1 - c, t ^ d if c == core else t))
            for d in range(tiles)
        ]

    def call(kernel, smem, operands, out_shape, scratch, name, flops=0):
        many = isinstance(out_shape, tuple)
        return pl.pallas_call(
            kernel,
            out_shape=out_shape,
            in_specs=[SMEM] * smem + [VMEM] * (len(operands) - smem),
            out_specs=(VMEM,) * len(out_shape) if many else VMEM,
            scratch_shapes=scratch,
            compiler_params=PARAMS,
            cost_estimate=pl.CostEstimate(
                flops=flops, bytes_accessed=0, transcendentals=0
            ),
            name=name,
        )(*operands)

    blocks2 = swapped(blocks)
    chunks = 8 if count % 8 == 0 else 1
    note, table, own, blocks = pl.pallas_call(
        functools.partial(head_kernel, row_blocks, chunks),
        out_shape=(
            jax.ShapeDtypeStruct((quarter + 1, slices, BS), jnp.bfloat16),
            jax.ShapeDtypeStruct((2, count), jnp.int32),
            pltpu.SMEM((3, count), jnp.int32),
            pltpu.VMEM(blocks.shape, blocks.dtype),
        ),
        in_specs=[SMEM] + [pl.BlockSpec(memory_space=pltpu.HBM)] * 4,
        out_specs=(VMEM, SMEM, SMEM, VMEM),
        scratch_shapes=[
            pltpu.SMEM(block_rows.shape, jnp.int32),
            pltpu.SMEM(block_cols.shape, jnp.int32),
            pltpu.VMEM(sinogram.shape, jnp.float32),
            pltpu.SMEM((row_blocks,), jnp.int32),
            pltpu.VMEM((row_blocks, BS, BS), jnp.float32),
            pltpu.VMEM((row_blocks, BS), jnp.float32),
            pltpu.SemaphoreType.DMA((3 + chunks,)),
        ],
        compiler_params=PARAMS,
        name="head",
    )(
        pos,
        *(
            pltpu.with_memory_space_constraint(value, pltpu.HBM)
            for value in (block_rows, block_cols, blocks, sinogram)
        ),
    )
    notes = spread(note)
    table2 = swapped(table)

    own = pltpu.with_memory_space_constraint(own, pltpu.SMEM)
    blocks2 = pltpu.with_memory_space_constraint(blocks2, pltpu.VMEM)
    wide = pl.pallas_call(
        pack_own_kernel,
        out_shape=pltpu.VMEM((row_blocks, BS, each * BS), jnp.bfloat16),
        in_specs=[SMEM, VMEM, pl.BlockSpec(memory_space=pl.ANY)],
        out_specs=VMEM,
        compiler_params=PARAMS,
        name="pack_own",
    )(own, blocks, note)
    info, tall = pl.pallas_call(
        pack_other_kernel,
        out_shape=(
            pltpu.SMEM((3, count), jnp.int32),
            pltpu.VMEM((row_blocks, each * BS, BS), jnp.bfloat16),
        ),
        in_specs=[SMEM, SMEM, VMEM],
        out_specs=(SMEM, VMEM),
        compiler_params=PARAMS,
        name="pack_other",
    )(own, table2, blocks2)
    info = pltpu.with_memory_space_constraint(info, pltpu.SMEM)

    held = []
    image, rays = None, None
    change_out = jax.ShapeDtypeStruct(image_shape, jnp.float32)

    def updated(place, core, terms):
        return call(
            functools.partial(update_kernel, place, core, 0, len(terms)),
            1,
            [info, wide, rays] + terms,
            change_out,
            [w_scr],
            "update",
            UPDATE_FLOPS,
        )

    for place in range(places):
        last = place == places - 1
        if place == 0:
            change, rays = call(
                functools.partial(update_kernel, place, 0, len(notes), 0),
                1,
                [info, wide] + notes,
                (change_out, rays_out),
                [w_scr, rays_scr],
                "update",
                UPDATE_FLOPS,
            )
            before = []
        else:
            def hop(p, c, t):
                if p == place - 1:
                    return (place, 1, t) if c else (p, 1, t)
                if p == place:
                    return (p, 0, t) if c else (place - 1, 0, t)
                return p, 1 - c, t

            image = sent(image, hop)
            terms = call(
                functools.partial(project_kernel, place),
                1,
                [info, image, tall],
                terms_out,
                [],
                "project",
            )
            change = updated(place, 0, passed(terms, 1))
            before = [swapped(image)]
        shot, terms = call(
            functools.partial(first_kernel, place),
            1,
            [info, tall, change] + before,
            (image_out, terms_out),
            [],
            "first",
        )
        change = updated(place, 1, passed(terms, 0))
        outs = call(
            functools.partial(second_kernel, place, last),
            1,
            [info, change, swapped(shot), shot] + held,
            final_out if last else (image_out, image_out),
            [],
            "second",
        )
        if last:
            return outs[None]
        image = outs[0]
        held = [outs[1]]


def solution(mesh):
    in_specs = (
        P("subset", "tile", None, None, None),
        P("subset", "tile", None),
        P("subset", "tile", None),
        P(None, None, ("subset", "tile")),
    )
    out_specs = P("subset", None, None, "tile")
    return jax.shard_map(
        per_device, mesh=mesh, in_specs=in_specs, out_specs=out_specs, check_vma=False
    )
```

```python
import functools

import jax
import jax.numpy as jnp
from jax import lax
from jax.experimental import pallas as pl
from jax.experimental.pallas import tpu as pltpu
from jax.sharding import PartitionSpec as P

BS = 128
PIX = 4096
CB = PIX // BS
relaxation = 0.5

UPDATE_FLOPS = 10**10

DIRECT = 4

NN = (((1,), (0,)), ((), ()))
NT = (((1,), (1,)), ((), ()))
VMEM = pl.BlockSpec(memory_space=pltpu.VMEM)
SMEM = pl.BlockSpec(memory_space=pltpu.SMEM)
PARAMS = pltpu.CompilerParams(vmem_limit_bytes=20 * 2**20)


def dot(lhs, rhs, dims):
    return lax.dot_general(lhs, rhs, dims, preferred_element_type=jnp.float32)


def head_kernel(row_blocks, chunks, pos, rows_in, cols_in, blocks_in, rays_in, *refs):
    note, table, own, blocks, rows, cols, rays, seen, squares, norms, sems = refs
    count = blocks.shape[2]
    each = count // row_blocks
    per_chunk = count // chunks
    batches, per_batch, here = rays.shape
    quarter = here // BS
    small = [
        pltpu.make_async_copy(src, dst, sems.at[i])
        for i, (src, dst) in enumerate(((rows_in, rows), (cols_in, cols), (rays_in, rays)))
    ]
    large = []
    for k in range(chunks):
        where = pl.ds(k * per_chunk, per_chunk)
        large.append(
            pltpu.make_async_copy(
                blocks_in.at[0, 0, where], blocks.at[0, 0, where], sems.at[3 + k]
            )
        )
    for copy in small + large:
        copy.start()
    squares[...] = jnp.zeros_like(squares)
    for copy in small:
        copy.wait()
    for i in range(3):
        own[0, i] = pos[i]
    for r in range(row_blocks):
        seen[r] = r * each
    for i in range(quarter):
        parts = [rays[g, :, i * BS : (i + 1) * BS] for g in range(batches)]
        note[i] = jnp.concatenate(parts, axis=0).astype(jnp.bfloat16)
    for k in range(chunks):
        large[k].wait()
        for n in range(k * per_chunk, (k + 1) * per_chunk):
            block = blocks[0, 0, n].astype(jnp.float32)
            row = rows[0, 0, n]
            squares[row] = squares[row] + block * block
            at = seen[row]
            seen[row] = at + 1
            col = cols[0, 0, n]
            for out, first in ((table, 0), (own, 1)):
                out[first, at] = n
                out[first + 1, at] = col
    ones = jnp.ones((BS, BS), jnp.bfloat16)
    on_diagonal = lax.broadcasted_iota(jnp.int32, (BS, BS), 0) == lax.broadcasted_iota(
        jnp.int32, (BS, BS), 1
    )
    for r in range(row_blocks):
        left = squares[r]
        coarse = left.astype(jnp.bfloat16)
        fine = (left - coarse.astype(jnp.float32)).astype(jnp.bfloat16)
        total = dot(coarse, ones, NN) + dot(fine, ones, NN)
        total = jnp.sum(jnp.where(on_diagonal, total, 0.0), axis=0, keepdims=True)
        norms[r : r + 1] = total
    coarse = norms[...].astype(jnp.bfloat16)
    fine = (norms[...] - coarse.astype(jnp.float32)).astype(jnp.bfloat16)
    parts = [coarse, fine]
    pad = note.shape[1] - 2 * row_blocks
    if pad:
        parts.append(jnp.zeros((pad, BS), jnp.bfloat16))
    note[quarter] = jnp.concatenate(parts, axis=0)


def pack_own_kernel(own, blocks, _, wide):
    row_blocks = wide.shape[0]
    each = wide.shape[2] // BS
    for r in range(row_blocks):
        for j in range(each):
            block = blocks[0, 0, own[1, r * each + j]]
            wide[r, :, j * BS : (j + 1) * BS] = block


def pack_other_kernel(own, table2, blocks2, info, tall):
    row_blocks = tall.shape[0]
    each = tall.shape[1] // BS
    for i in range(3):
        info[0, i] = own[0, i]
    for r in range(row_blocks):
        for j in range(each):
            k = r * each + j
            info[1, k] = own[2, k]
            info[2, k] = table2[1, k]
            block = blocks2[0, 0, table2[0, k]]
            tall[r, j * BS : (j + 1) * BS] = block.T


def gather_rays(info, notes, rays, rays_scr):
    tiles, quarter, _, _ = rays_scr.shape
    row_blocks = tiles * quarter
    if len(notes) > 1:
        parts = [ref[quarter] for ref in notes]
        for i, ref in enumerate(notes):
            rays_scr[info[0, 2] ^ i] = ref[0:quarter].astype(jnp.float32)
    else:
        parts = [notes[0][t, quarter] for t in range(tiles)]
        rays_scr[...] = notes[0][:, 0:quarter].astype(jnp.float32)
    norms = sum(part.astype(jnp.float32) for part in parts)
    scale = relaxation / (norms[0:row_blocks] + norms[row_blocks : 2 * row_blocks])
    for r in range(row_blocks):
        row = scale[r : r + 1]
        rays[r] = rays_scr[r // quarter, r % quarter] * row
        rays[row_blocks, r : r + 1] = row


def weights(rays, terms, w_scr):
    row_blocks = w_scr.shape[0]
    for r in range(row_blocks):
        left = rays[r]
        if terms:
            total = sum(ref[r].astype(jnp.float32) for ref in terms)
            left = left - total * rays[row_blocks, r : r + 1]
        w_scr[r] = left.astype(jnp.bfloat16)


def back_project(info, wide, w_scr, image):
    row_blocks = wide.shape[0]
    each = wide.shape[2] // BS
    for r in range(row_blocks):
        back = dot(w_scr[r], wide[r], NN)
        for j in range(each):
            col = info[1, r * each + j]
            image[col] = image[col] + back[:, j * BS : (j + 1) * BS]


def project(info, tall, image, terms):
    row_blocks = tall.shape[0]
    each = tall.shape[1] // BS
    for r in range(row_blocks):
        parts = [image[info[2, r * each + j]] for j in range(each)]
        total = dot(jnp.concatenate(parts, axis=1), tall[r], NN)
        terms[r] = total.astype(jnp.bfloat16)


def take(refs, n):
    taken = refs[:n]
    del refs[:n]
    return taken


def on_core(info, place, core):
    return jnp.logical_and(info[0, 0] == place, info[0, 1] == core)


def project_kernel(place, info, image, tall, terms):
    @pl.when(on_core(info, place, 1))
    def _():
        project(info, tall, image, terms)


def update_kernel(place, core, n_notes, n_terms, *refs):
    refs = list(refs)
    info, wide = take(refs, 2)
    if n_notes:
        notes, terms_in = take(refs, n_notes), []
        change, rays, w_scr, rays_scr = refs
        gather_rays(info, notes, rays, rays_scr)
    else:
        (rays,) = take(refs, 1)
        terms_in = take(refs, n_terms)
        change, w_scr = refs

    @pl.when(on_core(info, place, core))
    def _():
        weights(rays, terms_in, w_scr)
        change[...] = jnp.zeros_like(change)
        back_project(info, wide, w_scr, change)


def first_kernel(place, *refs):
    refs = list(refs)
    info, tall, change = take(refs, 3)
    image_in = take(refs, 1)[0] if place > 0 else None
    shot, terms = refs

    @pl.when(on_core(info, place, 0))
    def _():
        value = change[...]
        if image_in is not None:
            value = value + image_in[...].astype(jnp.float32)
        shot[...] = value.astype(jnp.bfloat16)
        project(info, tall, shot, terms)


def second_kernel(place, last, *refs):
    refs = list(refs)
    info, change, image_in, shot = take(refs, 4)
    held = take(refs, 1) if place > 0 else []
    image = None if last else take(refs, 1)[0]
    (out,) = refs
    batches, per_batch, _ = out.shape

    def value(c):
        return change[c] + image_in[c].astype(jnp.float32)

    def write(source):
        for c in range(CB):
            if last:
                block = source(c).reshape(batches, per_batch, BS)
                out[:, :, c * BS : (c + 1) * BS] = block.astype(jnp.bfloat16)
            else:
                out[c] = source(c).astype(jnp.bfloat16)

    @pl.when(on_core(info, place, 1))
    def _():
        write(value)
        if not last:
            image[...] = out[...]

    @pl.when(on_core(info, place, 0))
    def _():
        write(lambda c: shot[c].astype(jnp.float32))

    if held:

        @pl.when(info[0, 0] != place)
        def _():
            write(lambda c: held[0][c].astype(jnp.float32))


def per_device(blocks, block_rows, block_cols, sinogram):
    batches, per_batch, here = sinogram.shape
    slices = batches * per_batch
    quarter = here // BS
    count = blocks.shape[2]
    subsets = lax.axis_size("subset")
    tiles = lax.axis_size("tile")
    row_blocks = quarter * tiles
    each = count // row_blocks
    places = subsets // 2
    direct = tiles <= DIRECT
    subset = lax.axis_index("subset")
    pos = jnp.stack([subset // 2, subset % 2, lax.axis_index("tile")]).astype(jnp.int32)

    image_shape = (CB, slices, BS)
    image_out = jax.ShapeDtypeStruct(image_shape, jnp.bfloat16)
    terms_out = jax.ShapeDtypeStruct((row_blocks, slices, BS), jnp.bfloat16)
    rays_out = jax.ShapeDtypeStruct((row_blocks + 1, slices, BS), jnp.float32)
    final_out = jax.ShapeDtypeStruct((batches, per_batch, PIX), jnp.bfloat16)
    w_scr = pltpu.VMEM((row_blocks, slices, BS), jnp.bfloat16)
    x_scr = pltpu.VMEM(image_shape, jnp.float32)
    rays_scr = pltpu.VMEM((tiles, quarter, slices, BS), jnp.float32)

    def sent(value, target):
        pairs = []
        for p in range(places):
            for c in range(2):
                for t in range(tiles):
                    q, e, u = target(p, c, t)
                    pairs.append(((2 * p + c) * tiles + t, (2 * q + e) * tiles + u))
        return lax.ppermute(value, ("subset", "tile"), pairs)

    def swapped(value):
        return sent(value, lambda p, c, t: (p, 1 - c, t))

    def spread(value):
        if direct:
            far = range(1, tiles)
            return [value] + [sent(value, lambda p, c, t: (p, c, t ^ d)) for d in far]
        return [lax.all_gather(value, "tile")]

    def passed(terms, core, place):
        if not direct:
            return [swapped(lax.psum(terms, "tile"))]
        if core == 1:
            ahead = place + 1 if place + 1 < places else place - 2
        else:
            ahead = place + 2 if place + 2 < places else 0
        helped = place > 0 and ahead >= 0 and ahead != place

        def way(d):
            def target(p, c, t):
                if helped and d == tiles - 1 and p in (place, ahead):
                    if c != core:
                        return (ahead, c, t) if p == place else (place, core, t)
                    return (p, 1 - c, t ^ d) if p == place else (p, c, t ^ 1)
                return p, 1 - c, t ^ d if c == core else t

            return target

        return [sent(terms, way(d)) for d in range(tiles)]

    def call(kernel, smem, operands, out_shape, scratch, name, flops=0):
        many = isinstance(out_shape, tuple)
        return pl.pallas_call(
            kernel,
            out_shape=out_shape,
            in_specs=[SMEM] * smem + [VMEM] * (len(operands) - smem),
            out_specs=(VMEM,) * len(out_shape) if many else VMEM,
            scratch_shapes=scratch,
            compiler_params=PARAMS,
            cost_estimate=pl.CostEstimate(
                flops=flops, bytes_accessed=0, transcendentals=0
            ),
            name=name,
        )(*operands)

    blocks2 = swapped(blocks)
    chunks = 8 if count % 8 == 0 else 1
    note, table, own, blocks = pl.pallas_call(
        functools.partial(head_kernel, row_blocks, chunks),
        out_shape=(
            jax.ShapeDtypeStruct((quarter + 1, slices, BS), jnp.bfloat16),
            jax.ShapeDtypeStruct((2, count), jnp.int32),
            pltpu.SMEM((3, count), jnp.int32),
            pltpu.VMEM(blocks.shape, blocks.dtype),
        ),
        in_specs=[SMEM] + [pl.BlockSpec(memory_space=pltpu.HBM)] * 4,
        out_specs=(VMEM, SMEM, SMEM, VMEM),
        scratch_shapes=[
            pltpu.SMEM(block_rows.shape, jnp.int32),
            pltpu.SMEM(block_cols.shape, jnp.int32),
            pltpu.VMEM(sinogram.shape, jnp.float32),
            pltpu.SMEM((row_blocks,), jnp.int32),
            pltpu.VMEM((row_blocks, BS, BS), jnp.float32),
            pltpu.VMEM((row_blocks, BS), jnp.float32),
            pltpu.SemaphoreType.DMA((3 + chunks,)),
        ],
        compiler_params=PARAMS,
        name="head",
    )(
        pos,
        *(
            pltpu.with_memory_space_constraint(value, pltpu.HBM)
            for value in (block_rows, block_cols, blocks, sinogram)
        ),
    )
    notes = spread(note)
    table2 = swapped(table)

    own = pltpu.with_memory_space_constraint(own, pltpu.SMEM)
    blocks2 = pltpu.with_memory_space_constraint(blocks2, pltpu.VMEM)
    wide = pl.pallas_call(
        pack_own_kernel,
        out_shape=pltpu.VMEM((row_blocks, BS, each * BS), jnp.bfloat16),
        in_specs=[SMEM, VMEM, pl.BlockSpec(memory_space=pl.ANY)],
        out_specs=VMEM,
        compiler_params=PARAMS,
        name="pack_own",
    )(own, blocks, note)
    info, tall = pl.pallas_call(
        pack_other_kernel,
        out_shape=(
            pltpu.SMEM((3, count), jnp.int32),
            pltpu.VMEM((row_blocks, each * BS, BS), jnp.bfloat16),
        ),
        in_specs=[SMEM, SMEM, VMEM],
        out_specs=(SMEM, VMEM),
        compiler_params=PARAMS,
        name="pack_other",
    )(own, table2, blocks2)
    info = pltpu.with_memory_space_constraint(info, pltpu.SMEM)

    held = []
    image, rays = None, None
    change_out = jax.ShapeDtypeStruct(image_shape, jnp.float32)

    def updated(place, core, terms):
        return call(
            functools.partial(update_kernel, place, core, 0, len(terms)),
            1,
            [info, wide, rays] + terms,
            change_out,
            [w_scr],
            "update",
            UPDATE_FLOPS,
        )

    for place in range(places):
        last = place == places - 1
        if place == 0:
            change, rays = call(
                functools.partial(update_kernel, place, 0, len(notes), 0),
                1,
                [info, wide] + notes,
                (change_out, rays_out),
                [w_scr, rays_scr],
                "update",
                UPDATE_FLOPS,
            )
            before = []
        else:
            def hop(p, c, t):
                if p == place - 1:
                    return (place, 1, t) if c else (p, 1, t)
                if p == place:
                    return (p, 0, t) if c else (place - 1, 0, t)
                return p, 1 - c, t

            image = sent(image, hop)
            terms = call(
                functools.partial(project_kernel, place),
                1,
                [info, image, tall],
                terms_out,
                [],
                "project",
            )
            change = updated(place, 0, passed(terms, 1, place))
            before = [swapped(image)]
        shot, terms = call(
            functools.partial(first_kernel, place),
            1,
            [info, tall, change] + before,
            (image_out, terms_out),
            [],
            "first",
        )
        change = updated(place, 1, passed(terms, 0, place))
        outs = call(
            functools.partial(second_kernel, place, last),
            1,
            [info, change, swapped(shot), shot] + held,
            final_out if last else (image_out, image_out),
            [],
            "second",
        )
        if last:
            return outs[None]
        image = outs[0]
        held = [outs[1]]


def solution(mesh):
    in_specs = (
        P("subset", "tile", None, None, None),
        P("subset", "tile", None),
        P("subset", "tile", None),
        P(None, None, ("subset", "tile")),
    )
    out_specs = P("subset", None, None, "tile")
    return jax.shard_map(
        per_device, mesh=mesh, in_specs=in_specs, out_specs=out_specs, check_vma=False
    )
```

```python
import functools

import jax
import jax.numpy as jnp
from jax import lax
from jax.experimental import pallas as pl
from jax.experimental.pallas import tpu as pltpu
from jax.sharding import PartitionSpec as P

BS = 128
PIX = 4096
CB = PIX // BS
relaxation = 0.5

UPDATE_FLOPS = 10**10

DIRECT = 4

NN = (((1,), (0,)), ((), ()))
NT = (((1,), (1,)), ((), ()))
VMEM = pl.BlockSpec(memory_space=pltpu.VMEM)
SMEM = pl.BlockSpec(memory_space=pltpu.SMEM)
PARAMS = pltpu.CompilerParams(vmem_limit_bytes=20 * 2**20)


def dot(lhs, rhs, dims):
    return lax.dot_general(lhs, rhs, dims, preferred_element_type=jnp.float32)


def head_kernel(row_blocks, chunks, pos, rows_in, cols_in, blocks_in, rays_in, *refs):
    note, table, own, blocks, rows, cols, rays, seen, squares, norms, sems = refs
    count = blocks.shape[2]
    each = count // row_blocks
    per_chunk = count // chunks
    batches, per_batch, here = rays.shape
    quarter = here // BS
    small = [
        pltpu.make_async_copy(src, dst, sems.at[i])
        for i, (src, dst) in enumerate(((rows_in, rows), (cols_in, cols), (rays_in, rays)))
    ]
    large = []
    for k in range(chunks):
        where = pl.ds(k * per_chunk, per_chunk)
        large.append(
            pltpu.make_async_copy(
                blocks_in.at[0, 0, where], blocks.at[0, 0, where], sems.at[3 + k]
            )
        )
    for copy in small + large:
        copy.start()
    squares[...] = jnp.zeros_like(squares)
    for copy in small:
        copy.wait()
    for i in range(3):
        own[0, i] = pos[i]
    for r in range(row_blocks):
        seen[r] = r * each
    for i in range(quarter):
        parts = [rays[g, :, i * BS : (i + 1) * BS] for g in range(batches)]
        note[i] = jnp.concatenate(parts, axis=0).astype(jnp.bfloat16)
    for k in range(chunks):
        large[k].wait()
        for n in range(k * per_chunk, (k + 1) * per_chunk):
            block = blocks[0, 0, n].astype(jnp.float32)
            row = rows[0, 0, n]
            squares[row] = squares[row] + block * block
            at = seen[row]
            seen[row] = at + 1
            col = cols[0, 0, n]
            for out, first in ((table, 0), (own, 1)):
                out[first, at] = n
                out[first + 1, at] = col
    ones = jnp.ones((BS, BS), jnp.bfloat16)
    on_diagonal = lax.broadcasted_iota(jnp.int32, (BS, BS), 0) == lax.broadcasted_iota(
        jnp.int32, (BS, BS), 1
    )
    for r in range(row_blocks):
        left = squares[r]
        coarse = left.astype(jnp.bfloat16)
        fine = (left - coarse.astype(jnp.float32)).astype(jnp.bfloat16)
        total = dot(coarse, ones, NN) + dot(fine, ones, NN)
        total = jnp.sum(jnp.where(on_diagonal, total, 0.0), axis=0, keepdims=True)
        norms[r : r + 1] = total
    coarse = norms[...].astype(jnp.bfloat16)
    fine = (norms[...] - coarse.astype(jnp.float32)).astype(jnp.bfloat16)
    parts = [coarse, fine]
    pad = note.shape[1] - 2 * row_blocks
    if pad:
        parts.append(jnp.zeros((pad, BS), jnp.bfloat16))
    note[quarter] = jnp.concatenate(parts, axis=0)


def pack_own_kernel(own, blocks, _, wide):
    row_blocks = wide.shape[0]
    each = wide.shape[2] // BS
    for r in range(row_blocks):
        for j in range(each):
            block = blocks[0, 0, own[1, r * each + j]]
            wide[r, :, j * BS : (j + 1) * BS] = block


def pack_other_kernel(own, table2, blocks2, info, tall):
    row_blocks = tall.shape[0]
    each = tall.shape[1] // BS
    for i in range(3):
        info[0, i] = own[0, i]
    for r in range(row_blocks):
        for j in range(each):
            k = r * each + j
            info[1, k] = own[2, k]
            info[2, k] = table2[1, k]
            block = blocks2[0, 0, table2[0, k]]
            tall[r, j * BS : (j + 1) * BS] = block.T


def gather_rays(info, notes, rays, rays_scr):
    tiles, quarter, _, _ = rays_scr.shape
    row_blocks = tiles * quarter
    if len(notes) > 1:
        parts = [ref[quarter] for ref in notes]
        for i, ref in enumerate(notes):
            rays_scr[info[0, 2] ^ i] = ref[0:quarter].astype(jnp.float32)
    else:
        parts = [notes[0][t, quarter] for t in range(tiles)]
        rays_scr[...] = notes[0][:, 0:quarter].astype(jnp.float32)
    norms = sum(part.astype(jnp.float32) for part in parts)
    scale = relaxation / (norms[0:row_blocks] + norms[row_blocks : 2 * row_blocks])
    for r in range(row_blocks):
        row = scale[r : r + 1]
        rays[r] = rays_scr[r // quarter, r % quarter] * row
        rays[row_blocks, r : r + 1] = row


def weights(rays, terms, w_scr):
    row_blocks = w_scr.shape[0]
    for r in range(row_blocks):
        left = rays[r]
        if terms:
            total = sum(ref[r].astype(jnp.float32) for ref in terms)
            left = left - total * rays[row_blocks, r : r + 1]
        w_scr[r] = left.astype(jnp.bfloat16)


def back_project(info, wide, w_scr, image):
    row_blocks = wide.shape[0]
    each = wide.shape[2] // BS
    for r in range(row_blocks):
        back = dot(w_scr[r], wide[r], NN)
        for j in range(each):
            col = info[1, r * each + j]
            image[col] = image[col] + back[:, j * BS : (j + 1) * BS]


def project(info, tall, image, terms):
    row_blocks = tall.shape[0]
    each = tall.shape[1] // BS
    for r in range(row_blocks):
        parts = [image[info[2, r * each + j]] for j in range(each)]
        total = dot(jnp.concatenate(parts, axis=1), tall[r], NN)
        terms[r] = total.astype(jnp.bfloat16)


def take(refs, n):
    taken = refs[:n]
    del refs[:n]
    return taken


def on_core(info, place, core):
    return jnp.logical_and(info[0, 0] == place, info[0, 1] == core)


def project_kernel(place, info, image, tall, terms):
    @pl.when(on_core(info, place, 1))
    def _():
        project(info, tall, image, terms)


def update_kernel(place, core, n_notes, n_terms, *refs):
    refs = list(refs)
    info, wide = take(refs, 2)
    if n_notes:
        notes, terms_in = take(refs, n_notes), []
        change, rays, w_scr, rays_scr = refs
        gather_rays(info, notes, rays, rays_scr)
    else:
        (rays,) = take(refs, 1)
        terms_in = take(refs, n_terms)
        change, w_scr = refs

    @pl.when(on_core(info, place, core))
    def _():
        weights(rays, terms_in, w_scr)
        change[...] = jnp.zeros_like(change)
        back_project(info, wide, w_scr, change)


def first_kernel(place, *refs):
    refs = list(refs)
    info, tall, change = take(refs, 3)
    image_in = take(refs, 1)[0] if place > 0 else None
    shot, terms = refs

    @pl.when(on_core(info, place, 0))
    def _():
        value = change[...]
        if image_in is not None:
            value = value + image_in[...].astype(jnp.float32)
        shot[...] = value.astype(jnp.bfloat16)
        project(info, tall, shot, terms)


def second_kernel(place, last, *refs):
    refs = list(refs)
    info, change, image_in, shot = take(refs, 4)
    held = take(refs, 1) if place > 0 else []
    image = None if last else take(refs, 1)[0]
    (out,) = refs
    batches, per_batch, _ = out.shape

    def value(c):
        return change[c] + image_in[c].astype(jnp.float32)

    def write(source):
        for c in range(CB):
            if last:
                block = source(c).reshape(batches, per_batch, BS)
                out[:, :, c * BS : (c + 1) * BS] = block.astype(jnp.bfloat16)
            else:
                out[c] = source(c).astype(jnp.bfloat16)

    @pl.when(on_core(info, place, 1))
    def _():
        write(value)
        if not last:
            image[...] = out[...]

    @pl.when(on_core(info, place, 0))
    def _():
        write(lambda c: shot[c].astype(jnp.float32))

    if held:

        @pl.when(info[0, 0] != place)
        def _():
            write(lambda c: held[0][c].astype(jnp.float32))


def per_device(blocks, block_rows, block_cols, sinogram):
    batches, per_batch, here = sinogram.shape
    slices = batches * per_batch
    quarter = here // BS
    count = blocks.shape[2]
    subsets = lax.axis_size("subset")
    tiles = lax.axis_size("tile")
    row_blocks = quarter * tiles
    each = count // row_blocks
    places = subsets // 2
    direct = tiles <= DIRECT
    subset = lax.axis_index("subset")
    pos = jnp.stack([subset // 2, subset % 2, lax.axis_index("tile")]).astype(jnp.int32)

    image_shape = (CB, slices, BS)
    image_out = jax.ShapeDtypeStruct(image_shape, jnp.bfloat16)
    terms_out = jax.ShapeDtypeStruct((row_blocks, slices, BS), jnp.bfloat16)
    rays_out = jax.ShapeDtypeStruct((row_blocks + 1, slices, BS), jnp.float32)
    final_out = jax.ShapeDtypeStruct((batches, per_batch, PIX), jnp.bfloat16)
    w_scr = pltpu.VMEM((row_blocks, slices, BS), jnp.bfloat16)
    x_scr = pltpu.VMEM(image_shape, jnp.float32)
    rays_scr = pltpu.VMEM((tiles, quarter, slices, BS), jnp.float32)

    def sent(value, target):
        pairs = []
        for p in range(places):
            for c in range(2):
                for t in range(tiles):
                    q, e, u = target(p, c, t)
                    pairs.append(((2 * p + c) * tiles + t, (2 * q + e) * tiles + u))
        return lax.ppermute(value, ("subset", "tile"), pairs)

    def swapped(value):
        return sent(value, lambda p, c, t: (p, 1 - c, t))

    def spread(value):
        if direct:
            far = range(1, tiles)
            return [value] + [sent(value, lambda p, c, t: (p, c, t ^ d)) for d in far]
        return [lax.all_gather(value, "tile")]

    def passed(terms, core, place):
        if not direct:
            return [swapped(lax.psum(terms, "tile"))]
        ahead = place + 2 if place + 2 < places else 0
        helped = core == 0 and place > 0

        def way(d):
            def target(p, c, t):
                if helped and d == tiles - 1 and p in (place, ahead):
                    if c != core:
                        return (ahead, c, t) if p == place else (place, core, t)
                    return (p, 1 - c, t ^ d) if p == place else (p, c, t ^ 1)
                return p, 1 - c, t ^ d if c == core else t

            return target

        return [sent(terms, way(d)) for d in range(tiles)]

    def call(kernel, smem, operands, out_shape, scratch, name, flops=0):
        many = isinstance(out_shape, tuple)
        return pl.pallas_call(
            kernel,
            out_shape=out_shape,
            in_specs=[SMEM] * smem + [VMEM] * (len(operands) - smem),
            out_specs=(VMEM,) * len(out_shape) if many else VMEM,
            scratch_shapes=scratch,
            compiler_params=PARAMS,
            cost_estimate=pl.CostEstimate(
                flops=flops, bytes_accessed=0, transcendentals=0
            ),
            name=name,
        )(*operands)

    blocks2 = swapped(blocks)
    chunks = 8 if count % 8 == 0 else 1
    note, table, own, blocks = pl.pallas_call(
        functools.partial(head_kernel, row_blocks, chunks),
        out_shape=(
            jax.ShapeDtypeStruct((quarter + 1, slices, BS), jnp.bfloat16),
            jax.ShapeDtypeStruct((2, count), jnp.int32),
            pltpu.SMEM((3, count), jnp.int32),
            pltpu.VMEM(blocks.shape, blocks.dtype),
        ),
        in_specs=[SMEM] + [pl.BlockSpec(memory_space=pltpu.HBM)] * 4,
        out_specs=(VMEM, SMEM, SMEM, VMEM),
        scratch_shapes=[
            pltpu.SMEM(block_rows.shape, jnp.int32),
            pltpu.SMEM(block_cols.shape, jnp.int32),
            pltpu.VMEM(sinogram.shape, jnp.float32),
            pltpu.SMEM((row_blocks,), jnp.int32),
            pltpu.VMEM((row_blocks, BS, BS), jnp.float32),
            pltpu.VMEM((row_blocks, BS), jnp.float32),
            pltpu.SemaphoreType.DMA((3 + chunks,)),
        ],
        compiler_params=PARAMS,
        name="head",
    )(
        pos,
        *(
            pltpu.with_memory_space_constraint(value, pltpu.HBM)
            for value in (block_rows, block_cols, blocks, sinogram)
        ),
    )
    notes = spread(note)
    table2 = swapped(table)

    own = pltpu.with_memory_space_constraint(own, pltpu.SMEM)
    blocks2 = pltpu.with_memory_space_constraint(blocks2, pltpu.VMEM)
    wide = pl.pallas_call(
        pack_own_kernel,
        out_shape=pltpu.VMEM((row_blocks, BS, each * BS), jnp.bfloat16),
        in_specs=[SMEM, VMEM, pl.BlockSpec(memory_space=pl.ANY)],
        out_specs=VMEM,
        compiler_params=PARAMS,
        name="pack_own",
    )(own, blocks, note)
    info, tall = pl.pallas_call(
        pack_other_kernel,
        out_shape=(
            pltpu.SMEM((3, count), jnp.int32),
            pltpu.VMEM((row_blocks, each * BS, BS), jnp.bfloat16),
        ),
        in_specs=[SMEM, SMEM, VMEM],
        out_specs=(SMEM, VMEM),
        compiler_params=PARAMS,
        name="pack_other",
    )(own, table2, blocks2)
    info = pltpu.with_memory_space_constraint(info, pltpu.SMEM)

    held = []
    image, rays = None, None
    change_out = jax.ShapeDtypeStruct(image_shape, jnp.float32)

    def updated(place, core, terms):
        return call(
            functools.partial(update_kernel, place, core, 0, len(terms)),
            1,
            [info, wide, rays] + terms,
            change_out,
            [w_scr],
            "update",
            UPDATE_FLOPS,
        )

    for place in range(places):
        last = place == places - 1
        if place == 0:
            change, rays = call(
                functools.partial(update_kernel, place, 0, len(notes), 0),
                1,
                [info, wide] + notes,
                (change_out, rays_out),
                [w_scr, rays_scr],
                "update",
                UPDATE_FLOPS,
            )
            before = []
        else:
            def hop(p, c, t):
                if p == place - 1:
                    return (place, 1, t) if c else (p, 1, t)
                if p == place:
                    return (p, 0, t) if c else (place - 1, 0, t)
                return p, 1 - c, t

            image = sent(image, hop)
            terms = call(
                functools.partial(project_kernel, place),
                1,
                [info, image, tall],
                terms_out,
                [],
                "project",
            )
            change = updated(place, 0, passed(terms, 1, place))
            before = [swapped(image)]
        shot, terms = call(
            functools.partial(first_kernel, place),
            1,
            [info, tall, change] + before,
            (image_out, terms_out),
            [],
            "first",
        )
        change = updated(place, 1, passed(terms, 0, place))
        outs = call(
            functools.partial(second_kernel, place, last),
            1,
            [info, change, swapped(shot), shot] + held,
            final_out if last else (image_out, image_out),
            [],
            "second",
        )
        if last:
            return outs[None]
        image = outs[0]
        held = [outs[1]]


def solution(mesh):
    in_specs = (
        P("subset", "tile", None, None, None),
        P("subset", "tile", None),
        P("subset", "tile", None),
        P(None, None, ("subset", "tile")),
    )
    out_specs = P("subset", None, None, "tile")
    return jax.shard_map(
        per_device, mesh=mesh, in_specs=in_specs, out_specs=out_specs, check_vma=False
    )
```

```python
import functools

import jax
import jax.numpy as jnp
from jax import lax
from jax.experimental import pallas as pl
from jax.experimental.pallas import tpu as pltpu
from jax.sharding import PartitionSpec as P

BS = 128
PIX = 4096
CB = PIX // BS
relaxation = 0.5

UPDATE_FLOPS = 10**10

DIRECT = 4

NN = (((1,), (0,)), ((), ()))
NT = (((1,), (1,)), ((), ()))
VMEM = pl.BlockSpec(memory_space=pltpu.VMEM)
SMEM = pl.BlockSpec(memory_space=pltpu.SMEM)
PARAMS = pltpu.CompilerParams(vmem_limit_bytes=20 * 2**20)


def dot(lhs, rhs, dims):
    return lax.dot_general(lhs, rhs, dims, preferred_element_type=jnp.float32)


def head_kernel(row_blocks, chunks, pos, rows_in, cols_in, blocks_in, rays_in, *refs):
    note, table, own, blocks, rows, cols, rays, seen, squares, norms, sems = refs
    count = blocks.shape[2]
    each = count // row_blocks
    per_chunk = count // chunks
    batches, per_batch, here = rays.shape
    quarter = here // BS
    small = [
        pltpu.make_async_copy(src, dst, sems.at[i])
        for i, (src, dst) in enumerate(((rows_in, rows), (cols_in, cols), (rays_in, rays)))
    ]
    large = []
    for k in range(chunks):
        where = pl.ds(k * per_chunk, per_chunk)
        large.append(
            pltpu.make_async_copy(
                blocks_in.at[0, 0, where], blocks.at[0, 0, where], sems.at[3 + k]
            )
        )
    for copy in small + large:
        copy.start()
    squares[...] = jnp.zeros_like(squares)
    for copy in small:
        copy.wait()
    for i in range(3):
        own[0, i] = pos[i]
    for r in range(row_blocks):
        seen[r] = r * each
    for i in range(quarter):
        parts = [rays[g, :, i * BS : (i + 1) * BS] for g in range(batches)]
        note[i] = jnp.concatenate(parts, axis=0).astype(jnp.bfloat16)
    for k in range(chunks):
        large[k].wait()
        for n in range(k * per_chunk, (k + 1) * per_chunk):
            block = blocks[0, 0, n].astype(jnp.float32)
            row = rows[0, 0, n]
            squares[row] = squares[row] + block * block
            at = seen[row]
            seen[row] = at + 1
            col = cols[0, 0, n]
            for out, first in ((table, 0), (own, 1)):
                out[first, at] = n
                out[first + 1, at] = col
    ones = jnp.ones((BS, BS), jnp.bfloat16)
    on_diagonal = lax.broadcasted_iota(jnp.int32, (BS, BS), 0) == lax.broadcasted_iota(
        jnp.int32, (BS, BS), 1
    )
    for r in range(row_blocks):
        left = squares[r]
        coarse = left.astype(jnp.bfloat16)
        fine = (left - coarse.astype(jnp.float32)).astype(jnp.bfloat16)
        total = dot(coarse, ones, NN) + dot(fine, ones, NN)
        total = jnp.sum(jnp.where(on_diagonal, total, 0.0), axis=0, keepdims=True)
        norms[r : r + 1] = total
    coarse = norms[...].astype(jnp.bfloat16)
    fine = (norms[...] - coarse.astype(jnp.float32)).astype(jnp.bfloat16)
    parts = [coarse, fine]
    pad = note.shape[1] - 2 * row_blocks
    if pad:
        parts.append(jnp.zeros((pad, BS), jnp.bfloat16))
    note[quarter] = jnp.concatenate(parts, axis=0)


def pack_own_kernel(own, blocks, _, wide):
    row_blocks = wide.shape[0]
    each = wide.shape[2] // BS
    for r in range(row_blocks):
        for j in range(each):
            block = blocks[0, 0, own[1, r * each + j]]
            wide[r, :, j * BS : (j + 1) * BS] = block


def pack_other_kernel(own, table2, blocks2, info, tall):
    row_blocks = tall.shape[0]
    each = tall.shape[1] // BS
    for i in range(3):
        info[0, i] = own[0, i]
    for r in range(row_blocks):
        for j in range(each):
            k = r * each + j
            info[1, k] = own[2, k]
            info[2, k] = table2[1, k]
            block = blocks2[0, 0, table2[0, k]]
            tall[r, j * BS : (j + 1) * BS] = block.T


def gather_rays(info, notes, rays, rays_scr):
    tiles, quarter, _, _ = rays_scr.shape
    row_blocks = tiles * quarter
    if len(notes) > 1:
        parts = [ref[quarter] for ref in notes]
        for i, ref in enumerate(notes):
            rays_scr[info[0, 2] ^ i] = ref[0:quarter].astype(jnp.float32)
    else:
        parts = [notes[0][t, quarter] for t in range(tiles)]
        rays_scr[...] = notes[0][:, 0:quarter].astype(jnp.float32)
    norms = sum(part.astype(jnp.float32) for part in parts)
    scale = relaxation / (norms[0:row_blocks] + norms[row_blocks : 2 * row_blocks])
    for r in range(row_blocks):
        row = scale[r : r + 1]
        rays[r] = rays_scr[r // quarter, r % quarter] * row
        rays[row_blocks, r : r + 1] = row


def weights(rays, terms, w_scr):
    row_blocks = w_scr.shape[0]
    for r in range(row_blocks):
        left = rays[r]
        if terms:
            total = sum(ref[r].astype(jnp.float32) for ref in terms)
            left = left - total * rays[row_blocks, r : r + 1]
        w_scr[r] = left.astype(jnp.bfloat16)


def back_project(info, wide, w_scr, image):
    row_blocks = wide.shape[0]
    each = wide.shape[2] // BS
    for r in range(row_blocks):
        back = dot(w_scr[r], wide[r], NN)
        for j in range(each):
            col = info[1, r * each + j]
            image[col] = image[col] + back[:, j * BS : (j + 1) * BS]


def project(info, tall, image, terms):
    row_blocks = tall.shape[0]
    each = tall.shape[1] // BS
    for r in range(row_blocks):
        parts = [image[info[2, r * each + j]] for j in range(each)]
        total = dot(jnp.concatenate(parts, axis=1), tall[r], NN)
        terms[r] = total.astype(jnp.bfloat16)


def take(refs, n):
    taken = refs[:n]
    del refs[:n]
    return taken


def on_core(info, place, core):
    return jnp.logical_and(info[0, 0] == place, info[0, 1] == core)


def project_kernel(place, info, image, tall, terms):
    @pl.when(on_core(info, place, 1))
    def _():
        project(info, tall, image, terms)


def update_kernel(place, core, n_notes, n_terms, *refs):
    refs = list(refs)
    info, wide = take(refs, 2)
    if n_notes:
        notes, terms_in = take(refs, n_notes), []
        change, rays, w_scr, rays_scr = refs
        gather_rays(info, notes, rays, rays_scr)
    else:
        (rays,) = take(refs, 1)
        terms_in = take(refs, n_terms)
        change, w_scr = refs

    @pl.when(on_core(info, place, core))
    def _():
        weights(rays, terms_in, w_scr)
        change[...] = jnp.zeros_like(change)
        back_project(info, wide, w_scr, change)


def first_kernel(place, *refs):
    refs = list(refs)
    info, tall, change = take(refs, 3)
    image_in = take(refs, 1)[0] if place > 0 else None
    shot, terms = refs

    @pl.when(on_core(info, place, 0))
    def _():
        value = change[...]
        if image_in is not None:
            value = value + image_in[...].astype(jnp.float32)
        shot[...] = value.astype(jnp.bfloat16)
        project(info, tall, shot, terms)


def second_kernel(place, last, *refs):
    refs = list(refs)
    info, change, image_in, shot = take(refs, 4)
    held = take(refs, 1) if place > 0 else []
    image = None if last else take(refs, 1)[0]
    (out,) = refs
    batches, per_batch, _ = out.shape

    def value(c):
        return change[c] + image_in[c].astype(jnp.float32)

    def write(source):
        for c in range(CB):
            if last:
                block = source(c).reshape(batches, per_batch, BS)
                out[:, :, c * BS : (c + 1) * BS] = block.astype(jnp.bfloat16)
            else:
                out[c] = source(c).astype(jnp.bfloat16)

    @pl.when(on_core(info, place, 1))
    def _():
        write(value)
        if not last:
            image[...] = out[...]

    @pl.when(on_core(info, place, 0))
    def _():
        write(lambda c: shot[c].astype(jnp.float32))

    if held:

        @pl.when(info[0, 0] != place)
        def _():
            write(lambda c: held[0][c].astype(jnp.float32))


def per_device(blocks, block_rows, block_cols, sinogram):
    batches, per_batch, here = sinogram.shape
    slices = batches * per_batch
    quarter = here // BS
    count = blocks.shape[2]
    subsets = lax.axis_size("subset")
    tiles = lax.axis_size("tile")
    row_blocks = quarter * tiles
    each = count // row_blocks
    places = subsets // 2
    direct = tiles <= DIRECT
    subset = lax.axis_index("subset")
    pos = jnp.stack([subset // 2, subset % 2, lax.axis_index("tile")]).astype(jnp.int32)

    image_shape = (CB, slices, BS)
    image_out = jax.ShapeDtypeStruct(image_shape, jnp.bfloat16)
    terms_out = jax.ShapeDtypeStruct((row_blocks, slices, BS), jnp.bfloat16)
    rays_out = jax.ShapeDtypeStruct((row_blocks + 1, slices, BS), jnp.float32)
    final_out = jax.ShapeDtypeStruct((batches, per_batch, PIX), jnp.bfloat16)
    w_scr = pltpu.VMEM((row_blocks, slices, BS), jnp.bfloat16)
    x_scr = pltpu.VMEM(image_shape, jnp.float32)
    rays_scr = pltpu.VMEM((tiles, quarter, slices, BS), jnp.float32)

    def sent(value, target):
        pairs = []
        for p in range(places):
            for c in range(2):
                for t in range(tiles):
                    q, e, u = target(p, c, t)
                    pairs.append(((2 * p + c) * tiles + t, (2 * q + e) * tiles + u))
        return lax.ppermute(value, ("subset", "tile"), pairs)

    def swapped(value):
        return sent(value, lambda p, c, t: (p, 1 - c, t))

    def spread(value):
        if direct:
            far = range(1, tiles)
            return [value] + [sent(value, lambda p, c, t: (p, c, t ^ d)) for d in far]
        return [lax.all_gather(value, "tile")]

    def passed(terms, core, place):
        if not direct:
            return [swapped(lax.psum(terms, "tile"))]
        ahead = 0
        helped = core == 0 and 0 < place == places - 1

        def way(d):
            def target(p, c, t):
                if helped and d == tiles - 1 and p in (place, ahead):
                    if c != core:
                        return (ahead, c, t) if p == place else (place, core, t)
                    return (p, 1 - c, t ^ d) if p == place else (p, c, t ^ 1)
                return p, 1 - c, t ^ d if c == core else t

            return target

        return [sent(terms, way(d)) for d in range(tiles)]

    def call(kernel, smem, operands, out_shape, scratch, name, flops=0):
        many = isinstance(out_shape, tuple)
        return pl.pallas_call(
            kernel,
            out_shape=out_shape,
            in_specs=[SMEM] * smem + [VMEM] * (len(operands) - smem),
            out_specs=(VMEM,) * len(out_shape) if many else VMEM,
            scratch_shapes=scratch,
            compiler_params=PARAMS,
            cost_estimate=pl.CostEstimate(
                flops=flops, bytes_accessed=0, transcendentals=0
            ),
            name=name,
        )(*operands)

    blocks2 = swapped(blocks)
    chunks = 8 if count % 8 == 0 else 1
    note, table, own, blocks = pl.pallas_call(
        functools.partial(head_kernel, row_blocks, chunks),
        out_shape=(
            jax.ShapeDtypeStruct((quarter + 1, slices, BS), jnp.bfloat16),
            jax.ShapeDtypeStruct((2, count), jnp.int32),
            pltpu.SMEM((3, count), jnp.int32),
            pltpu.VMEM(blocks.shape, blocks.dtype),
        ),
        in_specs=[SMEM] + [pl.BlockSpec(memory_space=pltpu.HBM)] * 4,
        out_specs=(VMEM, SMEM, SMEM, VMEM),
        scratch_shapes=[
            pltpu.SMEM(block_rows.shape, jnp.int32),
            pltpu.SMEM(block_cols.shape, jnp.int32),
            pltpu.VMEM(sinogram.shape, jnp.float32),
            pltpu.SMEM((row_blocks,), jnp.int32),
            pltpu.VMEM((row_blocks, BS, BS), jnp.float32),
            pltpu.VMEM((row_blocks, BS), jnp.float32),
            pltpu.SemaphoreType.DMA((3 + chunks,)),
        ],
        compiler_params=PARAMS,
        name="head",
    )(
        pos,
        *(
            pltpu.with_memory_space_constraint(value, pltpu.HBM)
            for value in (block_rows, block_cols, blocks, sinogram)
        ),
    )
    notes = spread(note)
    table2 = swapped(table)

    own = pltpu.with_memory_space_constraint(own, pltpu.SMEM)
    blocks2 = pltpu.with_memory_space_constraint(blocks2, pltpu.VMEM)
    wide = pl.pallas_call(
        pack_own_kernel,
        out_shape=pltpu.VMEM((row_blocks, BS, each * BS), jnp.bfloat16),
        in_specs=[SMEM, VMEM, pl.BlockSpec(memory_space=pl.ANY)],
        out_specs=VMEM,
        compiler_params=PARAMS,
        name="pack_own",
    )(own, blocks, note)
    info, tall = pl.pallas_call(
        pack_other_kernel,
        out_shape=(
            pltpu.SMEM((3, count), jnp.int32),
            pltpu.VMEM((row_blocks, each * BS, BS), jnp.bfloat16),
        ),
        in_specs=[SMEM, SMEM, VMEM],
        out_specs=(SMEM, VMEM),
        compiler_params=PARAMS,
        name="pack_other",
    )(own, table2, blocks2)
    info = pltpu.with_memory_space_constraint(info, pltpu.SMEM)

    held = []
    image, rays = None, None
    change_out = jax.ShapeDtypeStruct(image_shape, jnp.float32)

    def updated(place, core, terms):
        return call(
            functools.partial(update_kernel, place, core, 0, len(terms)),
            1,
            [info, wide, rays] + terms,
            change_out,
            [w_scr],
            "update",
            UPDATE_FLOPS,
        )

    for place in range(places):
        last = place == places - 1
        if place == 0:
            change, rays = call(
                functools.partial(update_kernel, place, 0, len(notes), 0),
                1,
                [info, wide] + notes,
                (change_out, rays_out),
                [w_scr, rays_scr],
                "update",
                UPDATE_FLOPS,
            )
            before = []
        else:
            def hop(p, c, t):
                if p == place - 1:
                    return (place, 1, t) if c else (p, 1, t)
                if p == place:
                    return (p, 0, t) if c else (place - 1, 0, t)
                return p, 1 - c, t

            image = sent(image, hop)
            terms = call(
                functools.partial(project_kernel, place),
                1,
                [info, image, tall],
                terms_out,
                [],
                "project",
            )
            change = updated(place, 0, passed(terms, 1, place))
            before = [swapped(image)]
        shot, terms = call(
            functools.partial(first_kernel, place),
            1,
            [info, tall, change] + before,
            (image_out, terms_out),
            [],
            "first",
        )
        change = updated(place, 1, passed(terms, 0, place))
        outs = call(
            functools.partial(second_kernel, place, last),
            1,
            [info, change, swapped(shot), shot] + held,
            final_out if last else (image_out, image_out),
            [],
            "second",
        )
        if last:
            return outs[None]
        image = outs[0]
        held = [outs[1]]


def solution(mesh):
    in_specs = (
        P("subset", "tile", None, None, None),
        P("subset", "tile", None),
        P("subset", "tile", None),
        P(None, None, ("subset", "tile")),
    )
    out_specs = P("subset", None, None, "tile")
    return jax.shard_map(
        per_device, mesh=mesh, in_specs=in_specs, out_specs=out_specs, check_vma=False
    )
```

```python
import functools

import jax
import jax.numpy as jnp
from jax import lax
from jax.experimental import pallas as pl
from jax.experimental.pallas import tpu as pltpu
from jax.sharding import PartitionSpec as P

BS = 128
PIX = 4096
CB = PIX // BS
relaxation = 0.5

UPDATE_FLOPS = 10**10

DIRECT = 4

NN = (((1,), (0,)), ((), ()))
NT = (((1,), (1,)), ((), ()))
VMEM = pl.BlockSpec(memory_space=pltpu.VMEM)
SMEM = pl.BlockSpec(memory_space=pltpu.SMEM)
PARAMS = pltpu.CompilerParams(vmem_limit_bytes=20 * 2**20)


def dot(lhs, rhs, dims):
    return lax.dot_general(lhs, rhs, dims, preferred_element_type=jnp.float32)


def head_kernel(row_blocks, chunks, pos, rows_in, cols_in, blocks_in, rays_in, *refs):
    note, table, own, blocks, rows, cols, rays, seen, squares, squares2, norms, sems = refs
    count = blocks.shape[2]
    each = count // row_blocks
    per_chunk = count // chunks
    batches, per_batch, here = rays.shape
    quarter = here // BS
    small = [
        pltpu.make_async_copy(src, dst, sems.at[i])
        for i, (src, dst) in enumerate(((rows_in, rows), (cols_in, cols), (rays_in, rays)))
    ]
    large = []
    for k in range(chunks):
        where = pl.ds(k * per_chunk, per_chunk)
        large.append(
            pltpu.make_async_copy(
                blocks_in.at[0, 0, where], blocks.at[0, 0, where], sems.at[3 + k]
            )
        )
    for copy in small + large:
        copy.start()
    squares[...] = jnp.zeros_like(squares)
    squares2[...] = jnp.zeros_like(squares2)
    for copy in small:
        copy.wait()
    for i in range(3):
        own[0, i] = pos[i]
    for r in range(row_blocks):
        seen[r] = r * each
    for i in range(quarter):
        parts = [rays[g, :, i * BS : (i + 1) * BS] for g in range(batches)]
        note[i] = jnp.concatenate(parts, axis=0).astype(jnp.bfloat16)
    for k in range(chunks):
        large[k].wait()
        for n in range(k * per_chunk, (k + 1) * per_chunk):
            block = blocks[0, 0, n].astype(jnp.float32)
            row = rows[0, 0, n]
            into = squares2 if n % 2 else squares
            into[row] = into[row] + block * block
            at = seen[row]
            seen[row] = at + 1
            col = cols[0, 0, n]
            for out, first in ((table, 0), (own, 1)):
                out[first, at] = n
                out[first + 1, at] = col
    ones = jnp.ones((BS, BS), jnp.bfloat16)
    on_diagonal = lax.broadcasted_iota(jnp.int32, (BS, BS), 0) == lax.broadcasted_iota(
        jnp.int32, (BS, BS), 1
    )
    for r in range(row_blocks):
        left = squares[r] + squares2[r]
        coarse = left.astype(jnp.bfloat16)
        fine = (left - coarse.astype(jnp.float32)).astype(jnp.bfloat16)
        total = dot(coarse, ones, NN) + dot(fine, ones, NN)
        total = jnp.sum(jnp.where(on_diagonal, total, 0.0), axis=0, keepdims=True)
        norms[r : r + 1] = total
    coarse = norms[...].astype(jnp.bfloat16)
    fine = (norms[...] - coarse.astype(jnp.float32)).astype(jnp.bfloat16)
    parts = [coarse, fine]
    pad = note.shape[1] - 2 * row_blocks
    if pad:
        parts.append(jnp.zeros((pad, BS), jnp.bfloat16))
    note[quarter] = jnp.concatenate(parts, axis=0)


def pack_own_kernel(own, blocks, _, wide):
    row_blocks = wide.shape[0]
    each = wide.shape[2] // BS
    for r in range(row_blocks):
        for j in range(each):
            block = blocks[0, 0, own[1, r * each + j]]
            wide[r, :, j * BS : (j + 1) * BS] = block


def pack_other_kernel(own, table2, blocks2, info, tall):
    row_blocks = tall.shape[0]
    each = tall.shape[1] // BS
    for i in range(3):
        info[0, i] = own[0, i]
    for r in range(row_blocks):
        for j in range(each):
            k = r * each + j
            info[1, k] = own[2, k]
            info[2, k] = table2[1, k]
            block = blocks2[0, 0, table2[0, k]]
            tall[r, j * BS : (j + 1) * BS] = block.T


def gather_rays(info, notes, rays, rays_scr):
    tiles, quarter, _, _ = rays_scr.shape
    row_blocks = tiles * quarter
    if len(notes) > 1:
        parts = [ref[quarter] for ref in notes]
        for i, ref in enumerate(notes):
            rays_scr[info[0, 2] ^ i] = ref[0:quarter].astype(jnp.float32)
    else:
        parts = [notes[0][t, quarter] for t in range(tiles)]
        rays_scr[...] = notes[0][:, 0:quarter].astype(jnp.float32)
    norms = sum(part.astype(jnp.float32) for part in parts)
    scale = relaxation / (norms[0:row_blocks] + norms[row_blocks : 2 * row_blocks])
    for r in range(row_blocks):
        row = scale[r : r + 1]
        rays[r] = rays_scr[r // quarter, r % quarter] * row
        rays[row_blocks, r : r + 1] = row


def weights(rays, terms, w_scr):
    row_blocks = w_scr.shape[0]
    for r in range(row_blocks):
        left = rays[r]
        if terms:
            total = sum(ref[r].astype(jnp.float32) for ref in terms)
            left = left - total * rays[row_blocks, r : r + 1]
        w_scr[r] = left.astype(jnp.bfloat16)


def back_project(info, wide, w_scr, changes):
    row_blocks = wide.shape[0]
    each = wide.shape[2] // BS
    for r in range(row_blocks):
        back = dot(w_scr[r], wide[r], NN)
        for j in range(each):
            col = info[1, r * each + j]
            into = changes[(r * each + j) % 2]
            into[col] = into[col] + back[:, j * BS : (j + 1) * BS]


def project(info, tall, image, terms):
    row_blocks = tall.shape[0]
    each = tall.shape[1] // BS
    for r in range(row_blocks):
        parts = [image[info[2, r * each + j]] for j in range(each)]
        total = dot(jnp.concatenate(parts, axis=1), tall[r], NN)
        terms[r] = total.astype(jnp.bfloat16)


def take(refs, n):
    taken = refs[:n]
    del refs[:n]
    return taken


def on_core(info, place, core):
    return jnp.logical_and(info[0, 0] == place, info[0, 1] == core)


def project_kernel(place, info, image, tall, terms):
    @pl.when(on_core(info, place, 1))
    def _():
        project(info, tall, image, terms)


def update_kernel(place, core, n_notes, n_terms, *refs):
    refs = list(refs)
    info, wide = take(refs, 2)
    if n_notes:
        notes, terms_in = take(refs, n_notes), []
        change, change2, rays, w_scr, rays_scr = refs
        gather_rays(info, notes, rays, rays_scr)
    else:
        (rays,) = take(refs, 1)
        terms_in = take(refs, n_terms)
        change, change2, w_scr = refs

    @pl.when(on_core(info, place, core))
    def _():
        weights(rays, terms_in, w_scr)
        change[...] = jnp.zeros_like(change)
        change2[...] = jnp.zeros_like(change2)
        back_project(info, wide, w_scr, (change, change2))


def first_kernel(place, *refs):
    refs = list(refs)
    info, tall, change, change2 = take(refs, 4)
    image_in = take(refs, 1)[0] if place > 0 else None
    shot, terms = refs

    @pl.when(on_core(info, place, 0))
    def _():
        value = change[...] + change2[...]
        if image_in is not None:
            value = value + image_in[...].astype(jnp.float32)
        shot[...] = value.astype(jnp.bfloat16)
        project(info, tall, shot, terms)


def second_kernel(place, last, *refs):
    refs = list(refs)
    info, change, change2, image_in, shot = take(refs, 5)
    held = take(refs, 1) if place > 0 else []
    image = None if last else take(refs, 1)[0]
    (out,) = refs
    batches, per_batch, _ = out.shape

    def value(c):
        return change[c] + change2[c] + image_in[c].astype(jnp.float32)

    def write(source):
        for c in range(CB):
            if last:
                block = source(c).reshape(batches, per_batch, BS)
                out[:, :, c * BS : (c + 1) * BS] = block.astype(jnp.bfloat16)
            else:
                out[c] = source(c).astype(jnp.bfloat16)

    @pl.when(on_core(info, place, 1))
    def _():
        write(value)
        if not last:
            image[...] = out[...]

    @pl.when(on_core(info, place, 0))
    def _():
        write(lambda c: shot[c].astype(jnp.float32))

    if held:

        @pl.when(info[0, 0] != place)
        def _():
            write(lambda c: held[0][c].astype(jnp.float32))


def per_device(blocks, block_rows, block_cols, sinogram):
    batches, per_batch, here = sinogram.shape
    slices = batches * per_batch
    quarter = here // BS
    count = blocks.shape[2]
    subsets = lax.axis_size("subset")
    tiles = lax.axis_size("tile")
    row_blocks = quarter * tiles
    each = count // row_blocks
    places = subsets // 2
    direct = tiles <= DIRECT
    subset = lax.axis_index("subset")
    pos = jnp.stack([subset // 2, subset % 2, lax.axis_index("tile")]).astype(jnp.int32)

    image_shape = (CB, slices, BS)
    image_out = jax.ShapeDtypeStruct(image_shape, jnp.bfloat16)
    terms_out = jax.ShapeDtypeStruct((row_blocks, slices, BS), jnp.bfloat16)
    rays_out = jax.ShapeDtypeStruct((row_blocks + 1, slices, BS), jnp.float32)
    final_out = jax.ShapeDtypeStruct((batches, per_batch, PIX), jnp.bfloat16)
    w_scr = pltpu.VMEM((row_blocks, slices, BS), jnp.bfloat16)
    x_scr = pltpu.VMEM(image_shape, jnp.float32)
    rays_scr = pltpu.VMEM((tiles, quarter, slices, BS), jnp.float32)

    def sent(value, target):
        pairs = []
        for p in range(places):
            for c in range(2):
                for t in range(tiles):
                    q, e, u = target(p, c, t)
                    pairs.append(((2 * p + c) * tiles + t, (2 * q + e) * tiles + u))
        return lax.ppermute(value, ("subset", "tile"), pairs)

    def swapped(value):
        return sent(value, lambda p, c, t: (p, 1 - c, t))

    def spread(value):
        if direct:
            far = range(1, tiles)
            return [value] + [sent(value, lambda p, c, t: (p, c, t ^ d)) for d in far]
        return [lax.all_gather(value, "tile")]

    def passed(terms, core):
        if not direct:
            return [swapped(lax.psum(terms, "tile"))]
        return [
            sent(terms, lambda p, c, t: (p, 1 - c, t ^ d if c == core else t))
            for d in range(tiles)
        ]

    def call(kernel, smem, operands, out_shape, scratch, name, flops=0):
        many = isinstance(out_shape, tuple)
        return pl.pallas_call(
            kernel,
            out_shape=out_shape,
            in_specs=[SMEM] * smem + [VMEM] * (len(operands) - smem),
            out_specs=(VMEM,) * len(out_shape) if many else VMEM,
            scratch_shapes=scratch,
            compiler_params=PARAMS,
            cost_estimate=pl.CostEstimate(
                flops=flops, bytes_accessed=0, transcendentals=0
            ),
            name=name,
        )(*operands)

    blocks2 = swapped(blocks)
    chunks = 8 if count % 8 == 0 else 1
    note, table, own, blocks = pl.pallas_call(
        functools.partial(head_kernel, row_blocks, chunks),
        out_shape=(
            jax.ShapeDtypeStruct((quarter + 1, slices, BS), jnp.bfloat16),
            jax.ShapeDtypeStruct((2, count), jnp.int32),
            pltpu.SMEM((3, count), jnp.int32),
            pltpu.VMEM(blocks.shape, blocks.dtype),
        ),
        in_specs=[SMEM] + [pl.BlockSpec(memory_space=pltpu.HBM)] * 4,
        out_specs=(VMEM, SMEM, SMEM, VMEM),
        scratch_shapes=[
            pltpu.SMEM(block_rows.shape, jnp.int32),
            pltpu.SMEM(block_cols.shape, jnp.int32),
            pltpu.VMEM(sinogram.shape, jnp.float32),
            pltpu.SMEM((row_blocks,), jnp.int32),
            pltpu.VMEM((row_blocks, BS, BS), jnp.float32),
            pltpu.VMEM((row_blocks, BS, BS), jnp.float32),
            pltpu.VMEM((row_blocks, BS), jnp.float32),
            pltpu.SemaphoreType.DMA((3 + chunks,)),
        ],
        compiler_params=PARAMS,
        name="head",
    )(
        pos,
        *(
            pltpu.with_memory_space_constraint(value, pltpu.HBM)
            for value in (block_rows, block_cols, blocks, sinogram)
        ),
    )
    notes = spread(note)
    table2 = swapped(table)

    own = pltpu.with_memory_space_constraint(own, pltpu.SMEM)
    blocks2 = pltpu.with_memory_space_constraint(blocks2, pltpu.VMEM)
    wide = pl.pallas_call(
        pack_own_kernel,
        out_shape=pltpu.VMEM((row_blocks, BS, each * BS), jnp.bfloat16),
        in_specs=[SMEM, VMEM, pl.BlockSpec(memory_space=pl.ANY)],
        out_specs=VMEM,
        compiler_params=PARAMS,
        name="pack_own",
    )(own, blocks, note)
    info, tall = pl.pallas_call(
        pack_other_kernel,
        out_shape=(
            pltpu.SMEM((3, count), jnp.int32),
            pltpu.VMEM((row_blocks, each * BS, BS), jnp.bfloat16),
        ),
        in_specs=[SMEM, SMEM, VMEM],
        out_specs=(SMEM, VMEM),
        compiler_params=PARAMS,
        name="pack_other",
    )(own, table2, blocks2)
    info = pltpu.with_memory_space_constraint(info, pltpu.SMEM)

    held = []
    image, rays = None, None
    change_out = jax.ShapeDtypeStruct(image_shape, jnp.float32)

    def updated(place, core, terms):
        return call(
            functools.partial(update_kernel, place, core, 0, len(terms)),
            1,
            [info, wide, rays] + terms,
            (change_out, change_out),
            [w_scr],
            "update",
            UPDATE_FLOPS,
        )

    for place in range(places):
        last = place == places - 1
        if place == 0:
            *changes, rays = call(
                functools.partial(update_kernel, place, 0, len(notes), 0),
                1,
                [info, wide] + notes,
                (change_out, change_out, rays_out),
                [w_scr, rays_scr],
                "update",
                UPDATE_FLOPS,
            )
            before = []
        else:
            def hop(p, c, t):
                if p == place - 1:
                    return (place, 1, t) if c else (p, 1, t)
                if p == place:
                    return (p, 0, t) if c else (place - 1, 0, t)
                return p, 1 - c, t

            image = sent(image, hop)
            terms = call(
                functools.partial(project_kernel, place),
                1,
                [info, image, tall],
                terms_out,
                [],
                "project",
            )
            changes = updated(place, 0, passed(terms, 1))
            before = [swapped(image)]
        shot, terms = call(
            functools.partial(first_kernel, place),
            1,
            [info, tall, *changes] + before,
            (image_out, terms_out),
            [],
            "first",
        )
        changes = updated(place, 1, passed(terms, 0))
        outs = call(
            functools.partial(second_kernel, place, last),
            1,
            [info, *changes, swapped(shot), shot] + held,
            final_out if last else (image_out, image_out),
            [],
            "second",
        )
        if last:
            return outs[None]
        image = outs[0]
        held = [outs[1]]


def solution(mesh):
    in_specs = (
        P("subset", "tile", None, None, None),
        P("subset", "tile", None),
        P("subset", "tile", None),
        P(None, None, ("subset", "tile")),
    )
    out_specs = P("subset", None, None, "tile")
    return jax.shard_map(
        per_device, mesh=mesh, in_specs=in_specs, out_specs=out_specs, check_vma=False
    )
```

```python
import functools

import jax
import jax.numpy as jnp
from jax import lax
from jax.experimental import pallas as pl
from jax.experimental.pallas import tpu as pltpu
from jax.sharding import PartitionSpec as P

BS = 128
PIX = 4096
CB = PIX // BS
relaxation = 0.5

UPDATE_FLOPS = 10**10

DIRECT = 4

NN = (((1,), (0,)), ((), ()))
NT = (((1,), (1,)), ((), ()))
VMEM = pl.BlockSpec(memory_space=pltpu.VMEM)
SMEM = pl.BlockSpec(memory_space=pltpu.SMEM)
PARAMS = pltpu.CompilerParams(vmem_limit_bytes=20 * 2**20)


def dot(lhs, rhs, dims):
    return lax.dot_general(lhs, rhs, dims, preferred_element_type=jnp.float32)


def head_kernel(row_blocks, chunks, pos, rows_in, cols_in, blocks_in, rays_in, *refs):
    note, table, own, blocks, rows, cols, rays, seen, squares, norms, sems = refs
    count = blocks.shape[2]
    each = count // row_blocks
    per_chunk = count // chunks
    batches, per_batch, here = rays.shape
    quarter = here // BS
    small = [
        pltpu.make_async_copy(src, dst, sems.at[i])
        for i, (src, dst) in enumerate(((rows_in, rows), (cols_in, cols), (rays_in, rays)))
    ]
    large = []
    for k in range(chunks):
        where = pl.ds(k * per_chunk, per_chunk)
        large.append(
            pltpu.make_async_copy(
                blocks_in.at[0, 0, where], blocks.at[0, 0, where], sems.at[3 + k]
            )
        )
    for copy in small + large:
        copy.start()
    squares[...] = jnp.zeros_like(squares)
    for copy in small:
        copy.wait()
    for i in range(3):
        own[0, i] = pos[i]
    for r in range(row_blocks):
        seen[r] = r * each
    for i in range(quarter):
        parts = [rays[g, :, i * BS : (i + 1) * BS] for g in range(batches)]
        note[i] = jnp.concatenate(parts, axis=0).astype(jnp.bfloat16)
    for k in range(chunks):
        large[k].wait()
        for n in range(k * per_chunk, (k + 1) * per_chunk):
            block = blocks[0, 0, n].astype(jnp.float32)
            row = rows[0, 0, n]
            squares[row] = squares[row] + block * block
            at = seen[row]
            seen[row] = at + 1
            col = cols[0, 0, n]
            for out, first in ((table, 0), (own, 1)):
                out[first, at] = n
                out[first + 1, at] = col
    ones = jnp.ones((BS, BS), jnp.bfloat16)
    on_diagonal = lax.broadcasted_iota(jnp.int32, (BS, BS), 0) == lax.broadcasted_iota(
        jnp.int32, (BS, BS), 1
    )
    for r in range(row_blocks):
        left = squares[r]
        coarse = left.astype(jnp.bfloat16)
        fine = (left - coarse.astype(jnp.float32)).astype(jnp.bfloat16)
        total = dot(coarse, ones, NN) + dot(fine, ones, NN)
        total = jnp.sum(jnp.where(on_diagonal, total, 0.0), axis=0, keepdims=True)
        norms[r : r + 1] = total
    coarse = norms[...].astype(jnp.bfloat16)
    fine = (norms[...] - coarse.astype(jnp.float32)).astype(jnp.bfloat16)
    parts = [coarse, fine]
    pad = note.shape[1] - 2 * row_blocks
    if pad:
        parts.append(jnp.zeros((pad, BS), jnp.bfloat16))
    note[quarter] = jnp.concatenate(parts, axis=0)


def pack_own_kernel(own, blocks, _, wide):
    row_blocks = wide.shape[0]
    each = wide.shape[2] // BS
    for r in range(row_blocks):
        for j in range(each):
            block = blocks[0, 0, own[1, r * each + j]]
            wide[r, :, j * BS : (j + 1) * BS] = block


def pack_other_kernel(own, table2, blocks2, info, tall):
    row_blocks = tall.shape[0]
    each = tall.shape[1] // BS
    for i in range(3):
        info[0, i] = own[0, i]
    for r in range(row_blocks):
        for j in range(each):
            k = r * each + j
            info[1, k] = own[2, k]
            info[2, k] = table2[1, k]
            block = blocks2[0, 0, table2[0, k]]
            tall[r, j * BS : (j + 1) * BS] = block.T


def gather_rays(info, notes, rays, rays_scr):
    tiles, quarter, _, _ = rays_scr.shape
    row_blocks = tiles * quarter
    if len(notes) > 1:
        parts = [ref[quarter] for ref in notes]
        for i, ref in enumerate(notes):
            rays_scr[info[0, 2] ^ i] = ref[0:quarter].astype(jnp.float32)
    else:
        parts = [notes[0][t, quarter] for t in range(tiles)]
        rays_scr[...] = notes[0][:, 0:quarter].astype(jnp.float32)
    norms = sum(part.astype(jnp.float32) for part in parts)
    scale = relaxation / (norms[0:row_blocks] + norms[row_blocks : 2 * row_blocks])
    for r in range(row_blocks):
        row = scale[r : r + 1]
        rays[r] = rays_scr[r // quarter, r % quarter] * row
        rays[row_blocks, r : r + 1] = row


def weights(rays, terms, w_scr):
    row_blocks = w_scr.shape[0]
    for r in range(row_blocks):
        left = rays[r]
        if terms:
            total = sum(ref[r].astype(jnp.float32) for ref in terms)
            left = left - total * rays[row_blocks, r : r + 1]
        w_scr[r] = left.astype(jnp.bfloat16)


def back_project(info, wide, w_scr, image):
    row_blocks = wide.shape[0]
    each = wide.shape[2] // BS
    for r in range(row_blocks):
        back = dot(w_scr[r], wide[r], NN)
        for j in range(each):
            col = info[1, r * each + j]
            image[col] = image[col] + back[:, j * BS : (j + 1) * BS]


def project(info, tall, image, terms):
    row_blocks = tall.shape[0]
    each = tall.shape[1] // BS
    for r in range(row_blocks):
        parts = [image[info[2, r * each + j]] for j in range(each)]
        total = dot(jnp.concatenate(parts, axis=1), tall[r], NN)
        terms[r] = total.astype(jnp.bfloat16)


def take(refs, n):
    taken = refs[:n]
    del refs[:n]
    return taken


def on_core(info, place, core):
    return jnp.logical_and(info[0, 0] == place, info[0, 1] == core)


def project_kernel(place, info, lower, upper, tall, terms, image):
    @pl.when(on_core(info, place, 1))
    def _():
        image[: CB // 2] = lower[...]
        image[CB // 2 :] = upper[...]
        project(info, tall, image, terms)


def update_kernel(place, core, n_notes, n_terms, *refs):
    refs = list(refs)
    info, wide = take(refs, 2)
    if n_notes:
        notes, terms_in = take(refs, n_notes), []
        change, rays, w_scr, rays_scr = refs
        gather_rays(info, notes, rays, rays_scr)
    else:
        (rays,) = take(refs, 1)
        terms_in = take(refs, n_terms)
        change, w_scr = refs

    @pl.when(on_core(info, place, core))
    def _():
        weights(rays, terms_in, w_scr)
        change[...] = jnp.zeros_like(change)
        back_project(info, wide, w_scr, change)


def first_kernel(place, *refs):
    refs = list(refs)
    info, tall, change = take(refs, 3)
    image_in = take(refs, 1)[0] if place > 0 else None
    shot, terms = refs

    @pl.when(on_core(info, place, 0))
    def _():
        value = change[...]
        if image_in is not None:
            value = value + image_in[...].astype(jnp.float32)
        shot[...] = value.astype(jnp.bfloat16)
        project(info, tall, shot, terms)


def second_kernel(place, last, *refs):
    refs = list(refs)
    info, change, image_in, shot = take(refs, 4)
    held = take(refs, 1) if place > 0 else []
    parts = [] if last else take(refs, 2)
    (out,) = refs
    batches, per_batch, _ = out.shape

    def value(c):
        return change[c] + image_in[c].astype(jnp.float32)

    def write(source):
        for c in range(CB):
            if last:
                block = source(c).reshape(batches, per_batch, BS)
                out[:, :, c * BS : (c + 1) * BS] = block.astype(jnp.bfloat16)
            else:
                out[c] = source(c).astype(jnp.bfloat16)

    @pl.when(on_core(info, place, 1))
    def _():
        write(value)
        for i, part in enumerate(parts):
            part[...] = out[i * (CB // 2) : (i + 1) * (CB // 2)]

    @pl.when(on_core(info, place, 0))
    def _():
        write(lambda c: shot[c].astype(jnp.float32))

    if held:

        @pl.when(info[0, 0] != place)
        def _():
            write(lambda c: held[0][c].astype(jnp.float32))


def per_device(blocks, block_rows, block_cols, sinogram):
    batches, per_batch, here = sinogram.shape
    slices = batches * per_batch
    quarter = here // BS
    count = blocks.shape[2]
    subsets = lax.axis_size("subset")
    tiles = lax.axis_size("tile")
    row_blocks = quarter * tiles
    each = count // row_blocks
    places = subsets // 2
    direct = tiles <= DIRECT
    subset = lax.axis_index("subset")
    pos = jnp.stack([subset // 2, subset % 2, lax.axis_index("tile")]).astype(jnp.int32)

    image_shape = (CB, slices, BS)
    image_out = jax.ShapeDtypeStruct(image_shape, jnp.bfloat16)
    part_out = jax.ShapeDtypeStruct((CB // 2, slices, BS), jnp.bfloat16)
    terms_out = jax.ShapeDtypeStruct((row_blocks, slices, BS), jnp.bfloat16)
    rays_out = jax.ShapeDtypeStruct((row_blocks + 1, slices, BS), jnp.float32)
    final_out = jax.ShapeDtypeStruct((batches, per_batch, PIX), jnp.bfloat16)
    w_scr = pltpu.VMEM((row_blocks, slices, BS), jnp.bfloat16)
    x_scr = pltpu.VMEM(image_shape, jnp.float32)
    rays_scr = pltpu.VMEM((tiles, quarter, slices, BS), jnp.float32)

    def sent(value, target):
        pairs = []
        for p in range(places):
            for c in range(2):
                for t in range(tiles):
                    q, e, u = target(p, c, t)
                    pairs.append(((2 * p + c) * tiles + t, (2 * q + e) * tiles + u))
        return lax.ppermute(value, ("subset", "tile"), pairs)

    def swapped(value):
        return sent(value, lambda p, c, t: (p, 1 - c, t))

    def spread(value):
        if direct:
            far = range(1, tiles)
            return [value] + [sent(value, lambda p, c, t: (p, c, t ^ d)) for d in far]
        return [lax.all_gather(value, "tile")]

    def passed(terms, core):
        if not direct:
            return [swapped(lax.psum(terms, "tile"))]
        return [
            sent(terms, lambda p, c, t: (p, 1 - c, t ^ d if c == core else t))
            for d in range(tiles)
        ]

    def call(kernel, smem, operands, out_shape, scratch, name, flops=0):
        many = isinstance(out_shape, tuple)
        return pl.pallas_call(
            kernel,
            out_shape=out_shape,
            in_specs=[SMEM] * smem + [VMEM] * (len(operands) - smem),
            out_specs=(VMEM,) * len(out_shape) if many else VMEM,
            scratch_shapes=scratch,
            compiler_params=PARAMS,
            cost_estimate=pl.CostEstimate(
                flops=flops, bytes_accessed=0, transcendentals=0
            ),
            name=name,
        )(*operands)

    blocks2 = swapped(blocks)
    chunks = 8 if count % 8 == 0 else 1
    note, table, own, blocks = pl.pallas_call(
        functools.partial(head_kernel, row_blocks, chunks),
        out_shape=(
            jax.ShapeDtypeStruct((quarter + 1, slices, BS), jnp.bfloat16),
            jax.ShapeDtypeStruct((2, count), jnp.int32),
            pltpu.SMEM((3, count), jnp.int32),
            pltpu.VMEM(blocks.shape, blocks.dtype),
        ),
        in_specs=[SMEM] + [pl.BlockSpec(memory_space=pltpu.HBM)] * 4,
        out_specs=(VMEM, SMEM, SMEM, VMEM),
        scratch_shapes=[
            pltpu.SMEM(block_rows.shape, jnp.int32),
            pltpu.SMEM(block_cols.shape, jnp.int32),
            pltpu.VMEM(sinogram.shape, jnp.float32),
            pltpu.SMEM((row_blocks,), jnp.int32),
            pltpu.VMEM((row_blocks, BS, BS), jnp.float32),
            pltpu.VMEM((row_blocks, BS), jnp.float32),
            pltpu.SemaphoreType.DMA((3 + chunks,)),
        ],
        compiler_params=PARAMS,
        name="head",
    )(
        pos,
        *(
            pltpu.with_memory_space_constraint(value, pltpu.HBM)
            for value in (block_rows, block_cols, blocks, sinogram)
        ),
    )
    notes = spread(note)
    table2 = swapped(table)

    own = pltpu.with_memory_space_constraint(own, pltpu.SMEM)
    blocks2 = pltpu.with_memory_space_constraint(blocks2, pltpu.VMEM)
    wide = pl.pallas_call(
        pack_own_kernel,
        out_shape=pltpu.VMEM((row_blocks, BS, each * BS), jnp.bfloat16),
        in_specs=[SMEM, VMEM, pl.BlockSpec(memory_space=pl.ANY)],
        out_specs=VMEM,
        compiler_params=PARAMS,
        name="pack_own",
    )(own, blocks, note)
    info, tall = pl.pallas_call(
        pack_other_kernel,
        out_shape=(
            pltpu.SMEM((3, count), jnp.int32),
            pltpu.VMEM((row_blocks, each * BS, BS), jnp.bfloat16),
        ),
        in_specs=[SMEM, SMEM, VMEM],
        out_specs=(SMEM, VMEM),
        compiler_params=PARAMS,
        name="pack_other",
    )(own, table2, blocks2)
    info = pltpu.with_memory_space_constraint(info, pltpu.SMEM)

    held = []
    parts, rays = None, None
    change_out = jax.ShapeDtypeStruct(image_shape, jnp.float32)

    def updated(place, core, terms):
        return call(
            functools.partial(update_kernel, place, core, 0, len(terms)),
            1,
            [info, wide, rays] + terms,
            change_out,
            [w_scr],
            "update",
            UPDATE_FLOPS,
        )

    for place in range(places):
        last = place == places - 1
        if place == 0:
            change, rays = call(
                functools.partial(update_kernel, place, 0, len(notes), 0),
                1,
                [info, wide] + notes,
                (change_out, rays_out),
                [w_scr, rays_scr],
                "update",
                UPDATE_FLOPS,
            )
            before = []
        else:
            def hop(p, c, t):
                if p == place - 1:
                    return (place, 1, t) if c else (p, 1, t)
                if p == place:
                    return (p, 0, t) if c else (place - 1, 0, t)
                return p, 1 - c, t

            terms, image = call(
                functools.partial(project_kernel, place),
                1,
                [info] + [sent(part, hop) for part in parts] + [tall],
                (terms_out, image_out),
                [],
                "project",
            )
            change = updated(place, 0, passed(terms, 1))
            before = [swapped(image)]
        shot, terms = call(
            functools.partial(first_kernel, place),
            1,
            [info, tall, change] + before,
            (image_out, terms_out),
            [],
            "first",
        )
        change = updated(place, 1, passed(terms, 0))
        outs = call(
            functools.partial(second_kernel, place, last),
            1,
            [info, change, swapped(shot), shot] + held,
            final_out if last else (part_out, part_out, image_out),
            [],
            "second",
        )
        if last:
            return outs[None]
        parts = outs[:2]
        held = [outs[2]]


def solution(mesh):
    in_specs = (
        P("subset", "tile", None, None, None),
        P("subset", "tile", None),
        P("subset", "tile", None),
        P(None, None, ("subset", "tile")),
    )
    out_specs = P("subset", None, None, "tile")
    return jax.shard_map(
        per_device, mesh=mesh, in_specs=in_specs, out_specs=out_specs, check_vma=False
    )
```

```python
import functools

import jax
import jax.numpy as jnp
from jax import lax
from jax.experimental import pallas as pl
from jax.experimental.pallas import tpu as pltpu
from jax.sharding import PartitionSpec as P

BS = 128
PIX = 4096
CB = PIX // BS
relaxation = 0.5

UPDATE_FLOPS = 10**10

DIRECT = 4

NN = (((1,), (0,)), ((), ()))
NT = (((1,), (1,)), ((), ()))
VMEM = pl.BlockSpec(memory_space=pltpu.VMEM)
SMEM = pl.BlockSpec(memory_space=pltpu.SMEM)
PARAMS = pltpu.CompilerParams(vmem_limit_bytes=20 * 2**20)


def dot(lhs, rhs, dims):
    return lax.dot_general(lhs, rhs, dims, preferred_element_type=jnp.float32)


def head_kernel(row_blocks, chunks, pos, rows_in, cols_in, blocks_in, rays_in, *refs):
    note, table, own, blocks, rows, cols, rays, seen, squares, norms, sems = refs
    count = blocks.shape[2]
    each = count // row_blocks
    per_chunk = count // chunks
    batches, per_batch, here = rays.shape
    quarter = here // BS
    small = [
        pltpu.make_async_copy(src, dst, sems.at[i])
        for i, (src, dst) in enumerate(((rows_in, rows), (cols_in, cols), (rays_in, rays)))
    ]
    large = []
    for k in range(chunks):
        where = pl.ds(k * per_chunk, per_chunk)
        large.append(
            pltpu.make_async_copy(
                blocks_in.at[0, 0, where], blocks.at[0, 0, where], sems.at[3 + k]
            )
        )
    for copy in small + large:
        copy.start()
    squares[...] = jnp.zeros_like(squares)
    for copy in small:
        copy.wait()
    for i in range(3):
        own[0, i] = pos[i]
    for r in range(row_blocks):
        seen[r] = r * each
    for i in range(quarter):
        parts = [rays[g, :, i * BS : (i + 1) * BS] for g in range(batches)]
        note[i] = jnp.concatenate(parts, axis=0).astype(jnp.bfloat16)
    for k in range(chunks):
        large[k].wait()
        for n in range(k * per_chunk, (k + 1) * per_chunk):
            block = blocks[0, 0, n].astype(jnp.float32)
            row = rows[0, 0, n]
            squares[row] = squares[row] + block * block
            at = seen[row]
            seen[row] = at + 1
            col = cols[0, 0, n]
            for out, first in ((table, 0), (own, 1)):
                out[first, at] = n
                out[first + 1, at] = col
    ones = jnp.ones((BS, BS), jnp.bfloat16)
    on_diagonal = lax.broadcasted_iota(jnp.int32, (BS, BS), 0) == lax.broadcasted_iota(
        jnp.int32, (BS, BS), 1
    )
    for r in range(row_blocks):
        left = squares[r]
        coarse = left.astype(jnp.bfloat16)
        fine = (left - coarse.astype(jnp.float32)).astype(jnp.bfloat16)
        total = dot(coarse, ones, NN) + dot(fine, ones, NN)
        total = jnp.sum(jnp.where(on_diagonal, total, 0.0), axis=0, keepdims=True)
        norms[r : r + 1] = total
    coarse = norms[...].astype(jnp.bfloat16)
    fine = (norms[...] - coarse.astype(jnp.float32)).astype(jnp.bfloat16)
    parts = [coarse, fine]
    pad = note.shape[1] - 2 * row_blocks
    if pad:
        parts.append(jnp.zeros((pad, BS), jnp.bfloat16))
    note[quarter] = jnp.concatenate(parts, axis=0)


def pack_own_kernel(own, blocks, _, wide):
    row_blocks = wide.shape[0]
    each = wide.shape[2] // BS
    for r in range(row_blocks):
        for j in range(each):
            block = blocks[0, 0, own[1, r * each + j]]
            wide[r, :, j * BS : (j + 1) * BS] = block


def pack_other_kernel(own, table2, blocks2, info, tall):
    row_blocks = tall.shape[0]
    each = tall.shape[1] // BS
    for i in range(3):
        info[0, i] = own[0, i]
    for r in range(row_blocks):
        for j in range(each):
            k = r * each + j
            info[1, k] = own[2, k]
            info[2, k] = table2[1, k]
            block = blocks2[0, 0, table2[0, k]]
            tall[r, j * BS : (j + 1) * BS] = block.T


def gather_rays(info, notes, rays, rays_scr):
    tiles, quarter, _, _ = rays_scr.shape
    row_blocks = tiles * quarter
    if len(notes) > 1:
        parts = [ref[quarter] for ref in notes]
        for i, ref in enumerate(notes):
            rays_scr[info[0, 2] ^ i] = ref[0:quarter].astype(jnp.float32)
    else:
        parts = [notes[0][t, quarter] for t in range(tiles)]
        rays_scr[...] = notes[0][:, 0:quarter].astype(jnp.float32)
    norms = sum(part.astype(jnp.float32) for part in parts)
    scale = relaxation / (norms[0:row_blocks] + norms[row_blocks : 2 * row_blocks])
    for r in range(row_blocks):
        row = scale[r : r + 1]
        rays[r] = rays_scr[r // quarter, r % quarter] * row
        rays[row_blocks, r : r + 1] = row


def rest_of(rays, left, terms, out):
    row_blocks = out.shape[0]
    for r in range(row_blocks):
        rest = left[r]
        if terms:
            total = sum(ref[r].astype(jnp.float32) for ref in terms)
            rest = rest - total * rays[row_blocks, r : r + 1]
        out[r] = rest.astype(out.dtype)


def early_kernel(place, core, info, rays, *refs):
    terms, left = refs[:-1], refs[-1]

    @pl.when(on_core(info, place, core))
    def _():
        rest_of(rays, rays, terms, left)


def back_project(info, wide, w_scr, image):
    row_blocks = wide.shape[0]
    each = wide.shape[2] // BS
    for r in range(row_blocks):
        back = dot(w_scr[r], wide[r], NN)
        for j in range(each):
            col = info[1, r * each + j]
            image[col] = image[col] + back[:, j * BS : (j + 1) * BS]


def project(info, tall, image, terms):
    row_blocks = tall.shape[0]
    each = tall.shape[1] // BS
    for r in range(row_blocks):
        parts = [image[info[2, r * each + j]] for j in range(each)]
        total = dot(jnp.concatenate(parts, axis=1), tall[r], NN)
        terms[r] = total.astype(jnp.bfloat16)


def take(refs, n):
    taken = refs[:n]
    del refs[:n]
    return taken


def on_core(info, place, core):
    return jnp.logical_and(info[0, 0] == place, info[0, 1] == core)


def project_kernel(place, info, image, tall, terms):
    @pl.when(on_core(info, place, 1))
    def _():
        project(info, tall, image, terms)


def update_kernel(place, core, n_notes, n_terms, *refs):
    refs = list(refs)
    info, wide = take(refs, 2)
    if n_notes:
        notes, terms_in = take(refs, n_notes), []
        change, rays, w_scr, rays_scr = refs
        gather_rays(info, notes, rays, rays_scr)
        left = rays
    else:
        rays, left = take(refs, 2)
        terms_in = take(refs, n_terms)
        change, w_scr = refs

    @pl.when(on_core(info, place, core))
    def _():
        rest_of(rays, left, terms_in, w_scr)
        change[...] = jnp.zeros_like(change)
        back_project(info, wide, w_scr, change)


def first_kernel(place, *refs):
    refs = list(refs)
    info, tall, change = take(refs, 3)
    image_in = take(refs, 1)[0] if place > 0 else None
    shot, terms = refs

    @pl.when(on_core(info, place, 0))
    def _():
        value = change[...]
        if image_in is not None:
            value = value + image_in[...].astype(jnp.float32)
        shot[...] = value.astype(jnp.bfloat16)
        project(info, tall, shot, terms)


def second_kernel(place, last, *refs):
    refs = list(refs)
    info, change, image_in, shot = take(refs, 4)
    held = take(refs, 1) if place > 0 else []
    image = None if last else take(refs, 1)[0]
    (out,) = refs
    batches, per_batch, _ = out.shape

    def value(c):
        return change[c] + image_in[c].astype(jnp.float32)

    def write(source):
        for c in range(CB):
            if last:
                block = source(c).reshape(batches, per_batch, BS)
                out[:, :, c * BS : (c + 1) * BS] = block.astype(jnp.bfloat16)
            else:
                out[c] = source(c).astype(jnp.bfloat16)

    @pl.when(on_core(info, place, 1))
    def _():
        write(value)
        if not last:
            image[...] = out[...]

    @pl.when(on_core(info, place, 0))
    def _():
        write(lambda c: shot[c].astype(jnp.float32))

    if held:

        @pl.when(info[0, 0] != place)
        def _():
            write(lambda c: held[0][c].astype(jnp.float32))


def per_device(blocks, block_rows, block_cols, sinogram):
    batches, per_batch, here = sinogram.shape
    slices = batches * per_batch
    quarter = here // BS
    count = blocks.shape[2]
    subsets = lax.axis_size("subset")
    tiles = lax.axis_size("tile")
    row_blocks = quarter * tiles
    each = count // row_blocks
    places = subsets // 2
    direct = tiles <= DIRECT
    subset = lax.axis_index("subset")
    pos = jnp.stack([subset // 2, subset % 2, lax.axis_index("tile")]).astype(jnp.int32)

    image_shape = (CB, slices, BS)
    image_out = jax.ShapeDtypeStruct(image_shape, jnp.bfloat16)
    terms_out = jax.ShapeDtypeStruct((row_blocks, slices, BS), jnp.bfloat16)
    rays_out = jax.ShapeDtypeStruct((row_blocks + 1, slices, BS), jnp.float32)
    final_out = jax.ShapeDtypeStruct((batches, per_batch, PIX), jnp.bfloat16)
    w_scr = pltpu.VMEM((row_blocks, slices, BS), jnp.bfloat16)
    x_scr = pltpu.VMEM(image_shape, jnp.float32)
    rays_scr = pltpu.VMEM((tiles, quarter, slices, BS), jnp.float32)

    def sent(value, target):
        pairs = []
        for p in range(places):
            for c in range(2):
                for t in range(tiles):
                    q, e, u = target(p, c, t)
                    pairs.append(((2 * p + c) * tiles + t, (2 * q + e) * tiles + u))
        return lax.ppermute(value, ("subset", "tile"), pairs)

    def swapped(value):
        return sent(value, lambda p, c, t: (p, 1 - c, t))

    def spread(value):
        if direct:
            far = range(1, tiles)
            return [value] + [sent(value, lambda p, c, t: (p, c, t ^ d)) for d in far]
        return [lax.all_gather(value, "tile")]

    def passed(terms, core):
        if not direct:
            return [swapped(lax.psum(terms, "tile"))]
        return [
            sent(terms, lambda p, c, t: (p, 1 - c, t ^ d if c == core else t))
            for d in range(tiles)
        ]

    def call(kernel, smem, operands, out_shape, scratch, name, flops=0):
        many = isinstance(out_shape, tuple)
        return pl.pallas_call(
            kernel,
            out_shape=out_shape,
            in_specs=[SMEM] * smem + [VMEM] * (len(operands) - smem),
            out_specs=(VMEM,) * len(out_shape) if many else VMEM,
            scratch_shapes=scratch,
            compiler_params=PARAMS,
            cost_estimate=pl.CostEstimate(
                flops=flops, bytes_accessed=0, transcendentals=0
            ),
            name=name,
        )(*operands)

    blocks2 = swapped(blocks)
    chunks = 8 if count % 8 == 0 else 1
    note, table, own, blocks = pl.pallas_call(
        functools.partial(head_kernel, row_blocks, chunks),
        out_shape=(
            jax.ShapeDtypeStruct((quarter + 1, slices, BS), jnp.bfloat16),
            jax.ShapeDtypeStruct((2, count), jnp.int32),
            pltpu.SMEM((3, count), jnp.int32),
            pltpu.VMEM(blocks.shape, blocks.dtype),
        ),
        in_specs=[SMEM] + [pl.BlockSpec(memory_space=pltpu.HBM)] * 4,
        out_specs=(VMEM, SMEM, SMEM, VMEM),
        scratch_shapes=[
            pltpu.SMEM(block_rows.shape, jnp.int32),
            pltpu.SMEM(block_cols.shape, jnp.int32),
            pltpu.VMEM(sinogram.shape, jnp.float32),
            pltpu.SMEM((row_blocks,), jnp.int32),
            pltpu.VMEM((row_blocks, BS, BS), jnp.float32),
            pltpu.VMEM((row_blocks, BS), jnp.float32),
            pltpu.SemaphoreType.DMA((3 + chunks,)),
        ],
        compiler_params=PARAMS,
        name="head",
    )(
        pos,
        *(
            pltpu.with_memory_space_constraint(value, pltpu.HBM)
            for value in (block_rows, block_cols, blocks, sinogram)
        ),
    )
    notes = spread(note)
    table2 = swapped(table)

    own = pltpu.with_memory_space_constraint(own, pltpu.SMEM)
    blocks2 = pltpu.with_memory_space_constraint(blocks2, pltpu.VMEM)
    wide = pl.pallas_call(
        pack_own_kernel,
        out_shape=pltpu.VMEM((row_blocks, BS, each * BS), jnp.bfloat16),
        in_specs=[SMEM, VMEM, pl.BlockSpec(memory_space=pl.ANY)],
        out_specs=VMEM,
        compiler_params=PARAMS,
        name="pack_own",
    )(own, blocks, note)
    info, tall = pl.pallas_call(
        pack_other_kernel,
        out_shape=(
            pltpu.SMEM((3, count), jnp.int32),
            pltpu.VMEM((row_blocks, each * BS, BS), jnp.bfloat16),
        ),
        in_specs=[SMEM, SMEM, VMEM],
        out_specs=(SMEM, VMEM),
        compiler_params=PARAMS,
        name="pack_other",
    )(own, table2, blocks2)
    info = pltpu.with_memory_space_constraint(info, pltpu.SMEM)

    held = []
    image, rays = None, None
    left_out = jax.ShapeDtypeStruct((row_blocks, slices, BS), jnp.float32)
    change_out = jax.ShapeDtypeStruct(image_shape, jnp.float32)

    def updated(place, core, terms):
        left = rays
        if len(terms) > 2:
            left = call(
                functools.partial(early_kernel, place, core),
                1,
                [info, rays] + terms[1::2],
                left_out,
                [],
                "early",
            )
            terms = terms[0::2]
        return call(
            functools.partial(update_kernel, place, core, 0, len(terms)),
            1,
            [info, wide, rays, left] + terms,
            change_out,
            [w_scr],
            "update",
            UPDATE_FLOPS,
        )

    for place in range(places):
        last = place == places - 1
        if place == 0:
            change, rays = call(
                functools.partial(update_kernel, place, 0, len(notes), 0),
                1,
                [info, wide] + notes,
                (change_out, rays_out),
                [w_scr, rays_scr],
                "update",
                UPDATE_FLOPS,
            )
            before = []
        else:
            def hop(p, c, t):
                if p == place - 1:
                    return (place, 1, t) if c else (p, 1, t)
                if p == place:
                    return (p, 0, t) if c else (place - 1, 0, t)
                return p, 1 - c, t

            image = sent(image, hop)
            terms = call(
                functools.partial(project_kernel, place),
                1,
                [info, image, tall],
                terms_out,
                [],
                "project",
            )
            change = updated(place, 0, passed(terms, 1))
            before = [swapped(image)]
        shot, terms = call(
            functools.partial(first_kernel, place),
            1,
            [info, tall, change] + before,
            (image_out, terms_out),
            [],
            "first",
        )
        change = updated(place, 1, passed(terms, 0))
        outs = call(
            functools.partial(second_kernel, place, last),
            1,
            [info, change, swapped(shot), shot] + held,
            final_out if last else (image_out, image_out),
            [],
            "second",
        )
        if last:
            return outs[None]
        image = outs[0]
        held = [outs[1]]


def solution(mesh):
    in_specs = (
        P("subset", "tile", None, None, None),
        P("subset", "tile", None),
        P("subset", "tile", None),
        P(None, None, ("subset", "tile")),
    )
    out_specs = P("subset", None, None, "tile")
    return jax.shard_map(
        per_device, mesh=mesh, in_specs=in_specs, out_specs=out_specs, check_vma=False
    )
```

```python
import functools

import jax
import jax.numpy as jnp
from jax import lax
from jax.experimental import pallas as pl
from jax.experimental.pallas import tpu as pltpu
from jax.sharding import PartitionSpec as P

BS = 128
PIX = 4096
CB = PIX // BS
relaxation = 0.5

UPDATE_FLOPS = 10**10

DIRECT = 4

NN = (((1,), (0,)), ((), ()))
NT = (((1,), (1,)), ((), ()))
VMEM = pl.BlockSpec(memory_space=pltpu.VMEM)
SMEM = pl.BlockSpec(memory_space=pltpu.SMEM)
PARAMS = pltpu.CompilerParams(vmem_limit_bytes=20 * 2**20)


def dot(lhs, rhs, dims):
    return lax.dot_general(lhs, rhs, dims, preferred_element_type=jnp.float32)


def head_kernel(row_blocks, chunks, pos, rows_in, cols_in, blocks_in, rays_in, *refs):
    note, table, own, blocks, rows, cols, rays, seen, squares, norms, sems = refs
    count = blocks.shape[2]
    each = count // row_blocks
    per_chunk = count // chunks
    batches, per_batch, here = rays.shape
    quarter = here // BS
    small = [
        pltpu.make_async_copy(src, dst, sems.at[i])
        for i, (src, dst) in enumerate(((rows_in, rows), (cols_in, cols), (rays_in, rays)))
    ]
    large = []
    for k in range(chunks):
        where = pl.ds(k * per_chunk, per_chunk)
        large.append(
            pltpu.make_async_copy(
                blocks_in.at[0, 0, where], blocks.at[0, 0, where], sems.at[3 + k]
            )
        )
    for copy in small + large:
        copy.start()
    squares[...] = jnp.zeros_like(squares)
    for copy in small:
        copy.wait()
    for i in range(3):
        own[0, i] = pos[i]
    for r in range(row_blocks):
        seen[r] = r * each
    for i in range(quarter):
        parts = [rays[g, :, i * BS : (i + 1) * BS] for g in range(batches)]
        note[i] = jnp.concatenate(parts, axis=0).astype(jnp.bfloat16)
    for k in range(chunks):
        large[k].wait()
        for n in range(k * per_chunk, (k + 1) * per_chunk):
            block = blocks[0, 0, n].astype(jnp.float32)
            row = rows[0, 0, n]
            squares[row] = squares[row] + block * block
            at = seen[row]
            seen[row] = at + 1
            col = cols[0, 0, n]
            for out, first in ((table, 0), (own, 1)):
                out[first, at] = n
                out[first + 1, at] = col
    ones = jnp.ones((BS, BS), jnp.bfloat16)
    on_diagonal = lax.broadcasted_iota(jnp.int32, (BS, BS), 0) == lax.broadcasted_iota(
        jnp.int32, (BS, BS), 1
    )
    for r in range(row_blocks):
        left = squares[r]
        coarse = left.astype(jnp.bfloat16)
        fine = (left - coarse.astype(jnp.float32)).astype(jnp.bfloat16)
        total = dot(coarse, ones, NN) + dot(fine, ones, NN)
        total = jnp.sum(jnp.where(on_diagonal, total, 0.0), axis=0, keepdims=True)
        norms[r : r + 1] = total
    coarse = norms[...].astype(jnp.bfloat16)
    fine = (norms[...] - coarse.astype(jnp.float32)).astype(jnp.bfloat16)
    parts = [coarse, fine]
    pad = note.shape[1] - 2 * row_blocks
    if pad:
        parts.append(jnp.zeros((pad, BS), jnp.bfloat16))
    note[quarter] = jnp.concatenate(parts, axis=0)


def pack_own_kernel(own, blocks, _, wide):
    row_blocks = wide.shape[0]
    each = wide.shape[2] // BS
    for r in range(row_blocks):
        for j in range(each):
            block = blocks[0, 0, own[1, r * each + j]]
            wide[r, :, j * BS : (j + 1) * BS] = block


def pack_other_kernel(own, table2, blocks2, info, tall):
    row_blocks = tall.shape[0]
    each = tall.shape[1] // BS
    for i in range(3):
        info[0, i] = own[0, i]
    for r in range(row_blocks):
        for j in range(each):
            k = r * each + j
            info[1, k] = own[2, k]
            info[2, k] = table2[1, k]
            block = blocks2[0, 0, table2[0, k]]
            tall[r, j * BS : (j + 1) * BS] = block.T


def gather_rays(info, notes, rays, rays_scr):
    tiles, quarter, _, _ = rays_scr.shape
    row_blocks = tiles * quarter
    if len(notes) > 1:
        parts = [ref[quarter] for ref in notes]
        for i, ref in enumerate(notes):
            rays_scr[info[0, 2] ^ i] = ref[0:quarter].astype(jnp.float32)
    else:
        parts = [notes[0][t, quarter] for t in range(tiles)]
        rays_scr[...] = notes[0][:, 0:quarter].astype(jnp.float32)
    norms = sum(part.astype(jnp.float32) for part in parts)
    scale = relaxation / (norms[0:row_blocks] + norms[row_blocks : 2 * row_blocks])
    for r in range(row_blocks):
        row = scale[r : r + 1]
        rays[r] = rays_scr[r // quarter, r % quarter] * row
        rays[row_blocks, r : r + 1] = row


def weights(rays, terms, w_scr):
    row_blocks = w_scr.shape[0]
    for r in range(row_blocks):
        left = rays[r]
        if terms:
            total = sum(ref[r].astype(jnp.float32) for ref in terms)
            left = left - total * rays[row_blocks, r : r + 1]
        w_scr[r] = left.astype(jnp.bfloat16)


def back_project(info, wide, w_scr, image):
    row_blocks = wide.shape[0]
    each = wide.shape[2] // BS
    for r in range(row_blocks):
        back = dot(w_scr[r], wide[r], NN)
        for j in range(each):
            col = info[1, r * each + j]
            image[col] = image[col] + back[:, j * BS : (j + 1) * BS]


def project(info, tall, image, terms):
    row_blocks = tall.shape[0]
    each = tall.shape[1] // BS
    for r in range(row_blocks):
        parts = [image[info[2, r * each + j]] for j in range(each)]
        total = dot(jnp.concatenate(parts, axis=1), tall[r], NN)
        terms[r] = total.astype(jnp.bfloat16)


def take(refs, n):
    taken = refs[:n]
    del refs[:n]
    return taken


def on_core(info, place, core):
    return jnp.logical_and(info[0, 0] == place, info[0, 1] == core)


def project_kernel(place, info, image, tall, terms):
    @pl.when(on_core(info, place, 1))
    def _():
        project(info, tall, image, terms)


def update_kernel(place, core, n_notes, n_terms, *refs):
    refs = list(refs)
    info, wide = take(refs, 2)
    if n_notes:
        notes, terms_in = take(refs, n_notes), []
        change, rays, w_scr, rays_scr = refs
        gather_rays(info, notes, rays, rays_scr)
    else:
        (rays,) = take(refs, 1)
        terms_in = take(refs, n_terms)
        change, w_scr = refs

    @pl.when(on_core(info, place, core))
    def _():
        weights(rays, terms_in, w_scr)
        change[...] = jnp.zeros_like(change)
        back_project(info, wide, w_scr, change)


def first_kernel(place, *refs):
    refs = list(refs)
    info, tall, change = take(refs, 3)
    image_in = take(refs, 1)[0] if place > 0 else None
    shot, terms = refs

    @pl.when(on_core(info, place, 0))
    def _():
        value = change[...]
        if image_in is not None:
            value = value + image_in[...].astype(jnp.float32)
        shot[...] = value.astype(jnp.bfloat16)
        project(info, tall, shot, terms)


def second_kernel(place, last, *refs):
    refs = list(refs)
    info, change, image_in, shot = take(refs, 4)
    held = take(refs, 1) if place > 0 else []
    sink, sems, image = None, None, None
    if last:
        sink, out, sems = refs
    else:
        image, out = refs
    batches, per_batch, _ = out.shape

    def value(where):
        return change[where] + image_in[where].astype(jnp.float32)

    def write(source):
        if not last:
            for c in range(CB):
                out[c] = source(c).astype(jnp.bfloat16)
            return
        parts = 2 if batches % 2 == 0 and batches * per_batch % 32 == 0 else 1
        group = batches // parts
        copies = []
        for g in range(parts):
            rows = slice(g * group * per_batch, (g + 1) * group * per_batch)
            mine = slice(g * group, (g + 1) * group)
            for c in range(CB):
                block = source((c, rows)).reshape(group, per_batch, BS)
                out[mine, :, c * BS : (c + 1) * BS] = block.astype(jnp.bfloat16)
            where = pl.ds(g * group, group)
            copies.append(pltpu.make_async_copy(out.at[where], sink.at[where], sems.at[g]))
            copies[-1].start()
        for copy in copies:
            copy.wait()

    @pl.when(on_core(info, place, 1))
    def _():
        write(value)
        if not last:
            image[...] = out[...]

    @pl.when(on_core(info, place, 0))
    def _():
        write(lambda where: shot[where].astype(jnp.float32))

    if held:

        @pl.when(info[0, 0] != place)
        def _():
            write(lambda where: held[0][where].astype(jnp.float32))


def per_device(blocks, block_rows, block_cols, sinogram):
    batches, per_batch, here = sinogram.shape
    slices = batches * per_batch
    quarter = here // BS
    count = blocks.shape[2]
    subsets = lax.axis_size("subset")
    tiles = lax.axis_size("tile")
    row_blocks = quarter * tiles
    each = count // row_blocks
    places = subsets // 2
    direct = tiles <= DIRECT
    subset = lax.axis_index("subset")
    pos = jnp.stack([subset // 2, subset % 2, lax.axis_index("tile")]).astype(jnp.int32)

    image_shape = (CB, slices, BS)
    image_out = jax.ShapeDtypeStruct(image_shape, jnp.bfloat16)
    terms_out = jax.ShapeDtypeStruct((row_blocks, slices, BS), jnp.bfloat16)
    rays_out = jax.ShapeDtypeStruct((row_blocks + 1, slices, BS), jnp.float32)
    final_out = jax.ShapeDtypeStruct((batches, per_batch, PIX), jnp.bfloat16)
    w_scr = pltpu.VMEM((row_blocks, slices, BS), jnp.bfloat16)
    x_scr = pltpu.VMEM(image_shape, jnp.float32)
    rays_scr = pltpu.VMEM((tiles, quarter, slices, BS), jnp.float32)

    def sent(value, target):
        pairs = []
        for p in range(places):
            for c in range(2):
                for t in range(tiles):
                    q, e, u = target(p, c, t)
                    pairs.append(((2 * p + c) * tiles + t, (2 * q + e) * tiles + u))
        return lax.ppermute(value, ("subset", "tile"), pairs)

    def swapped(value):
        return sent(value, lambda p, c, t: (p, 1 - c, t))

    def spread(value):
        if direct:
            far = range(1, tiles)
            return [value] + [sent(value, lambda p, c, t: (p, c, t ^ d)) for d in far]
        return [lax.all_gather(value, "tile")]

    def passed(terms, core):
        if not direct:
            return [swapped(lax.psum(terms, "tile"))]
        return [
            sent(terms, lambda p, c, t: (p, 1 - c, t ^ d if c == core else t))
            for d in range(tiles)
        ]

    def call(kernel, smem, operands, out_shape, scratch, name, flops=0):
        many = isinstance(out_shape, tuple)
        return pl.pallas_call(
            kernel,
            out_shape=out_shape,
            in_specs=[SMEM] * smem + [VMEM] * (len(operands) - smem),
            out_specs=(VMEM,) * len(out_shape) if many else VMEM,
            scratch_shapes=scratch,
            compiler_params=PARAMS,
            cost_estimate=pl.CostEstimate(
                flops=flops, bytes_accessed=0, transcendentals=0
            ),
            name=name,
        )(*operands)

    blocks2 = swapped(blocks)
    chunks = 8 if count % 8 == 0 else 1
    note, table, own, blocks = pl.pallas_call(
        functools.partial(head_kernel, row_blocks, chunks),
        out_shape=(
            jax.ShapeDtypeStruct((quarter + 1, slices, BS), jnp.bfloat16),
            jax.ShapeDtypeStruct((2, count), jnp.int32),
            pltpu.SMEM((3, count), jnp.int32),
            pltpu.VMEM(blocks.shape, blocks.dtype),
        ),
        in_specs=[SMEM] + [pl.BlockSpec(memory_space=pltpu.HBM)] * 4,
        out_specs=(VMEM, SMEM, SMEM, VMEM),
        scratch_shapes=[
            pltpu.SMEM(block_rows.shape, jnp.int32),
            pltpu.SMEM(block_cols.shape, jnp.int32),
            pltpu.VMEM(sinogram.shape, jnp.float32),
            pltpu.SMEM((row_blocks,), jnp.int32),
            pltpu.VMEM((row_blocks, BS, BS), jnp.float32),
            pltpu.VMEM((row_blocks, BS), jnp.float32),
            pltpu.SemaphoreType.DMA((3 + chunks,)),
        ],
        compiler_params=PARAMS,
        name="head",
    )(
        pos,
        *(
            pltpu.with_memory_space_constraint(value, pltpu.HBM)
            for value in (block_rows, block_cols, blocks, sinogram)
        ),
    )
    notes = spread(note)
    table2 = swapped(table)

    own = pltpu.with_memory_space_constraint(own, pltpu.SMEM)
    blocks2 = pltpu.with_memory_space_constraint(blocks2, pltpu.VMEM)
    wide = pl.pallas_call(
        pack_own_kernel,
        out_shape=pltpu.VMEM((row_blocks, BS, each * BS), jnp.bfloat16),
        in_specs=[SMEM, VMEM, pl.BlockSpec(memory_space=pl.ANY)],
        out_specs=VMEM,
        compiler_params=PARAMS,
        name="pack_own",
    )(own, blocks, note)
    info, tall = pl.pallas_call(
        pack_other_kernel,
        out_shape=(
            pltpu.SMEM((3, count), jnp.int32),
            pltpu.VMEM((row_blocks, each * BS, BS), jnp.bfloat16),
        ),
        in_specs=[SMEM, SMEM, VMEM],
        out_specs=(SMEM, VMEM),
        compiler_params=PARAMS,
        name="pack_other",
    )(own, table2, blocks2)
    info = pltpu.with_memory_space_constraint(info, pltpu.SMEM)

    held = []
    image, rays = None, None
    change_out = jax.ShapeDtypeStruct(image_shape, jnp.float32)

    def updated(place, core, terms):
        return call(
            functools.partial(update_kernel, place, core, 0, len(terms)),
            1,
            [info, wide, rays] + terms,
            change_out,
            [w_scr],
            "update",
            UPDATE_FLOPS,
        )

    for place in range(places):
        last = place == places - 1
        if place == 0:
            change, rays = call(
                functools.partial(update_kernel, place, 0, len(notes), 0),
                1,
                [info, wide] + notes,
                (change_out, rays_out),
                [w_scr, rays_scr],
                "update",
                UPDATE_FLOPS,
            )
            before = []
        else:
            def hop(p, c, t):
                if p == place - 1:
                    return (place, 1, t) if c else (p, 1, t)
                if p == place:
                    return (p, 0, t) if c else (place - 1, 0, t)
                return p, 1 - c, t

            image = sent(image, hop)
            terms = call(
                functools.partial(project_kernel, place),
                1,
                [info, image, tall],
                terms_out,
                [],
                "project",
            )
            change = updated(place, 0, passed(terms, 1))
            before = [swapped(image)]
        shot, terms = call(
            functools.partial(first_kernel, place),
            1,
            [info, tall, change] + before,
            (image_out, terms_out),
            [],
            "first",
        )
        change = updated(place, 1, passed(terms, 0))
        operands = [info, change, swapped(shot), shot] + held
        if last:
            images = pl.pallas_call(
                functools.partial(second_kernel, place, last),
                out_shape=final_out,
                in_specs=[SMEM] + [VMEM] * (len(operands) - 1),
                out_specs=pl.BlockSpec(memory_space=pl.ANY),
                scratch_shapes=[
                    pltpu.VMEM(final_out.shape, jnp.bfloat16),
                    pltpu.SemaphoreType.DMA((2,)),
                ],
                compiler_params=PARAMS,
                name="second",
            )(*operands)
            return images[None]
        outs = call(
            functools.partial(second_kernel, place, last),
            1,
            operands,
            (image_out, image_out),
            [],
            "second",
        )
        image = outs[0]
        held = [outs[1]]


def solution(mesh):
    in_specs = (
        P("subset", "tile", None, None, None),
        P("subset", "tile", None),
        P("subset", "tile", None),
        P(None, None, ("subset", "tile")),
    )
    out_specs = P("subset", None, None, "tile")
    return jax.shard_map(
        per_device, mesh=mesh, in_specs=in_specs, out_specs=out_specs, check_vma=False
    )
```

```python
import functools

import jax
import jax.numpy as jnp
from jax import lax
from jax.experimental import pallas as pl
from jax.experimental.pallas import tpu as pltpu
from jax.sharding import PartitionSpec as P

BS = 128
PIX = 4096
CB = PIX // BS
relaxation = 0.5

UPDATE_FLOPS = 10**10

DIRECT = 4

NN = (((1,), (0,)), ((), ()))
NT = (((1,), (1,)), ((), ()))
VMEM = pl.BlockSpec(memory_space=pltpu.VMEM)
SMEM = pl.BlockSpec(memory_space=pltpu.SMEM)
PARAMS = pltpu.CompilerParams(vmem_limit_bytes=20 * 2**20)


def dot(lhs, rhs, dims):
    return lax.dot_general(lhs, rhs, dims, preferred_element_type=jnp.float32)


def head_kernel(row_blocks, chunks, pos, rows_in, cols_in, blocks_in, rays_in, *refs):
    note, table, own, blocks, rows, cols, rays, seen, norms, sems = refs
    count = blocks.shape[2]
    each = count // row_blocks
    per_chunk = count // chunks
    batches, per_batch, here = rays.shape
    quarter = here // BS
    small = [
        pltpu.make_async_copy(src, dst, sems.at[i])
        for i, (src, dst) in enumerate(((rows_in, rows), (cols_in, cols), (rays_in, rays)))
    ]
    large = []
    for k in range(chunks):
        where = pl.ds(k * per_chunk, per_chunk)
        large.append(
            pltpu.make_async_copy(
                blocks_in.at[0, 0, where], blocks.at[0, 0, where], sems.at[3 + k]
            )
        )
    for copy in small + large:
        copy.start()
    for copy in small:
        copy.wait()
    for i in range(3):
        own[0, i] = pos[i]
    for r in range(row_blocks):
        seen[r] = r * each
    for i in range(quarter):
        parts = [rays[g, :, i * BS : (i + 1) * BS] for g in range(batches)]
        note[i] = jnp.concatenate(parts, axis=0).astype(jnp.bfloat16)
    for n in range(count):
        row = rows[0, 0, n]
        at = seen[row]
        seen[row] = at + 1
        col = cols[0, 0, n]
        for out, first in ((table, 0), (own, 1)):
            out[first, at] = n
            out[first + 1, at] = col
    for copy in large:
        copy.wait()
    ones = jnp.ones((BS, BS), jnp.bfloat16)
    on_diagonal = lax.broadcasted_iota(jnp.int32, (BS, BS), 0) == lax.broadcasted_iota(
        jnp.int32, (BS, BS), 1
    )
    for r in range(row_blocks):
        left = 0.0
        for k in range(r * each, (r + 1) * each):
            block = blocks[0, 0, own[1, k]].astype(jnp.float32)
            left = left + block * block
        coarse = left.astype(jnp.bfloat16)
        fine = (left - coarse.astype(jnp.float32)).astype(jnp.bfloat16)
        total = dot(coarse, ones, NN) + dot(fine, ones, NN)
        total = jnp.sum(jnp.where(on_diagonal, total, 0.0), axis=0, keepdims=True)
        norms[r : r + 1] = total
    coarse = norms[...].astype(jnp.bfloat16)
    fine = (norms[...] - coarse.astype(jnp.float32)).astype(jnp.bfloat16)
    parts = [coarse, fine]
    pad = note.shape[1] - 2 * row_blocks
    if pad:
        parts.append(jnp.zeros((pad, BS), jnp.bfloat16))
    note[quarter] = jnp.concatenate(parts, axis=0)


def pack_own_kernel(own, blocks, _, wide):
    row_blocks = wide.shape[0]
    each = wide.shape[2] // BS
    for r in range(row_blocks):
        for j in range(each):
            block = blocks[0, 0, own[1, r * each + j]]
            wide[r, :, j * BS : (j + 1) * BS] = block


def pack_other_kernel(own, table2, blocks2, info, tall):
    row_blocks = tall.shape[0]
    each = tall.shape[1] // BS
    for i in range(3):
        info[0, i] = own[0, i]
    for r in range(row_blocks):
        for j in range(each):
            k = r * each + j
            info[1, k] = own[2, k]
            info[2, k] = table2[1, k]
            block = blocks2[0, 0, table2[0, k]]
            tall[r, j * BS : (j + 1) * BS] = block.T


def gather_rays(info, notes, rays, rays_scr):
    tiles, quarter, _, _ = rays_scr.shape
    row_blocks = tiles * quarter
    if len(notes) > 1:
        parts = [ref[quarter] for ref in notes]
        for i, ref in enumerate(notes):
            rays_scr[info[0, 2] ^ i] = ref[0:quarter].astype(jnp.float32)
    else:
        parts = [notes[0][t, quarter] for t in range(tiles)]
        rays_scr[...] = notes[0][:, 0:quarter].astype(jnp.float32)
    norms = sum(part.astype(jnp.float32) for part in parts)
    scale = relaxation / (norms[0:row_blocks] + norms[row_blocks : 2 * row_blocks])
    for r in range(row_blocks):
        row = scale[r : r + 1]
        rays[r] = rays_scr[r // quarter, r % quarter] * row
        rays[row_blocks, r : r + 1] = row


def weights(rays, terms, w_scr):
    row_blocks = w_scr.shape[0]
    for r in range(row_blocks):
        left = rays[r]
        if terms:
            total = sum(ref[r].astype(jnp.float32) for ref in terms)
            left = left - total * rays[row_blocks, r : r + 1]
        w_scr[r] = left.astype(jnp.bfloat16)


def back_project(info, wide, w_scr, image):
    row_blocks = wide.shape[0]
    each = wide.shape[2] // BS
    for r in range(row_blocks):
        back = dot(w_scr[r], wide[r], NN)
        for j in range(each):
            col = info[1, r * each + j]
            image[col] = image[col] + back[:, j * BS : (j + 1) * BS]


def project(info, tall, image, terms):
    row_blocks = tall.shape[0]
    each = tall.shape[1] // BS
    for r in range(row_blocks):
        parts = [image[info[2, r * each + j]] for j in range(each)]
        total = dot(jnp.concatenate(parts, axis=1), tall[r], NN)
        terms[r] = total.astype(jnp.bfloat16)


def take(refs, n):
    taken = refs[:n]
    del refs[:n]
    return taken


def on_core(info, place, core):
    return jnp.logical_and(info[0, 0] == place, info[0, 1] == core)


def project_kernel(place, info, image, tall, terms):
    @pl.when(on_core(info, place, 1))
    def _():
        project(info, tall, image, terms)


def update_kernel(place, core, n_notes, n_terms, *refs):
    refs = list(refs)
    info, wide = take(refs, 2)
    if n_notes:
        notes, terms_in = take(refs, n_notes), []
        change, rays, w_scr, rays_scr = refs
        gather_rays(info, notes, rays, rays_scr)
    else:
        (rays,) = take(refs, 1)
        terms_in = take(refs, n_terms)
        change, w_scr = refs

    @pl.when(on_core(info, place, core))
    def _():
        weights(rays, terms_in, w_scr)
        change[...] = jnp.zeros_like(change)
        back_project(info, wide, w_scr, change)


def first_kernel(place, *refs):
    refs = list(refs)
    info, tall, change = take(refs, 3)
    image_in = take(refs, 1)[0] if place > 0 else None
    shot, terms = refs

    @pl.when(on_core(info, place, 0))
    def _():
        value = change[...]
        if image_in is not None:
            value = value + image_in[...].astype(jnp.float32)
        shot[...] = value.astype(jnp.bfloat16)
        project(info, tall, shot, terms)


def second_kernel(place, last, *refs):
    refs = list(refs)
    info, change, image_in, shot = take(refs, 4)
    held = take(refs, 1) if place > 0 else []
    image = None if last else take(refs, 1)[0]
    (out,) = refs
    batches, per_batch, _ = out.shape

    def value(c):
        return change[c] + image_in[c].astype(jnp.float32)

    def write(source):
        for c in range(CB):
            if last:
                block = source(c).reshape(batches, per_batch, BS)
                out[:, :, c * BS : (c + 1) * BS] = block.astype(jnp.bfloat16)
            else:
                out[c] = source(c).astype(jnp.bfloat16)

    @pl.when(on_core(info, place, 1))
    def _():
        write(value)
        if not last:
            image[...] = out[...]

    @pl.when(on_core(info, place, 0))
    def _():
        write(lambda c: shot[c].astype(jnp.float32))

    if held:

        @pl.when(info[0, 0] != place)
        def _():
            write(lambda c: held[0][c].astype(jnp.float32))


def per_device(blocks, block_rows, block_cols, sinogram):
    batches, per_batch, here = sinogram.shape
    slices = batches * per_batch
    quarter = here // BS
    count = blocks.shape[2]
    subsets = lax.axis_size("subset")
    tiles = lax.axis_size("tile")
    row_blocks = quarter * tiles
    each = count // row_blocks
    places = subsets // 2
    direct = tiles <= DIRECT
    subset = lax.axis_index("subset")
    pos = jnp.stack([subset // 2, subset % 2, lax.axis_index("tile")]).astype(jnp.int32)

    image_shape = (CB, slices, BS)
    image_out = jax.ShapeDtypeStruct(image_shape, jnp.bfloat16)
    terms_out = jax.ShapeDtypeStruct((row_blocks, slices, BS), jnp.bfloat16)
    rays_out = jax.ShapeDtypeStruct((row_blocks + 1, slices, BS), jnp.float32)
    final_out = jax.ShapeDtypeStruct((batches, per_batch, PIX), jnp.bfloat16)
    w_scr = pltpu.VMEM((row_blocks, slices, BS), jnp.bfloat16)
    x_scr = pltpu.VMEM(image_shape, jnp.float32)
    rays_scr = pltpu.VMEM((tiles, quarter, slices, BS), jnp.float32)

    def sent(value, target):
        pairs = []
        for p in range(places):
            for c in range(2):
                for t in range(tiles):
                    q, e, u = target(p, c, t)
                    pairs.append(((2 * p + c) * tiles + t, (2 * q + e) * tiles + u))
        return lax.ppermute(value, ("subset", "tile"), pairs)

    def swapped(value):
        return sent(value, lambda p, c, t: (p, 1 - c, t))

    def spread(value):
        if direct:
            far = range(1, tiles)
            return [value] + [sent(value, lambda p, c, t: (p, c, t ^ d)) for d in far]
        return [lax.all_gather(value, "tile")]

    def passed(terms, core):
        if not direct:
            return [swapped(lax.psum(terms, "tile"))]
        return [
            sent(terms, lambda p, c, t: (p, 1 - c, t ^ d if c == core else t))
            for d in range(tiles)
        ]

    def call(kernel, smem, operands, out_shape, scratch, name, flops=0):
        many = isinstance(out_shape, tuple)
        return pl.pallas_call(
            kernel,
            out_shape=out_shape,
            in_specs=[SMEM] * smem + [VMEM] * (len(operands) - smem),
            out_specs=(VMEM,) * len(out_shape) if many else VMEM,
            scratch_shapes=scratch,
            compiler_params=PARAMS,
            cost_estimate=pl.CostEstimate(
                flops=flops, bytes_accessed=0, transcendentals=0
            ),
            name=name,
        )(*operands)

    blocks2 = swapped(blocks)
    chunks = 8 if count % 8 == 0 else 1
    note, table, own, blocks = pl.pallas_call(
        functools.partial(head_kernel, row_blocks, chunks),
        out_shape=(
            jax.ShapeDtypeStruct((quarter + 1, slices, BS), jnp.bfloat16),
            jax.ShapeDtypeStruct((2, count), jnp.int32),
            pltpu.SMEM((3, count), jnp.int32),
            pltpu.VMEM(blocks.shape, blocks.dtype),
        ),
        in_specs=[SMEM] + [pl.BlockSpec(memory_space=pltpu.HBM)] * 4,
        out_specs=(VMEM, SMEM, SMEM, VMEM),
        scratch_shapes=[
            pltpu.SMEM(block_rows.shape, jnp.int32),
            pltpu.SMEM(block_cols.shape, jnp.int32),
            pltpu.VMEM(sinogram.shape, jnp.float32),
            pltpu.SMEM((row_blocks,), jnp.int32),
            pltpu.VMEM((row_blocks, BS), jnp.float32),
            pltpu.SemaphoreType.DMA((3 + chunks,)),
        ],
        compiler_params=PARAMS,
        name="head",
    )(
        pos,
        *(
            pltpu.with_memory_space_constraint(value, pltpu.HBM)
            for value in (block_rows, block_cols, blocks, sinogram)
        ),
    )
    notes = spread(note)
    table2 = swapped(table)

    own = pltpu.with_memory_space_constraint(own, pltpu.SMEM)
    blocks2 = pltpu.with_memory_space_constraint(blocks2, pltpu.VMEM)
    wide = pl.pallas_call(
        pack_own_kernel,
        out_shape=pltpu.VMEM((row_blocks, BS, each * BS), jnp.bfloat16),
        in_specs=[SMEM, VMEM, pl.BlockSpec(memory_space=pl.ANY)],
        out_specs=VMEM,
        compiler_params=PARAMS,
        name="pack_own",
    )(own, blocks, note)
    info, tall = pl.pallas_call(
        pack_other_kernel,
        out_shape=(
            pltpu.SMEM((3, count), jnp.int32),
            pltpu.VMEM((row_blocks, each * BS, BS), jnp.bfloat16),
        ),
        in_specs=[SMEM, SMEM, VMEM],
        out_specs=(SMEM, VMEM),
        compiler_params=PARAMS,
        name="pack_other",
    )(own, table2, blocks2)
    info = pltpu.with_memory_space_constraint(info, pltpu.SMEM)

    held = []
    image, rays = None, None
    change_out = jax.ShapeDtypeStruct(image_shape, jnp.float32)

    def updated(place, core, terms):
        return call(
            functools.partial(update_kernel, place, core, 0, len(terms)),
            1,
            [info, wide, rays] + terms,
            change_out,
            [w_scr],
            "update",
            UPDATE_FLOPS,
        )

    for place in range(places):
        last = place == places - 1
        if place == 0:
            change, rays = call(
                functools.partial(update_kernel, place, 0, len(notes), 0),
                1,
                [info, wide] + notes,
                (change_out, rays_out),
                [w_scr, rays_scr],
                "update",
                UPDATE_FLOPS,
            )
            before = []
        else:
            def hop(p, c, t):
                if p == place - 1:
                    return (place, 1, t) if c else (p, 1, t)
                if p == place:
                    return (p, 0, t) if c else (place - 1, 0, t)
                return p, 1 - c, t

            image = sent(image, hop)
            terms = call(
                functools.partial(project_kernel, place),
                1,
                [info, image, tall],
                terms_out,
                [],
                "project",
            )
            change = updated(place, 0, passed(terms, 1))
            before = [swapped(image)]
        shot, terms = call(
            functools.partial(first_kernel, place),
            1,
            [info, tall, change] + before,
            (image_out, terms_out),
            [],
            "first",
        )
        change = updated(place, 1, passed(terms, 0))
        outs = call(
            functools.partial(second_kernel, place, last),
            1,
            [info, change, swapped(shot), shot] + held,
            final_out if last else (image_out, image_out),
            [],
            "second",
        )
        if last:
            return outs[None]
        image = outs[0]
        held = [outs[1]]


def solution(mesh):
    in_specs = (
        P("subset", "tile", None, None, None),
        P("subset", "tile", None),
        P("subset", "tile", None),
        P(None, None, ("subset", "tile")),
    )
    out_specs = P("subset", None, None, "tile")
    return jax.shard_map(
        per_device, mesh=mesh, in_specs=in_specs, out_specs=out_specs, check_vma=False
    )
```

```python
import functools

import jax
import jax.numpy as jnp
from jax import lax
from jax.experimental import pallas as pl
from jax.experimental.pallas import tpu as pltpu
from jax.sharding import PartitionSpec as P

BS = 128
PIX = 4096
CB = PIX // BS
relaxation = 0.5

UPDATE_FLOPS = 10**10

DIRECT = 4

NN = (((1,), (0,)), ((), ()))
NT = (((1,), (1,)), ((), ()))
VMEM = pl.BlockSpec(memory_space=pltpu.VMEM)
SMEM = pl.BlockSpec(memory_space=pltpu.SMEM)
PARAMS = pltpu.CompilerParams(vmem_limit_bytes=20 * 2**20)


def dot(lhs, rhs, dims):
    return lax.dot_general(lhs, rhs, dims, preferred_element_type=jnp.float32)


def head_kernel(row_blocks, chunks, pos, rows_in, cols_in, blocks_in, rays_in, *refs):
    note, table, own, blocks, rows, cols, rays, seen, squares, norms, sems = refs
    count = blocks.shape[2]
    each = count // row_blocks
    per_chunk = count // chunks
    batches, per_batch, here = rays.shape
    quarter = here // BS
    small = [
        pltpu.make_async_copy(src, dst, sems.at[i])
        for i, (src, dst) in enumerate(((rows_in, rows), (cols_in, cols), (rays_in, rays)))
    ]
    large = []
    for k in range(chunks):
        where = pl.ds(k * per_chunk, per_chunk)
        large.append(
            pltpu.make_async_copy(
                blocks_in.at[0, 0, where], blocks.at[0, 0, where], sems.at[3 + k]
            )
        )
    for copy in small + large:
        copy.start()
    squares[...] = jnp.zeros_like(squares)
    for copy in small:
        copy.wait()
    for i in range(3):
        own[0, i] = pos[i]
    for r in range(row_blocks):
        seen[r] = r * each
    for i in range(quarter):
        parts = [rays[g, :, i * BS : (i + 1) * BS] for g in range(batches)]
        note[i] = jnp.concatenate(parts, axis=0).astype(jnp.bfloat16)
    for k in range(chunks):
        large[k].wait()
        for n in range(k * per_chunk, (k + 1) * per_chunk):
            block = blocks[0, 0, n].astype(jnp.float32)
            row = rows[0, 0, n]
            squares[row] = squares[row] + block * block
            at = seen[row]
            seen[row] = at + 1
            col = cols[0, 0, n]
            for out, first in ((table, 0), (own, 1)):
                out[first, at] = n
                out[first + 1, at] = col
    ones = jnp.ones((BS, BS), jnp.bfloat16)
    on_diagonal = lax.broadcasted_iota(jnp.int32, (BS, BS), 0) == lax.broadcasted_iota(
        jnp.int32, (BS, BS), 1
    )
    for r in range(row_blocks):
        left = squares[r]
        coarse = left.astype(jnp.bfloat16)
        fine = (left - coarse.astype(jnp.float32)).astype(jnp.bfloat16)
        total = dot(coarse, ones, NN) + dot(fine, ones, NN)
        total = jnp.sum(jnp.where(on_diagonal, total, 0.0), axis=0, keepdims=True)
        norms[r : r + 1] = total
    coarse = norms[...].astype(jnp.bfloat16)
    fine = (norms[...] - coarse.astype(jnp.float32)).astype(jnp.bfloat16)
    parts = [coarse, fine]
    pad = note.shape[1] - 2 * row_blocks
    if pad:
        parts.append(jnp.zeros((pad, BS), jnp.bfloat16))
    note[quarter] = jnp.concatenate(parts, axis=0)


def pack_own_kernel(own, blocks, _, wide):
    row_blocks = wide.shape[0]
    each = wide.shape[2] // BS
    for r in range(row_blocks):
        for j in range(each):
            block = blocks[0, 0, own[1, r * each + j]]
            wide[r, :, j * BS : (j + 1) * BS] = block


def pack_other_kernel(own, table2, blocks2, info, tall):
    row_blocks = tall.shape[0]
    each = tall.shape[1] // BS
    for i in range(3):
        info[0, i] = own[0, i]
    for r in range(row_blocks):
        for j in range(each):
            k = r * each + j
            info[1, k] = own[2, k]
            info[2, k] = table2[1, k]
            block = blocks2[0, 0, table2[0, k]]
            tall[r, j * BS : (j + 1) * BS] = block.T


def gather_rays(info, notes, rays, rays_scr):
    tiles, quarter, _, _ = rays_scr.shape
    row_blocks = tiles * quarter
    if len(notes) > 1:
        parts = [ref[quarter] for ref in notes]
        for i, ref in enumerate(notes):
            rays_scr[info[0, 2] ^ i] = ref[0:quarter].astype(jnp.float32)
    else:
        parts = [notes[0][t, quarter] for t in range(tiles)]
        rays_scr[...] = notes[0][:, 0:quarter].astype(jnp.float32)
    norms = sum(part.astype(jnp.float32) for part in parts)
    scale = relaxation / (norms[0:row_blocks] + norms[row_blocks : 2 * row_blocks])
    for r in range(row_blocks):
        row = scale[r : r + 1]
        rays[r] = rays_scr[r // quarter, r % quarter] * row
        rays[row_blocks, r : r + 1] = row


def weights(rays, terms, w_scr):
    row_blocks = w_scr.shape[0]
    for r in range(row_blocks):
        left = rays[r]
        if terms:
            total = sum(ref[r].astype(jnp.float32) for ref in terms)
            left = left - total * rays[row_blocks, r : r + 1]
        w_scr[r] = left.astype(jnp.bfloat16)


def back_project(info, wide, w_scr, image):
    row_blocks = wide.shape[0]
    each = wide.shape[2] // BS
    for r in range(row_blocks):
        back = dot(w_scr[r], wide[r], NN)
        for j in range(each):
            col = info[1, r * each + j]
            image[col] = image[col] + back[:, j * BS : (j + 1) * BS]


def project(info, tall, image, terms):
    row_blocks = tall.shape[0]
    each = tall.shape[1] // BS
    for r in range(row_blocks):
        parts = [image[info[2, r * each + j]] for j in range(each)]
        total = dot(jnp.concatenate(parts, axis=1), tall[r], NN)
        terms[r] = total.astype(jnp.bfloat16)


def take(refs, n):
    taken = refs[:n]
    del refs[:n]
    return taken


def on_core(info, place, core):
    return jnp.logical_and(info[0, 0] == place, info[0, 1] == core)


def project_kernel(place, info, image, tall, terms):
    @pl.when(on_core(info, place, 1))
    def _():
        project(info, tall, image, terms)


def update_kernel(place, core, n_notes, n_terms, *refs):
    refs = list(refs)
    info, wide = take(refs, 2)
    if n_notes:
        notes, terms_in = take(refs, n_notes), []
        change, rays, w_scr, rays_scr = refs
        gather_rays(info, notes, rays, rays_scr)
    else:
        (rays,) = take(refs, 1)
        terms_in = take(refs, n_terms)
        change, w_scr = refs

    @pl.when(on_core(info, place, core))
    def _():
        weights(rays, terms_in, w_scr)
        change[...] = jnp.zeros_like(change)
        back_project(info, wide, w_scr, change)


def first_kernel(place, *refs):
    refs = list(refs)
    info, tall, change = take(refs, 3)
    image_in = take(refs, 1)[0] if place > 0 else None
    shot, terms = refs

    @pl.when(on_core(info, place, 0))
    def _():
        value = change[...]
        if image_in is not None:
            value = value + image_in[...].astype(jnp.float32)
        shot[...] = value.astype(jnp.bfloat16)
        project(info, tall, shot, terms)


def second_kernel(place, last, *refs):
    refs = list(refs)
    info, change, image_in, shot = take(refs, 4)
    held = take(refs, 1) if place > 0 else []
    image = None if last else take(refs, 1)[0]
    (out,) = refs
    batches, per_batch, _ = out.shape

    def value(c):
        return change[c] + image_in[c].astype(jnp.float32)

    def write(source):
        for c in range(CB):
            if last:
                block = source(c).reshape(batches, per_batch, BS)
                out[:, :, c * BS : (c + 1) * BS] = block.astype(jnp.bfloat16)
            else:
                out[c] = source(c).astype(jnp.bfloat16)

    @pl.when(on_core(info, place, 1))
    def _():
        write(value)
        if not last:
            image[...] = out[...]

    @pl.when(on_core(info, place, 0))
    def _():
        write(lambda c: shot[c].astype(jnp.float32))

    if held:

        @pl.when(info[0, 0] != place)
        def _():
            write(lambda c: held[0][c].astype(jnp.float32))


def per_device(blocks, block_rows, block_cols, sinogram):
    batches, per_batch, here = sinogram.shape
    slices = batches * per_batch
    quarter = here // BS
    count = blocks.shape[2]
    subsets = lax.axis_size("subset")
    tiles = lax.axis_size("tile")
    row_blocks = quarter * tiles
    each = count // row_blocks
    places = subsets // 2
    direct = tiles <= DIRECT
    subset = lax.axis_index("subset")
    pos = jnp.stack([subset // 2, subset % 2, lax.axis_index("tile")]).astype(jnp.int32)

    image_shape = (CB, slices, BS)
    image_out = jax.ShapeDtypeStruct(image_shape, jnp.bfloat16)
    terms_out = jax.ShapeDtypeStruct((row_blocks, slices, BS), jnp.bfloat16)
    rays_out = jax.ShapeDtypeStruct((row_blocks + 1, slices, BS), jnp.float32)
    final_out = jax.ShapeDtypeStruct((batches, per_batch, PIX), jnp.bfloat16)
    w_scr = pltpu.VMEM((row_blocks, slices, BS), jnp.bfloat16)
    x_scr = pltpu.VMEM(image_shape, jnp.float32)
    rays_scr = pltpu.VMEM((tiles, quarter, slices, BS), jnp.float32)

    def sent(value, target):
        pairs = []
        for p in range(places):
            for c in range(2):
                for t in range(tiles):
                    q, e, u = target(p, c, t)
                    pairs.append(((2 * p + c) * tiles + t, (2 * q + e) * tiles + u))
        return lax.ppermute(value, ("subset", "tile"), pairs)

    def swapped(value):
        return sent(value, lambda p, c, t: (p, 1 - c, t))

    def spread(value):
        if direct:
            far = range(1, tiles)
            return [value] + [sent(value, lambda p, c, t: (p, c, t ^ d)) for d in far]
        return [lax.all_gather(value, "tile")]

    def passed(terms, core):
        if not direct:
            return [swapped(lax.psum(terms, "tile"))]
        return [
            sent(terms, lambda p, c, t: (p, 1 - c, t ^ d if c == core else t))
            for d in range(tiles)
        ]

    def call(kernel, smem, operands, out_shape, scratch, name, flops=0):
        many = isinstance(out_shape, tuple)
        return pl.pallas_call(
            kernel,
            out_shape=out_shape,
            in_specs=[SMEM] * smem + [VMEM] * (len(operands) - smem),
            out_specs=(VMEM,) * len(out_shape) if many else VMEM,
            scratch_shapes=scratch,
            compiler_params=PARAMS,
            cost_estimate=pl.CostEstimate(
                flops=flops, bytes_accessed=0, transcendentals=0
            ),
            name=name,
        )(*operands)

    blocks2 = swapped(blocks)
    chunks = 16 if count % 16 == 0 else 1
    note, table, own, blocks = pl.pallas_call(
        functools.partial(head_kernel, row_blocks, chunks),
        out_shape=(
            jax.ShapeDtypeStruct((quarter + 1, slices, BS), jnp.bfloat16),
            jax.ShapeDtypeStruct((2, count), jnp.int32),
            pltpu.SMEM((3, count), jnp.int32),
            pltpu.VMEM(blocks.shape, blocks.dtype),
        ),
        in_specs=[SMEM] + [pl.BlockSpec(memory_space=pltpu.HBM)] * 4,
        out_specs=(VMEM, SMEM, SMEM, VMEM),
        scratch_shapes=[
            pltpu.SMEM(block_rows.shape, jnp.int32),
            pltpu.SMEM(block_cols.shape, jnp.int32),
            pltpu.VMEM(sinogram.shape, jnp.float32),
            pltpu.SMEM((row_blocks,), jnp.int32),
            pltpu.VMEM((row_blocks, BS, BS), jnp.float32),
            pltpu.VMEM((row_blocks, BS), jnp.float32),
            pltpu.SemaphoreType.DMA((3 + chunks,)),
        ],
        compiler_params=PARAMS,
        name="head",
    )(
        pos,
        *(
            pltpu.with_memory_space_constraint(value, pltpu.HBM)
            for value in (block_rows, block_cols, blocks, sinogram)
        ),
    )
    notes = spread(note)
    table2 = swapped(table)

    own = pltpu.with_memory_space_constraint(own, pltpu.SMEM)
    blocks2 = pltpu.with_memory_space_constraint(blocks2, pltpu.VMEM)
    wide = pl.pallas_call(
        pack_own_kernel,
        out_shape=pltpu.VMEM((row_blocks, BS, each * BS), jnp.bfloat16),
        in_specs=[SMEM, VMEM, pl.BlockSpec(memory_space=pl.ANY)],
        out_specs=VMEM,
        compiler_params=PARAMS,
        name="pack_own",
    )(own, blocks, note)
    info, tall = pl.pallas_call(
        pack_other_kernel,
        out_shape=(
            pltpu.SMEM((3, count), jnp.int32),
            pltpu.VMEM((row_blocks, each * BS, BS), jnp.bfloat16),
        ),
        in_specs=[SMEM, SMEM, VMEM],
        out_specs=(SMEM, VMEM),
        compiler_params=PARAMS,
        name="pack_other",
    )(own, table2, blocks2)
    info = pltpu.with_memory_space_constraint(info, pltpu.SMEM)

    held = []
    image, rays = None, None
    change_out = jax.ShapeDtypeStruct(image_shape, jnp.float32)

    def updated(place, core, terms):
        return call(
            functools.partial(update_kernel, place, core, 0, len(terms)),
            1,
            [info, wide, rays] + terms,
            change_out,
            [w_scr],
            "update",
            UPDATE_FLOPS,
        )

    for place in range(places):
        last = place == places - 1
        if place == 0:
            change, rays = call(
                functools.partial(update_kernel, place, 0, len(notes), 0),
                1,
                [info, wide] + notes,
                (change_out, rays_out),
                [w_scr, rays_scr],
                "update",
                UPDATE_FLOPS,
            )
            before = []
        else:
            def hop(p, c, t):
                if p == place - 1:
                    return (place, 1, t) if c else (p, 1, t)
                if p == place:
                    return (p, 0, t) if c else (place - 1, 0, t)
                return p, 1 - c, t

            image = sent(image, hop)
            terms = call(
                functools.partial(project_kernel, place),
                1,
                [info, image, tall],
                terms_out,
                [],
                "project",
            )
            change = updated(place, 0, passed(terms, 1))
            before = [swapped(image)]
        shot, terms = call(
            functools.partial(first_kernel, place),
            1,
            [info, tall, change] + before,
            (image_out, terms_out),
            [],
            "first",
        )
        change = updated(place, 1, passed(terms, 0))
        outs = call(
            functools.partial(second_kernel, place, last),
            1,
            [info, change, swapped(shot), shot] + held,
            final_out if last else (image_out, image_out),
            [],
            "second",
        )
        if last:
            return outs[None]
        image = outs[0]
        held = [outs[1]]


def solution(mesh):
    in_specs = (
        P("subset", "tile", None, None, None),
        P("subset", "tile", None),
        P("subset", "tile", None),
        P(None, None, ("subset", "tile")),
    )
    out_specs = P("subset", None, None, "tile")
    return jax.shard_map(
        per_device, mesh=mesh, in_specs=in_specs, out_specs=out_specs, check_vma=False
    )
```
